32 devices in a mesh: section: 2 (over core), dp: 4 (over z), ctx: 4 (over y, x).
Axes of the slice: x: 2, y: 2, z: 4, core: 2. Of those that a mesh axis runs over, the one named last changes fastest.
Arguments:
- inputs: bfloat16 [2, 4, 1024, 768], P(None, 'dp', 'ctx'), may hold values from -6 to 6
- lengths: int32 [2, 4], P(None, 'dp'), may hold values from 1 to 1024, as said below
- cotangent: bfloat16 [2, 4, 1024, 768], P(None, 'dp', 'ctx'), may hold values from -6 to 6
- first_gain: bfloat16 [2, 768], P('section'), may hold values from 0.5 to 1.5
- joint_weight: bfloat16 [2, 768, 2304], P('section'), may hold values from -0.21875 to 0.21875
- pre_mix: float32 [2, 12, 12], P('section'), may hold values from -1.75 to 1.75
- post_mix: float32 [2, 12, 12], P('section'), may hold values from -1.75 to 1.75
- mixer_weight: bfloat16 [2, 768, 768], P('section'), may hold values from -0.875 to 0.875
- second_gain: bfloat16 [2, 768], P('section'), may hold values from 0.5 to 1.5
- up_weight: bfloat16 [2, 768, 3072], P('section'), may hold values from -0.21875 to 0.21875
- down_weight: bfloat16 [2, 3072, 768], P('section'), may hold values from -0.109375 to 0.109375
Outputs:
- section_ends: bfloat16 [2, 2, 4, 1024, 768], P('section', None, 'dp', 'ctx')
- first_grad: float32 [2, 768], P('section', ('dp', 'ctx'))
- joint_grad: float32 [2, 768, 2304], P('section', ('dp', 'ctx'))
- premix_grad: float32 [2, 12, 12], P('section')
- postmix_grad: float32 [2, 12, 12], P('section')
- mixer_grad: float32 [2, 768, 768], P('section', ('dp', 'ctx'))
- second_grad: float32 [2, 768], P('section', ('dp', 'ctx'))
- up_grad: float32 [2, 768, 3072], P('section', ('dp', 'ctx'))
- down_grad: float32 [2, 3072, 768], P('section', ('dp', 'ctx'))
The draws below stay inside these ranges and needn't reach their ends.
Inputs may be any that keep to these rules, and one draw needn't show every extreme that they name: For each index of dp, of the rows it holds (one per micro-batch, 2 in all) one has length 1024; the others lean towards short lengths.
All inputs are finite; a program needn't handle non-finite values.
Results may differ from the reference program's by a relative error of at most 0.024.
Values may be sent and summed in bfloat16 or wider, within the bound.
No kernel may reach another device: no remote copies, remote signals or barrier semaphores. Data moves between devices by JAX's collectives and lax.ppermute only.
A program may use at most 320 MiB of HBM per device.

```python
from functools import partial
import jax
import jax.numpy as jnp
from jax import lax

D = 768
HEADS = 12
HEAD = 64
FF = 3072
MICRO = 2
ROWS_DEV = 1
SEQ = 1024
ROWS = 4


def draw_lengths(key, part):
    key = jax.random.fold_in(key, 7)
    key_a, key_b, key_c, key_d = jax.random.split(key, 4)
    grid_shape = (MICRO, ROWS)
    short_span = jnp.minimum(jax.random.randint(key_a, grid_shape, 0, SEQ), jnp.minimum(jax.random.randint(key_b, grid_shape, 0, SEQ), jax.random.randint(key_c, grid_shape, 0, SEQ)))
    row_lengths = 1 + short_span
    block_count = ROWS // ROWS_DEV
    chosen = jax.random.randint(key_d, (block_count,), 0, MICRO * ROWS_DEV)
    micro_pick = chosen // ROWS_DEV
    row_pick = jnp.arange(block_count) * ROWS_DEV + chosen % ROWS_DEV
    row_lengths = row_lengths.at[micro_pick, row_pick].set(SEQ)
    return row_lengths.astype(jnp.int32)


def block_levels(rng, extent, shards, smallest, high):
    def one(axis_at, parts):
        steps = jax.random.uniform(jax.random.fold_in(jax.random.fold_in(rng, 6), axis_at), (parts,), jnp.float32, smallest / len(shards), high / len(shards))
        return jnp.repeat(jnp.exp(steps), extent[axis_at] // parts).reshape((-1,) + (1,) * (len(extent) - axis_at - 1))

    factor_of = one(*shards[0])
    for cut in shards[1:]:
        factor_of = factor_of * one(*cut)
    return factor_of


def bell_draw(stream_key, shape, deviation, most, cuts=(), dtype=jnp.bfloat16):
    values = jax.random.normal(stream_key, shape, jnp.float32) * deviation
    if len(cuts) > 0:
        values = block_levels(stream_key, shape, cuts, -0.22, 0.18) * values
    return jnp.clip(values, min=-most, max=most).astype(dtype)


def setup_inputs(seed: int = 0) -> dict:
    keys = jax.random.split(jax.random.key(seed), 12)
    inputs = bell_draw(keys[0], (MICRO, ROWS, SEQ, D), 1.0, 6.0, ((1, 4), (2, 4)))
    lengths = draw_lengths(jax.random.fold_in(keys[11], 71), 0)
    cotangent = bell_draw(keys[2], (MICRO, ROWS, SEQ, D), 1.0, 6.0, ((1, 4), (2, 4)))
    first_gain = jnp.clip(1.0 + 0.1 * jax.random.normal(keys[3], (2, D), jnp.float32), 0.5, 1.5).astype(jnp.bfloat16)
    joint_weight = bell_draw(keys[4], (2, D, 3 * D), D ** -0.5, 0.21875, ((0, 2),))
    pre_mix = bell_draw(keys[5], (2, HEADS, HEADS), HEADS ** -0.5, 1.75, ((0, 2),), jnp.float32)
    post_mix = bell_draw(keys[6], (2, HEADS, HEADS), HEADS ** -0.5, 1.75, ((0, 2),), jnp.float32)
    mixer_weight = bell_draw(keys[7], (2, D, D), (D // 16) ** -0.5, 0.875, ((0, 2),))
    second_gain = jnp.clip(1.0 + 0.1 * jax.random.normal(keys[8], (2, D), jnp.float32), 0.5, 1.5).astype(jnp.bfloat16)
    up_weight = bell_draw(keys[9], (2, D, FF), D ** -0.5, 0.21875, ((0, 2),))
    down_weight = bell_draw(keys[10], (2, FF, D), FF ** -0.5, 0.109375, ((0, 2),))
    return dict(inputs=inputs, lengths=lengths, cotangent=cotangent, first_gain=first_gain, joint_weight=joint_weight, pre_mix=pre_mix, post_mix=post_mix, mixer_weight=mixer_weight, second_gain=second_gain, up_weight=up_weight, down_weight=down_weight)


@jax.custom_vjp
def low(v):
    return lax.optimization_barrier(v.astype(jnp.bfloat16)).astype(jnp.float32)

@jax.custom_vjp
def low_back(v):
    return v

def low_keep(v):
    return (low(v), None)

def low_pass(kept, grad):
    return (grad,)

def back_keep(v):
    return (v, None)

def back_low(kept, grad):
    return (low(grad),)
low.defvjp(low_keep, low_pass)
low_back.defvjp(back_keep, back_low)
HIGHEST = lax.Precision.HIGHEST
eps = 1e-06

def rms_scale(values, gain):
    inverse = lax.rsqrt(lax.optimization_barrier(jnp.mean(values * values, axis=-1, keepdims=True)) + eps)
    return values * inverse * gain

def matmul(left_side, right_side):
    return jnp.dot(left_side, right_side, precision=HIGHEST)

def attend_row(query, key_heads, value_heads, row_length, premix, postmix):
    scores = low_back(0.125 * jnp.einsum('che,she->hcs', query, key_heads, precision=HIGHEST))
    logits = jnp.einsum('gh,gcs->hcs', premix, scores, precision=HIGHEST)
    places = jnp.arange(SEQ)
    allowed = (places[None, :] <= places[:, None]) & (places[None, :] < row_length)
    logits = jnp.where(allowed[None], logits, -1e+30)
    highest = lax.optimization_barrier(jnp.max(logits, axis=-1, keepdims=True))
    exponent = jnp.exp(logits - highest)
    attention = exponent / lax.optimization_barrier(jnp.sum(exponent, axis=-1, keepdims=True))
    mixed_weights = low(jnp.einsum('gh,gcs->hcs', postmix, attention, precision=HIGHEST))
    return jnp.einsum('hcs,she->che', mixed_weights, value_heads, precision=HIGHEST)

def layer_step(block, row_lengths, gain_a, joint_w, premix, postmix, mixer_w, gain_b, upward_w, downward_w):
    row_count = block.shape[0]
    normed = low(rms_scale(block, gain_a))
    joint_out = low_back(low(matmul(normed, joint_w)))
    query = joint_out[:, :, :D].reshape(row_count, SEQ, HEADS, HEAD)
    key_heads = joint_out[:, :, D:2 * D].reshape(row_count, SEQ, HEADS, HEAD)
    value_heads = joint_out[:, :, 2 * D:].reshape(row_count, SEQ, HEADS, HEAD)
    attend_one = jax.checkpoint(partial(attend_row, premix=premix, postmix=postmix))
    attended = lax.map(lambda row_item: attend_one(*row_item), (query, key_heads, value_heads, row_lengths))
    attended = low_back(low(attended.reshape(row_count, SEQ, D)))
    hidden = block + low_back(matmul(attended, mixer_w))
    normed_two = low(rms_scale(hidden, gain_b))
    upward = low_back(matmul(normed_two, upward_w))
    active = low(jax.nn.gelu(upward, approximate=True))
    return hidden + low_back(matmul(active, downward_w))

def reference(inputs, lengths, cotangent, first_gain, joint_weight, pre_mix, post_mix, mixer_weight, second_gain, up_weight, down_weight):
    params = tuple((item_w.astype(jnp.float32) for item_w in (first_gain, joint_weight, pre_mix, post_mix, mixer_weight, second_gain, up_weight, down_weight)))

    def one_batch(totals, batch_item):
        block, row_lengths, cot_block = batch_item

        def two_layers(block_in, layer_params):
            first_out = layer_step(block_in, row_lengths, *[item_w[0] for item_w in layer_params])
            passed = low_back(low(first_out))
            return layer_step(passed, row_lengths, *[item_w[1] for item_w in layer_params])
        result, pull_back = jax.vjp(two_layers, block.astype(jnp.float32), params)
        input_grad, param_grads = pull_back(cot_block.astype(jnp.float32))
        totals = jax.tree.map(jnp.add, totals, param_grads)
        return (totals, (result.astype(jnp.bfloat16), input_grad.astype(jnp.bfloat16)))
    zero_grads = jax.tree.map(jnp.zeros_like, params)
    totals, (layer_outs, input_grads) = lax.scan(one_batch, zero_grads, (inputs, lengths, cotangent))
    section_ends = jnp.stack([input_grads, layer_outs])
    return (section_ends, totals[0], totals[1], totals[2], totals[3], totals[4], totals[5], totals[6], totals[7])
```

```python
import functools

import jax
import jax.numpy as jnp
from jax import lax
from jax.experimental import pallas as pl
from jax.experimental.pallas import tpu as pltpu
from jax.sharding import PartitionSpec as P

HEADS = 12
HEAD = 64
eps = 1e-06
MASKED = -1e30
f32 = jnp.float32
bf16 = jnp.bfloat16
VMEM_BYTES = 56 * 1024 * 1024


def dense(left_side, right_side):
    return jnp.dot(left_side, right_side, preferred_element_type=f32)


def dense_tn(left_side, right_side):
    return lax.dot_general(
        left_side, right_side, (((0,), (0,)), ((), ())), preferred_element_type=f32
    )


def dense_nt(left_side, right_side):
    return lax.dot_general(
        left_side, right_side, (((1,), (1,)), ((), ())), preferred_element_type=f32
    )


def forward_kernel(
    place, q_ref, k_ref, v_ref, pre_ref, post_ref, att_ref, u_ref, lse_ref, qp, logit, total, *, bq, bk
):
    step = pl.program_id(0)
    q_start = place[1 + step]
    length = place[0]
    q32 = q_ref[...].astype(f32)
    for h in range(HEADS):
        qp[pl.ds(h * bq, bq), :] = (q32 * pre_ref[h : h + 1, :]).astype(bf16)
    last = jnp.minimum(q_start + bq, length)
    blocks = (last + bk - 1) // bk
    rows = q_start + lax.broadcasted_iota(jnp.int32, (bq, bk), 0)

    def score(kb, top):
        k_blk = k_ref[pl.ds(pl.multiple_of(kb * bk, bk), bk), :]
        cols = kb * bk + lax.broadcasted_iota(jnp.int32, (bq, bk), 1)
        bias = jnp.where((cols <= rows) & (cols < length), 0.0, MASKED).astype(f32)
        tile = dense_nt(qp[...], k_blk)
        tile = (tile.reshape(HEADS, bq, bk) + bias[None]).reshape(HEADS * bq, bk)
        logit[kb] = tile
        return jnp.maximum(top, jnp.max(tile, axis=-1, keepdims=True))

    top = lax.fori_loop(0, blocks, score, jnp.full((HEADS * bq, 1), MASKED, f32))
    total[...] = jnp.zeros_like(total)

    def apply(kb, norm):
        e = jnp.exp(logit[kb] - top)
        v_blk = v_ref[pl.ds(pl.multiple_of(kb * bk, bk), bk), :]
        total[...] += dense(e.astype(bf16), v_blk)
        return norm + jnp.sum(e, axis=-1, keepdims=True)

    norm = lax.fori_loop(0, blocks, apply, jnp.zeros((HEADS * bq, 1), f32))
    scale = 1.0 / norm
    att = jnp.zeros((bq, q_ref.shape[1]), f32)
    for g in range(HEADS):
        u = total[pl.ds(g * bq, bq), :] * scale[g * bq : (g + 1) * bq]
        u_ref[pl.ds(g * bq, bq), :] = u.astype(bf16)
        att = att + u * post_ref[g : g + 1, :]
    att_ref[...] = att.astype(bf16)
    lse = jnp.broadcast_to(top + jnp.log(norm), (HEADS * bq, 128))
    lse_ref[0] = jnp.transpose(lse)[0:1, :]


def attention_forward(q, k, v, pre_vec, post_vec, place, bq, bk):
    count, width = q.shape
    seq = k.shape[0]
    steps = count // bq
    full = lambda i, place: (0, 0)
    return pl.pallas_call(
        functools.partial(forward_kernel, bq=bq, bk=bk),
        grid_spec=pltpu.PrefetchScalarGridSpec(
            num_scalar_prefetch=1,
            grid=(steps,),
            in_specs=[
                pl.BlockSpec((bq, width), lambda i, place: (i, 0)),
                pl.BlockSpec((seq, width), full),
                pl.BlockSpec((seq, width), full),
                pl.BlockSpec((HEADS, width), full),
                pl.BlockSpec((HEADS, width), full),
            ],
            out_specs=[
                pl.BlockSpec((bq, width), lambda i, place: (i, 0)),
                pl.BlockSpec((HEADS * bq, width), lambda i, place: (i, 0)),
                pl.BlockSpec((1, 1, HEADS * bq), lambda i, place: (i, 0, 0)),
            ],
            scratch_shapes=[
                pltpu.VMEM((HEADS * bq, width), bf16),
                pltpu.VMEM((seq // bk, HEADS * bq, bk), f32),
                pltpu.VMEM((HEADS * bq, width), f32),
            ],
        ),
        out_shape=[
            jax.ShapeDtypeStruct((count, width), bf16),
            jax.ShapeDtypeStruct((HEADS * count, width), bf16),
            jax.ShapeDtypeStruct((steps, 1, HEADS * bq), f32),
        ],
        compiler_params=pltpu.CompilerParams(vmem_limit_bytes=VMEM_BYTES),
        cost_estimate=pl.CostEstimate(
            flops=4 * HEADS * count * seq * width * 5 // 8,
            bytes_accessed=4 * seq * width + 2 * HEADS * count * width,
            transcendentals=HEADS * count * seq * 5 // 8,
        ),
    )(place, q, k, v, pre_vec, post_vec)


def backward_kernel(
    place, q_ref, datt_ref, u_ref, lse_ref, k_ref, kt_ref, v_ref, pre_ref, post_ref,
    dq_ref, dk_ref, dv_ref, pre_grad_ref, post_grad_ref,
    qp, dp, dk_sum, dv_sum, wt, delta, *, bq, bk,
):
    step = pl.program_id(0)
    q_start = place[1 + step]
    length = place[0]

    @pl.when(step == 0)
    def _():
        dk_sum[...] = jnp.zeros_like(dk_sum)
        dv_sum[...] = jnp.zeros_like(dv_sum)
        pre_grad_ref[...] = jnp.zeros_like(pre_grad_ref)
        post_grad_ref[...] = jnp.zeros_like(post_grad_ref)

    q32 = q_ref[...].astype(f32)
    datt = datt_ref[...].astype(f32)
    for h in range(HEADS):
        part = pl.ds(h * bq, bq)
        qp[part, :] = (q32 * pre_ref[h : h + 1, :]).astype(bf16)
        scaled = datt * post_ref[h : h + 1, :]
        dp[part, :] = scaled.astype(bf16)
        u = u_ref[part, :].astype(f32)
        spread = jnp.sum(scaled * u, axis=-1, keepdims=True)
        delta[part, :] = jnp.broadcast_to(spread, (bq, 128))
        post_grad_ref[h : h + 1, :] += jnp.sum(datt * u, axis=0, keepdims=True)
    spread = jnp.transpose(delta[...])[0:1, :]
    lse = lse_ref[0]
    wt[...] = jnp.zeros_like(wt)
    last = jnp.minimum(q_start + bq, length)
    blocks = (last + bk - 1) // bk
    cols = q_start + lax.broadcasted_iota(jnp.int32, (bk, HEADS * bq), 1) % bq

    def block(kb, carry):
        span = pl.ds(pl.multiple_of(kb * bk, bk), bk)
        rows = kb * bk + lax.broadcasted_iota(jnp.int32, (bk, HEADS * bq), 0)
        allowed = (rows <= cols) & (rows < length)
        logits = dense_nt(k_ref[span, :], qp[...])
        attention = jnp.exp(jnp.where(allowed, logits - lse, MASKED))
        grad = dense_nt(v_ref[span, :], dp[...])
        dlog = (attention * (grad - spread)).astype(bf16)
        dv_sum[span, :] += dense(attention.astype(bf16), dp[...])
        dk_sum[span, :] += dense(dlog, qp[...])
        wt[...] += dense(kt_ref[:, span], dlog)
        return carry

    lax.fori_loop(0, blocks, block, 0)
    w = jnp.transpose(wt[...])
    dq = jnp.zeros_like(q32)
    for h in range(HEADS):
        part = w[h * bq : (h + 1) * bq, :]
        dq = dq + part * pre_ref[h : h + 1, :]
        pre_grad_ref[h : h + 1, :] += jnp.sum(part * q32, axis=0, keepdims=True)
    dq_ref[...] = dq.astype(bf16)

    @pl.when(step == pl.num_programs(0) - 1)
    def _():
        dk_ref[...] = dk_sum[...].astype(bf16)
        dv_ref[...] = dv_sum[...].astype(bf16)


def attention_backward(q, datt, u, lse, k, kt, v, pre_vec, post_vec, place, bq, bk):
    count, width = q.shape
    seq = k.shape[0]
    steps = count // bq
    full = lambda i, place: (0, 0)
    row = lambda i, place: (i, 0)
    return pl.pallas_call(
        functools.partial(backward_kernel, bq=bq, bk=bk),
        grid_spec=pltpu.PrefetchScalarGridSpec(
            num_scalar_prefetch=1,
            grid=(steps,),
            in_specs=[
                pl.BlockSpec((bq, width), row),
                pl.BlockSpec((bq, width), row),
                pl.BlockSpec((HEADS * bq, width), row),
                pl.BlockSpec((1, 1, HEADS * bq), lambda i, place: (i, 0, 0)),
                pl.BlockSpec((seq, width), full),
                pl.BlockSpec((width, seq), full),
                pl.BlockSpec((seq, width), full),
                pl.BlockSpec((HEADS, width), full),
                pl.BlockSpec((HEADS, width), full),
            ],
            out_specs=[
                pl.BlockSpec((bq, width), row),
                pl.BlockSpec((seq, width), full),
                pl.BlockSpec((seq, width), full),
                pl.BlockSpec((HEADS, width), full),
                pl.BlockSpec((HEADS, width), full),
            ],
            scratch_shapes=[
                pltpu.VMEM((HEADS * bq, width), bf16),
                pltpu.VMEM((HEADS * bq, width), bf16),
                pltpu.VMEM((seq, width), f32),
                pltpu.VMEM((seq, width), f32),
                pltpu.VMEM((width, HEADS * bq), f32),
                pltpu.VMEM((HEADS * bq, 128), f32),
            ],
        ),
        out_shape=[
            jax.ShapeDtypeStruct((count, width), bf16),
            jax.ShapeDtypeStruct((seq, width), bf16),
            jax.ShapeDtypeStruct((seq, width), bf16),
            jax.ShapeDtypeStruct((HEADS, width), f32),
            jax.ShapeDtypeStruct((HEADS, width), f32),
        ],
        compiler_params=pltpu.CompilerParams(vmem_limit_bytes=VMEM_BYTES),
        cost_estimate=pl.CostEstimate(
            flops=10 * HEADS * count * seq * width * 5 // 8,
            bytes_accessed=10 * seq * width + 2 * HEADS * count * width,
            transcendentals=HEADS * count * seq * 5 // 8,
        ),
    )(place, q, datt, u, lse, k, kt, v, pre_vec, post_vec)


def swap_section(x):
    return lax.ppermute(x, "section", [(0, 1), (1, 0)])


def xor_permute(x, axis, by):
    return lax.ppermute(x, axis, [(i, i ^ by) for i in range(lax.axis_size(axis))])


def from_xor_order(x, index):
    places = range(x.shape[0])
    return jnp.concatenate([lax.dynamic_index_in_dim(x, index ^ i, 0) for i in places])


def reduce_scatter(block):
    dp_count, ctx_count = block.shape[:2]
    ctx, dp = lax.axis_index("ctx"), lax.axis_index("dp")
    bits = []
    bit = 1
    while bit < ctx_count:
        bits.append(bit)
        bit *= 2
    columns = block.shape[3]
    cut = (columns // 2 + 127) // 128 * 128
    halves = []
    for part, order in ((block[..., :cut], bits), (block[..., cut:], bits[::-1])):
        ids = list(range(len(bits)))
        part = part.reshape((dp_count,) + (2,) * len(bits) + part.shape[2:])
        left = list(bits[::-1])
        for bit in order:
            axis = 1 + left.index(bit)
            left.remove(bit)
            mine = (ctx // bit) % 2
            sent = lax.dynamic_index_in_dim(part, 1 - mine, axis, keepdims=False)
            kept = lax.dynamic_index_in_dim(part, mine, axis, keepdims=False)
            got = xor_permute(sent, "ctx", bit)
            part = (kept.astype(f32) + got.astype(f32)).astype(bf16)
        halves.append(part)
    whole = jnp.concatenate(halves, axis=-1)
    total = lax.dynamic_index_in_dim(whole, dp, 0, keepdims=False).astype(f32)
    for by in range(1, dp_count):
        sent = lax.dynamic_index_in_dim(whole, dp ^ by, 0, keepdims=False)
        total = total + xor_permute(sent, "dp", by).astype(f32)
    return total


def all_sum(vector):
    for axis in ("ctx", "dp"):
        bit = 1
        while bit < lax.axis_size(axis):
            vector = vector + xor_permute(vector, axis, bit)
            bit *= 2
    return vector


def local(
    inputs, lengths, cotangent, first_gain, joint_weight, pre_mix, post_mix,
    mixer_weight, second_gain, up_weight, down_weight,
):
    s = lax.axis_index("section")
    ctx = lax.axis_index("ctx")
    n = lax.axis_size("ctx")
    dp_count = lax.axis_size("dp")
    chips = n // 2
    micro_count, row_count, local_len, width = inputs.shape
    seq = local_len * n
    blk = local_len // 2
    m = ctx // chips
    xi = ctx % chips
    core = xi * 2 + s
    inputs = inputs.reshape(micro_count, 2, blk, width)
    cotangent = cotangent.reshape(micro_count, 2, blk, width)
    pick = lambda arr, i: lax.dynamic_index_in_dim(arr, i, 0, keepdims=False)

    mine = pick(inputs, m)
    pieces = []
    for d in range(1, n):
        target = m ^ (1 if d >= chips else 0)
        pieces.append(xor_permute(pick(pick(inputs, target), s), "ctx", d))
    own_half = jnp.stack([pick(mine, s)] + pieces)
    other_half = jnp.concatenate([pick(mine, 1 - s)[None], swap_section(jnp.stack(pieces))])
    first, second = jnp.where(s == 0, own_half, other_half), jnp.where(s == 0, other_half, own_half)
    x_all = from_xor_order(jnp.stack([first, second], axis=1), ctx).reshape(seq, width)

    both = []
    for w in (first_gain, joint_weight, pre_mix, post_mix, mixer_weight, second_gain, up_weight, down_weight):
        got = swap_section(w)
        both.append((jnp.where(s == 0, w[0], got[0]), jnp.where(s == 0, got[0], w[0])))
    gains_a, joints, premixes, postmixes, mixers, gains_b, ups, downs = both

    length = pick(lengths.reshape(-1), m)
    low_start = core * blk
    high_start = (2 * n - 1 - core) * blk
    bq = min(64, blk)
    bk = min(256, seq)
    per = blk // bq
    place = jnp.stack(
        [length]
        + [low_start + i * bq for i in range(per)]
        + [high_start + i * bq for i in range(per)]
    ).astype(jnp.int32)

    def own_rows(x):
        return jnp.concatenate(
            [
                lax.dynamic_slice_in_dim(x, low_start, blk, 0),
                lax.dynamic_slice_in_dim(x, high_start, blk, 0),
            ]
        )

    def gather_row(x):
        got = [x] + [xor_permute(x, "ctx", d) for d in range(1, chips)]
        own = jnp.stack(got)
        other = swap_section(own)
        first, second = jnp.where(s == 0, own, other), jnp.where(s == 0, other, own)
        cores = from_xor_order(jnp.stack([first, second], axis=1), xi).reshape(n, 2, blk, width)
        return jnp.concatenate([cores[i, 0] for i in range(n)] + [cores[n - 1 - i, 1] for i in range(n)])

    def scatter_row(x):
        parts = x.astype(bf16).reshape(2 * n, blk, width)
        cores = jnp.stack([parts[i if h == 0 else 2 * n - 1 - i] for i in range(n) for h in range(2)])
        cores = cores.reshape(chips, 2, 2, blk, width)
        kept = lax.dynamic_index_in_dim(cores, s, 1, keepdims=False)
        got = swap_section(lax.dynamic_index_in_dim(cores, 1 - s, 1, keepdims=False))
        chip = kept.astype(f32) + got.astype(f32)
        total = pick(chip, xi)
        low = chip.astype(bf16)
        for d in range(1, chips):
            total = total + xor_permute(pick(low, xi ^ d), "ctx", d).astype(f32)
        return total.reshape(2 * blk, width)

    def rms_parts(values, gain):
        inverse = lax.rsqrt(jnp.mean(values * values, axis=-1, keepdims=True) + eps)
        return inverse, (values * inverse * gain).astype(bf16)

    def forward(layer, x_own, normed_all, normed_own):
        gain_b = gains_b[layer].astype(f32)
        joint_w = joints[layer]
        pre_vec = 0.125 * jnp.repeat(premixes[layer].T, HEAD, axis=1)
        post_vec = jnp.repeat(postmixes[layer], HEAD, axis=1)
        q = dense(normed_own, joint_w[:, :width]).astype(bf16)
        k = dense(normed_all, joint_w[:, width : 2 * width]).astype(bf16)
        v = dense(normed_all, joint_w[:, 2 * width :]).astype(bf16)
        attended, u, lse = attention_forward(q, k, v, pre_vec, post_vec, place, bq, bk)
        hidden = x_own + dense(attended, mixers[layer])
        inverse_two, normed_two = rms_parts(hidden, gain_b)
        upward = dense(normed_two, ups[layer])
        active = jax.nn.gelu(upward, approximate=True).astype(bf16)
        output = hidden + dense(active, downs[layer])
        kept = (q, k, v, u, lse, attended, hidden, inverse_two, normed_two, upward, active, pre_vec, post_vec)
        return output, kept

    def chip_rows(x):
        return jnp.concatenate([x, swap_section(x)])

    def chip_product(left, right):
        half = right.shape[1] // 2
        kept = lax.dynamic_slice_in_dim(right, s * half, half, 1)
        got = swap_section(lax.dynamic_slice_in_dim(right, (1 - s) * half, half, 1))
        return dense_tn(chip_rows(left), jnp.concatenate([kept, got])).astype(bf16)

    def blocks_of(grad):
        return grad.reshape(dp_count, n, grad.shape[0] // (dp_count * n), grad.shape[1])

    def rms_back(grad_normed, values, inverse, gain):
        unit = values * inverse
        gain_grad = jnp.sum(grad_normed * unit, axis=0)
        scaled = grad_normed * gain
        back = inverse * (scaled - unit * jnp.mean(scaled * unit, axis=-1, keepdims=True))
        return back, gain_grad

    def backward(layer, dy, x_own, inverse, normed_all, normed_own, kept):
        q, k, v, u, lse, attended, hidden, inverse_two, normed_two, upward, active, pre_vec, post_vec = kept
        gain_a, gain_b = gains_a[layer].astype(f32), gains_b[layer].astype(f32)
        joint_w = joints[layer]
        dy_low = dy.astype(bf16)
        down_sum = reduce_scatter(blocks_of(chip_product(active, dy_low)))
        dactive = dense_nt(dy_low, downs[layer])
        _, pull = jax.vjp(lambda t: jax.nn.gelu(t, approximate=True), upward)
        dup = pull(dactive)[0].astype(bf16)
        up_sum = reduce_scatter(blocks_of(chip_product(normed_two, dup)))
        dnormed_two, gain_b_grad = rms_back(dense_nt(dup, ups[layer]), hidden, inverse_two, gain_b)
        dhidden = dy + dnormed_two
        dhidden_low = dhidden.astype(bf16)
        mixer_sum = reduce_scatter(blocks_of(chip_product(attended, dhidden_low)))
        datt = dense_nt(dhidden_low, mixers[layer]).astype(bf16)
        dq, dk, dv, pre_rows, post_rows = attention_backward(
            q, datt, u, lse, k, k.T, v, pre_vec, post_vec, place, bq, bk
        )
        got = swap_section(jnp.where(s == 0, dv, dk))
        dkv = (jnp.where(s == 0, dk, dv).astype(f32) + got.astype(f32)).astype(bf16)
        kv_w = lax.dynamic_slice_in_dim(joint_w, width * (1 + s), width, 1)
        dnormed = scatter_row(dense_nt(dkv, kv_w)) + dense_nt(dq, joint_w[:, :width])
        joint_sum = reduce_scatter(
            blocks_of(jnp.concatenate([chip_product(normed_own, dq), dense_tn(normed_all, dkv).astype(bf16)], axis=1))
        )
        dfront, gain_a_grad = rms_back(dnormed, x_own, inverse, gain_a)
        pre_grad = jnp.sum(pre_rows.reshape(HEADS, HEADS, HEAD), axis=-1).T * 0.125
        post_grad = jnp.sum(post_rows.reshape(HEADS, HEADS, HEAD), axis=-1)
        small = jnp.concatenate([gain_a_grad, gain_b_grad, pre_grad.reshape(-1), post_grad.reshape(-1)])
        return dhidden + dfront, (joint_sum, mixer_sum, up_sum, down_sum), small

    x0 = x_all.astype(f32)
    _, normed_all0 = rms_parts(x0, gains_a[0].astype(f32))
    x0_own = own_rows(x_all).astype(f32)
    inverse0, normed_own0 = rms_parts(x0_own, gains_a[0].astype(f32))
    out0, kept0 = forward(0, x0_own, normed_all0, normed_own0)
    x1_own = out0.astype(bf16).astype(f32)
    inverse1, normed_own1 = rms_parts(x1_own, gains_a[1].astype(f32))
    normed_all1 = gather_row(normed_own1)
    out1, kept1 = forward(1, x1_own, normed_all1, normed_own1)

    low_chip = ctx < chips
    there = [(i, chips + i) for i in range(chips)] + [(n - 1 - i, i) for i in range(chips)]
    here = [(n - 1 - i, chips + i) for i in range(chips)] + [(i, i) for i in range(chips)]
    one = lax.ppermute(jnp.where(low_chip, pick(cotangent[1], s), pick(cotangent[0], 1 - s)), "ctx", there)
    two = lax.ppermute(jnp.where(low_chip, pick(cotangent[0], s), pick(cotangent[1], 1 - s)), "ctx", here)
    dy1 = jnp.concatenate([jnp.where(m == 0, two, one), jnp.where(m == 0, one, two)]).astype(f32)

    def send_home(x):
        x = x.reshape(2, blk, width)
        one = lax.ppermute(jnp.where(m == 0, x[1], x[0]), "ctx", [(b, a) for a, b in there])
        two = lax.ppermute(jnp.where(m == 0, x[0], x[1]), "ctx", [(b, a) for a, b in here])
        return jnp.where(low_chip, jnp.stack([two, one]), jnp.stack([one, two]))

    y_home = send_home(out1.astype(bf16))
    dx1, sums1, small1 = backward(1, dy1, x1_own, inverse1, normed_all1, normed_own1, kept1)
    dy0 = dx1.astype(bf16).astype(f32)
    dx0, sums0, small0 = backward(0, dy0, x0_own, inverse0, normed_all0, normed_own0, kept0)
    dx_home = send_home(dx0.astype(bf16))

    got = swap_section(jnp.where(s == 0, y_home, dx_home))
    held = jnp.where(s == 0, dx_home, y_home)
    is_first = jnp.where(low_chip, s, 1 - s) == 0
    ends = jnp.stack([jnp.where(is_first, held, got), jnp.where(is_first, got, held)], axis=1)
    ends = ends.reshape(1, micro_count, row_count, local_len, width)

    small_got = swap_section(jnp.where(s == 0, small1, small0))
    small = all_sum(jnp.where(s == 0, small0, small1) + small_got)
    shard = width // (dp_count * n)
    at = (lax.axis_index("dp") * n + ctx) * shard
    gain_a_out = lax.dynamic_slice_in_dim(small[:width], at, shard, 0)
    gain_b_out = lax.dynamic_slice_in_dim(small[width : 2 * width], at, shard, 0)
    pre_out = small[2 * width : 2 * width + HEADS * HEADS].reshape(1, HEADS, HEADS)
    post_out = small[2 * width + HEADS * HEADS :].reshape(1, HEADS, HEADS)

    outs = []
    for at_zero, at_one in zip(sums0, sums1):
        other = swap_section(jnp.where(s == 0, at_one, at_zero))
        own = jnp.where(s == 0, at_zero, at_one)
        outs.append((jnp.where(s == 0, own, other), jnp.where(s == 0, other, own)))
    (joint_a, joint_b), mixer_halves, up_halves, down_halves = outs
    q_half = width // 2
    joint_out = jnp.concatenate([joint_a[:, :q_half], joint_b[:, :q_half], joint_a[:, q_half:], joint_b[:, q_half:]], axis=1)
    mixer_out, up_out, down_out = (jnp.concatenate(pair, axis=1) for pair in (mixer_halves, up_halves, down_halves))
    return (
        ends,
        gain_a_out[None],
        joint_out[None],
        pre_out,
        post_out,
        mixer_out[None],
        gain_b_out[None],
        up_out[None],
        down_out[None],
    )


def solution(mesh):
    in_specs = (
        P(None, "dp", "ctx", None),
        P(None, "dp"),
        P(None, "dp", "ctx", None),
        P("section", None),
        P("section", None, None),
        P("section", None, None),
        P("section", None, None),
        P("section", None, None),
        P("section", None),
        P("section", None, None),
        P("section", None, None),
    )
    out_specs = (
        P("section", None, "dp", "ctx", None),
        P("section", ("dp", "ctx")),
        P("section", ("dp", "ctx"), None),
        P("section", None, None),
        P("section", None, None),
        P("section", ("dp", "ctx"), None),
        P("section", ("dp", "ctx")),
        P("section", ("dp", "ctx"), None),
        P("section", ("dp", "ctx"), None),
    )
    return jax.shard_map(local, mesh=mesh, in_specs=in_specs, out_specs=out_specs, check_vma=False)
```

```python
import functools

import jax
import jax.numpy as jnp
from jax import lax
from jax.experimental import pallas as pl
from jax.experimental.pallas import tpu as pltpu
from jax.sharding import PartitionSpec as P

HEADS = 12
HEAD = 64
eps = 1e-06
MASKED = -1e30
f32 = jnp.float32
bf16 = jnp.bfloat16
VMEM_BYTES = 58 * 1024 * 1024


def dense(left_side, right_side):
    return jnp.dot(left_side, right_side, preferred_element_type=f32)


def dense_tn(left_side, right_side):
    return lax.dot_general(
        left_side, right_side, (((0,), (0,)), ((), ())), preferred_element_type=f32
    )


def dense_nt(left_side, right_side):
    return lax.dot_general(
        left_side, right_side, (((1,), (1,)), ((), ())), preferred_element_type=f32
    )


GAIN_A, GAIN_B, PRE, POST = 0, 1, 8, 24
SMALL_ROWS = 40


def small_of(own, got, which):
    return lambda at, size: jnp.where(which == 0, own[at : at + size, :], got[at : at + size, :])


def rms_inverse(values):
    return lax.rsqrt(jnp.mean(values * values, axis=-1, keepdims=True) + eps)


def lane_parts(x):
    return [x[:, i : i + 128] for i in range(0, x.shape[1], 128)]


def bias_of(q_start, k_start, length, bq, bk):
    rows = q_start + lax.broadcasted_iota(jnp.int32, (bq, bk), 0)
    cols = k_start + lax.broadcasted_iota(jnp.int32, (bq, bk), 1)
    return jnp.where((cols <= rows) & (cols < length), 0.0, MASKED).astype(f32)


def attend_kernel(
    place, x_ref, small_own, small_got, joint_own, joint_got, *rest, bk, extra
):
    (
        att_ref, q_ref, own_ref, token_ref, normed_hbm, k_hbm, v_hbm, u_hbm, lse_hbm,
        joint, normed, k, v, u, lse, qp, logit, total, top, norm, sems,
    ) = rest[extra:]
    token_ref[0] = 0
    length, which = place[0], place[1]
    fetch((joint_own, joint_got), which, joint, sems.at[0])
    seq, width = x_ref.shape
    count = att_ref.shape[0]
    bq = count // 2
    small = small_of(small_own, small_got, which)
    gain, pre, post = small(GAIN_A, 1), small(PRE, HEADS), small(POST, HEADS)
    step_rows = min(256, seq)

    def normalise(i, carry):
        span = pl.ds(pl.multiple_of(i * step_rows, step_rows), step_rows)
        x = x_ref[span, :].astype(f32)
        normed[span, :] = (x * rms_inverse(x) * gain).astype(bf16)
        return carry

    lax.fori_loop(0, seq // step_rows, normalise, 0)
    for i in range(2):
        own_ref[i * bq : (i + 1) * bq, :] = normed[pl.ds(pl.multiple_of(place[2 + i], bq), bq), :]
    fetched((joint_own, joint_got), joint, sems.at[0])
    cut = width // 3
    for i in range(3):
        cols = slice(width + i * cut, width + (i + 1) * cut)
        k[:, i * cut : (i + 1) * cut] = dense(normed[...], joint[:, cols]).astype(bf16)
    for i in range(3):
        cols = slice(2 * width + i * cut, 2 * width + (i + 1) * cut)
        v[:, i * cut : (i + 1) * cut] = dense(normed[...], joint[:, cols]).astype(bf16)
    q_ref[...] = dense(own_ref[...], joint[:, :width]).astype(bf16)
    outs = [
        pltpu.make_async_copy(a, b, sems.at[1 + i])
        for i, (a, b) in enumerate(((normed, normed_hbm), (k, k_hbm), (v, v_hbm)))
    ]
    for out in outs:
        out.start()

    def rows_step(step, carry):
        q_start = place[2 + step]
        mine = pl.ds(pl.multiple_of(step * bq, bq), bq)
        q32 = q_ref[mine, :].astype(f32)
        for h in range(HEADS):
            qp[h * bq : (h + 1) * bq, :] = (q32 * pre[h : h + 1, :]).astype(bf16)
        blocks = (jnp.minimum(q_start + bq, length) + bk - 1) // bk
        top[...] = jnp.full_like(top, MASKED)
        total[...] = jnp.zeros_like(total)
        norm[...] = jnp.zeros_like(norm)

        def score(kb, c):
            bias = bias_of(q_start, kb * bk, length, bq, bk)
            tile = dense_nt(qp[...], k[pl.ds(pl.multiple_of(kb * bk, bk), bk), :])
            tile = (tile.reshape(HEADS, bq, bk) + bias[None]).reshape(HEADS * bq, bk)
            logit[kb] = tile
            top[...] = functools.reduce(jnp.maximum, lane_parts(tile), top[...])
            return c

        lax.fori_loop(0, blocks, score, 0)
        highest = jnp.max(top[...], axis=-1, keepdims=True)
        top[...] = jnp.broadcast_to(highest, top.shape)

        def apply(kb, c):
            high = top[...]
            parts = [jnp.exp(x - high) for x in lane_parts(logit[kb])]
            norm[...] = functools.reduce(jnp.add, parts, norm[...])
            e = jnp.concatenate([x.astype(bf16) for x in parts], axis=1)
            total[...] += dense(e, v[pl.ds(pl.multiple_of(kb * bk, bk), bk), :])
            return c

        lax.fori_loop(0, blocks, apply, 0)
        sums = jnp.sum(norm[...], axis=-1, keepdims=True)
        scale = 1.0 / sums
        rows = pl.ds(pl.multiple_of(step * HEADS * bq, HEADS * bq), HEADS * bq)
        lse[rows, :] = jnp.broadcast_to(highest + jnp.log(sums), top.shape)
        att = jnp.zeros((bq, width), f32)
        for g in range(HEADS):
            part = total[g * bq : (g + 1) * bq, :] * scale[g * bq : (g + 1) * bq]
            u[pl.ds(pl.multiple_of(step * HEADS * bq + g * bq, bq), bq), :] = part.astype(bf16)
            att = att + part * post[g : g + 1, :]
        att_ref[mine, :] = att.astype(bf16)
        return carry

    lax.fori_loop(0, 2, rows_step, 0)
    outs += [pltpu.make_async_copy(u, u_hbm, sems.at[4]), pltpu.make_async_copy(lse, lse_hbm, sems.at[5])]
    for out in outs[3:]:
        out.start()
    for out in outs:
        out.wait()


VMEM_SPEC = pl.BlockSpec(memory_space=pltpu.VMEM)
HBM_SPEC = pl.BlockSpec(memory_space=pl.ANY)
SMEM_SPEC = pl.BlockSpec(memory_space=pltpu.SMEM)
TOKEN = jax.ShapeDtypeStruct((1,), jnp.int32)


def attend(place, x_all, count, smalls, joints, bk, extras):
    seq, width = x_all.shape
    bq = count // 2
    shape = jax.ShapeDtypeStruct
    return pl.pallas_call(
        functools.partial(attend_kernel, bk=bk, extra=len(extras)),
        in_specs=[SMEM_SPEC] + [VMEM_SPEC] * 3 + [HBM_SPEC] * (2 + len(extras)),
        out_specs=[VMEM_SPEC] * 3 + [SMEM_SPEC] + [HBM_SPEC] * 5,
        out_shape=[shape((count, width), bf16)] * 3
        + [TOKEN]
        + [shape((seq, width), bf16)] * 3
        + [shape((HEADS * count, width), bf16), shape((HEADS * count, 128), f32)],
        scratch_shapes=[
            pltpu.VMEM((width, 3 * width), bf16),
            pltpu.VMEM((seq, width), bf16),
            pltpu.VMEM((seq, width), bf16),
            pltpu.VMEM((seq, width), bf16),
            pltpu.VMEM((HEADS * count, width), bf16),
            pltpu.VMEM((HEADS * count, 128), f32),
            pltpu.VMEM((HEADS * bq, width), bf16),
            pltpu.VMEM((seq // bk, HEADS * bq, bk), f32),
            pltpu.VMEM((HEADS * bq, width), f32),
            pltpu.VMEM((HEADS * bq, 128), f32),
            pltpu.VMEM((HEADS * bq, 128), f32),
            pltpu.SemaphoreType.DMA((6,)),
        ],
        compiler_params=pltpu.CompilerParams(vmem_limit_bytes=VMEM_BYTES),
        cost_estimate=pl.CostEstimate(
            flops=4 * HEADS * count * seq * width, bytes_accessed=30 * seq * width, transcendentals=HEADS * count * seq
        ),
    )(place, x_all, *smalls, *joints, *extras)


def feed_kernel(
    which, x_ref, att_ref, small_own, small_got,
    mixer_own, mixer_got, up_own, up_got, down_own, down_got, *rest, tile, extra,
):
    (
        out_ref, hidden_ref, two_ref, upward_hbm, active_hbm, token_ref,
        mixer, up, down, upward, active, sems,
    ) = rest[extra:]
    token_ref[0] = 0
    pairs = ((mixer_own, mixer_got), (up_own, up_got), (down_own, down_got))
    buffers = (mixer, up, down)
    for i in range(3):
        fetch(pairs[i], which[0], buffers[i], sems.at[i])
    gain = small_of(small_own, small_got, which[0])(GAIN_B, 1)
    fetched(pairs[0], mixer, sems.at[0])
    hidden = x_ref[...].astype(f32) + dense(att_ref[...], mixer[...])
    hidden_ref[...] = hidden
    two = (hidden * rms_inverse(hidden) * gain).astype(bf16)
    two_ref[...] = two
    fetched(pairs[1], up, sems.at[1])
    result, outs = hidden, []
    for j in range(down.shape[0] // tile):
        span = slice(j * tile, (j + 1) * tile)
        u = dense(two, up[:, span])
        upward[:, span] = u
        act = (0.5 * u * (1.0 + jnp.tanh(0.7978845608 * (u + 0.044715 * (u * u * u))))).astype(bf16)
        active[:, span] = act
        if j == 0:
            fetched(pairs[2], down, sems.at[2])
        result = result + dense(act, down[span, :])
    outs = [pltpu.make_async_copy(upward, upward_hbm, sems.at[3]), pltpu.make_async_copy(active, active_hbm, sems.at[4])]
    for out in outs:
        out.start()
    out_ref[...] = result.astype(bf16)
    for out in outs:
        out.wait()


def feed(which, x, attended, smalls, weights, ff, extras):
    count, width = x.shape
    shape = jax.ShapeDtypeStruct
    return pl.pallas_call(
        functools.partial(feed_kernel, tile=width, extra=len(extras)),
        in_specs=[SMEM_SPEC] + [VMEM_SPEC] * 4 + [HBM_SPEC] * (6 + len(extras)),
        out_specs=[VMEM_SPEC] * 3 + [HBM_SPEC] * 2 + [SMEM_SPEC],
        out_shape=[
            shape((count, width), bf16),
            shape((count, width), f32),
            shape((count, width), bf16),
            shape((count, ff), f32),
            shape((count, ff), bf16),
            TOKEN,
        ],
        scratch_shapes=[
            pltpu.VMEM((width, width), bf16),
            pltpu.VMEM((width, ff), bf16),
            pltpu.VMEM((ff, width), bf16),
            pltpu.VMEM((count, ff), f32),
            pltpu.VMEM((count, ff), bf16),
            pltpu.SemaphoreType.DMA((5,)),
        ],
        compiler_params=pltpu.CompilerParams(vmem_limit_bytes=VMEM_BYTES),
        cost_estimate=pl.CostEstimate(
            flops=2 * count * width * (2 * ff + width), bytes_accessed=4 * width * ff, transcendentals=count * ff
        ),
    )(which, x, attended, *smalls, *weights, *extras)


def fetch(pair, which, buffer, semaphore):
    for i, ref in enumerate(pair):

        @pl.when(which == i)
        def _(ref=ref):
            pltpu.make_async_copy(ref.at[0], buffer, semaphore).start()


def fetched(pair, buffer, semaphore):
    pltpu.make_async_copy(pair[0].at[0], buffer, semaphore).wait()


def gelu_slope(u):
    inner = 0.7978845608 * (u + 0.044715 * (u * u * u))
    t = jnp.tanh(inner)
    return 0.5 * (1.0 + t) + 0.5 * u * (1.0 - t * t) * (0.7978845608 + 0.1070322243 * (u * u))


def feed_back_kernel(
    which, dy_ref, upward_ref, hidden_ref, small_own, small_got,
    mixer_own, mixer_got, up_own, up_got, down_own, down_got, *rest, tile, extra,
):
    (
        dup_ref, dhidden_ref, low_ref, datt_ref, gain_grad_ref, token_ref,
        mixer, up, down, sems,
    ) = rest[extra:]
    token_ref[0] = 0
    pairs = ((down_own, down_got), (up_own, up_got), (mixer_own, mixer_got))
    for i, (pair, buffer) in enumerate(zip(pairs, (down, up, mixer))):
        fetch(pair, which[0], buffer, sems.at[i])
    gain = small_of(small_own, small_got, which[0])(GAIN_B, 1)
    dy = dy_ref[...]
    fetched(pairs[0], down, sems.at[0])
    grad = jnp.zeros(hidden_ref.shape, f32)
    for j in range(down.shape[0] // tile):
        span = slice(j * tile, (j + 1) * tile)
        dactive = dense_nt(dy, down[span, :])
        dup = (dactive * gelu_slope(upward_ref[:, span])).astype(bf16)
        dup_ref[:, span] = dup
        if j == 0:
            fetched(pairs[1], up, sems.at[1])
        grad = grad + dense_nt(dup, up[:, span])
    hidden = hidden_ref[...]
    inverse = rms_inverse(hidden)
    unit = hidden * inverse
    gain_grad_ref[...] = jnp.sum(grad * unit, axis=0, keepdims=True)
    scaled = grad * gain
    dhidden = dy.astype(f32) + inverse * (scaled - unit * jnp.mean(scaled * unit, axis=-1, keepdims=True))
    dhidden_ref[...] = dhidden
    low = dhidden.astype(bf16)
    low_ref[...] = low
    fetched(pairs[2], mixer, sems.at[2])
    datt_ref[...] = dense_nt(low, mixer[...]).astype(bf16)


def feed_back(which, dy, upward, hidden, smalls, weights, extras):
    count, width = dy.shape
    ff = upward.shape[1]
    shape = jax.ShapeDtypeStruct
    return pl.pallas_call(
        functools.partial(feed_back_kernel, tile=width, extra=len(extras)),
        in_specs=[SMEM_SPEC] + [VMEM_SPEC] * 5 + [HBM_SPEC] * (6 + len(extras)),
        out_specs=[VMEM_SPEC] * 5 + [SMEM_SPEC],
        out_shape=[
            shape((count, ff), bf16),
            shape((count, width), f32),
            shape((count, width), bf16),
            shape((count, width), bf16),
            shape((1, width), f32),
            TOKEN,
        ],
        scratch_shapes=[
            pltpu.VMEM((width, width), bf16),
            pltpu.VMEM((width, ff), bf16),
            pltpu.VMEM((ff, width), bf16),
            pltpu.SemaphoreType.DMA((3,)),
        ],
        compiler_params=pltpu.CompilerParams(vmem_limit_bytes=VMEM_BYTES),
        cost_estimate=pl.CostEstimate(
            flops=2 * count * width * (2 * ff + width), bytes_accessed=4 * width * ff, transcendentals=count * ff
        ),
    )(which, dy, upward, hidden, *smalls, *weights, *extras)


def attend_back_kernel(
    place, q_ref, datt_ref, u_ref, lse_ref, k_ref, v_ref, small_own, small_got, *rest, bq, bk, extra
):
    (
        dq_ref, keep_ref, send_ref, pre_grad_ref, post_grad_ref, token_ref,
        qp, dp, dk, dv, w, delta,
    ) = rest[extra:]
    token_ref[0] = 0
    step = pl.program_id(0)
    length, which, q_start = place[0], place[1], place[2 + step]
    small = small_of(small_own, small_got, which)
    pre, post = small(PRE, HEADS), small(POST, HEADS)

    @pl.when(step == 0)
    def _():
        dk[...] = jnp.zeros_like(dk)
        dv[...] = jnp.zeros_like(dv)
        pre_grad_ref[...] = jnp.zeros_like(pre_grad_ref)
        post_grad_ref[...] = jnp.zeros_like(post_grad_ref)

    q32 = q_ref[...].astype(f32)
    datt = datt_ref[...].astype(f32)
    for h in range(HEADS):
        part = slice(h * bq, (h + 1) * bq)
        qp[part, :] = (q32 * pre[h : h + 1, :]).astype(bf16)
        scaled = datt * post[h : h + 1, :]
        dp[part, :] = scaled.astype(bf16)
        u = u_ref[part, :].astype(f32)
        delta[part, :] = jnp.broadcast_to(jnp.sum(scaled * u, axis=-1, keepdims=True), (bq, 128))
        post_grad_ref[h : h + 1, :] += jnp.sum(datt * u, axis=0, keepdims=True)
    w[...] = jnp.zeros_like(w)
    blocks = (jnp.minimum(q_start + bq, length) + bk - 1) // bk

    def block(kb, c):
        span = pl.ds(pl.multiple_of(kb * bk, bk), bk)
        bias = bias_of(q_start, kb * bk, length, bq, bk)
        k_blk, v_blk = k_ref[span, :], v_ref[span, :]
        logits = dense_nt(qp[...], k_blk)
        logits = (logits.reshape(HEADS, bq, bk) + bias[None]).reshape(HEADS * bq, bk)
        grad = dense_nt(dp[...], v_blk)
        lse, spread = lse_ref[...], delta[...]
        attention, dlog = [], []
        for x, g in zip(lane_parts(logits), lane_parts(grad)):
            a = jnp.exp(x - lse)
            attention.append(a.astype(bf16))
            dlog.append((a * (g - spread)).astype(bf16))
        attention, dlog = jnp.concatenate(attention, axis=1), jnp.concatenate(dlog, axis=1)
        dv[span, :] += dense_tn(attention, dp[...])
        dk[span, :] += dense_tn(dlog, qp[...])
        w[...] += dense(dlog, k_blk)
        return c

    lax.fori_loop(0, blocks, block, 0)
    dq = jnp.zeros_like(q32)
    for h in range(HEADS):
        part = w[h * bq : (h + 1) * bq, :]
        dq = dq + part * pre[h : h + 1, :]
        pre_grad_ref[h : h + 1, :] += jnp.sum(part * q32, axis=0, keepdims=True)
    dq_ref[...] = dq.astype(bf16)

    for section, (kept, sent) in enumerate(((dk, dv), (dv, dk))):

        @pl.when((step == pl.num_programs(0) - 1) & (place[4] == section))
        def _(kept=kept, sent=sent):
            keep_ref[...] = kept[...].astype(bf16)
            send_ref[...] = sent[...].astype(bf16)


def attend_back(place, q, datt, u, lse, k, v, smalls, bk, extras):
    count, width = q.shape
    seq = k.shape[0]
    bq = count // 2
    full = lambda i, place: (0, 0)
    row = lambda i, place: (i, 0)
    shape = jax.ShapeDtypeStruct
    return pl.pallas_call(
        functools.partial(attend_back_kernel, bq=bq, bk=bk, extra=len(extras)),
        grid_spec=pltpu.PrefetchScalarGridSpec(
            num_scalar_prefetch=1,
            grid=(2,),
            in_specs=[
                pl.BlockSpec((bq, width), row),
                pl.BlockSpec((bq, width), row),
                pl.BlockSpec((HEADS * bq, width), row),
                pl.BlockSpec((HEADS * bq, 128), row),
                pl.BlockSpec((seq, width), full),
                pl.BlockSpec((seq, width), full),
                pl.BlockSpec((SMALL_ROWS, width), full),
                pl.BlockSpec((SMALL_ROWS, width), full),
            ]
            + [HBM_SPEC] * len(extras),
            out_specs=[
                pl.BlockSpec((bq, width), row),
                pl.BlockSpec((seq, width), full),
                pl.BlockSpec((seq, width), full),
                pl.BlockSpec((HEADS, width), full),
                pl.BlockSpec((HEADS, width), full),
                SMEM_SPEC,
            ],
            scratch_shapes=[
                pltpu.VMEM((HEADS * bq, width), bf16),
                pltpu.VMEM((HEADS * bq, width), bf16),
                pltpu.VMEM((seq, width), f32),
                pltpu.VMEM((seq, width), f32),
                pltpu.VMEM((HEADS * bq, width), f32),
                pltpu.VMEM((HEADS * bq, 128), f32),
            ],
        ),
        out_shape=[
            shape((count, width), bf16),
            shape((seq, width), bf16),
            shape((seq, width), bf16),
            shape((HEADS, width), f32),
            shape((HEADS, width), f32),
            TOKEN,
        ],
        compiler_params=pltpu.CompilerParams(vmem_limit_bytes=VMEM_BYTES),
        cost_estimate=pl.CostEstimate(
            flops=10 * HEADS * count * seq * width * 5 // 8,
            bytes_accessed=10 * seq * width + 2 * HEADS * count * width,
            transcendentals=HEADS * count * seq * 5 // 8,
        ),
    )(place, q, datt, u, lse, k, v, *smalls, *extras)


def swap_section(x):
    return lax.ppermute(x, "section", [(0, 1), (1, 0)])


def xor_permute(x, axis, by):
    return lax.ppermute(x, axis, [(i, i ^ by) for i in range(lax.axis_size(axis))])


def from_xor_order(x, index):
    places = range(x.shape[0])
    return jnp.concatenate([lax.dynamic_index_in_dim(x, index ^ i, 0) for i in places])


def token_kernel(*refs):
    refs[-1][0] = 0


def token_after(*arrays):
    return pl.pallas_call(
        token_kernel,
        in_specs=[HBM_SPEC] * len(arrays),
        out_specs=SMEM_SPEC,
        out_shape=TOKEN,
    )(*arrays)[0]


class Summer:
    def __init__(self, blocks, backwards):
        self.dp_count, ctx_count = blocks[0].shape[:2]
        bits = [1 << i for i in range(ctx_count.bit_length() - 1)]
        self.left = bits[::-1]
        self.order = bits[::-1] if backwards else bits
        self.parts = [x.reshape((self.dp_count,) + (2,) * len(bits) + x.shape[2:]) for x in blocks]

    def send(self, token=0):
        bit, self.order = self.order[0], self.order[1:]
        self.axis = 1 + self.left.index(bit)
        self.left = [b for b in self.left if b != bit]
        self.mine = (lax.axis_index("ctx") // bit) % 2
        at = 1 - self.mine + token
        sent = [lax.dynamic_index_in_dim(x, at, self.axis, keepdims=False) for x in self.parts]
        sent = sent[0] if len(sent) == 1 else jnp.concatenate(sent, axis=-1)
        self.got = xor_permute(sent, "ctx", bit)
        return [sent]

    def add(self, token):
        at, parts = 0, []
        for x in self.parts:
            kept = lax.dynamic_index_in_dim(x, self.mine + token, self.axis, keepdims=False)
            got = self.got[..., at : at + x.shape[-1]]
            at += x.shape[-1]
            parts.append((kept.astype(f32) + got.astype(f32)).astype(bf16))
        self.parts = parts

    def rest(self, token):
        self.add(token)
        while self.order:
            self.send()
            self.add(0)


class LastSum:
    def __init__(self, summers, rows):
        pieces = []
        for x in [x for one in summers for x in one.parts]:
            pieces += [x[:, i : i + rows] for i in range(0, x.shape[1], rows)]
        self.part = jnp.concatenate(pieces, axis=-1)

    def send(self):
        dp = lax.axis_index("dp")
        sent = [
            lax.dynamic_index_in_dim(self.part, dp ^ by, 0, keepdims=False)
            for by in range(1, self.part.shape[0])
        ]
        self.got = [xor_permute(x, "dp", by) for by, x in enumerate(sent, 1)]
        return sent

    def finish(self, token):
        total = lax.dynamic_index_in_dim(self.part, lax.axis_index("dp") + token, 0, keepdims=False)
        total = total.astype(f32)
        for got in self.got:
            total = total + got.astype(f32)
        return total


def all_sum(vector):
    for axis in ("ctx", "dp"):
        parts = [xor_permute(vector, axis, by) for by in range(1, lax.axis_size(axis))]
        for part in parts:
            vector = vector + part
    return vector


def local(
    inputs, lengths, cotangent, first_gain, joint_weight, pre_mix, post_mix,
    mixer_weight, second_gain, up_weight, down_weight,
):
    s = lax.axis_index("section")
    ctx = lax.axis_index("ctx")
    n = lax.axis_size("ctx")
    dp_count = lax.axis_size("dp")
    chips = n // 2
    micro_count, row_count, local_len, width = inputs.shape
    ff = up_weight.shape[2]
    seq = local_len * n
    blk = local_len // 2
    m = ctx // chips
    xi = ctx % chips
    core = xi * 2 + s
    zero = jnp.zeros((), jnp.int32)
    inputs = inputs.reshape(micro_count, 2, blk, width)
    cotangent = cotangent.reshape(micro_count, 2, blk, width)
    pick = lambda arr, i: lax.dynamic_index_in_dim(arr, i, 0, keepdims=False)

    spread = lambda mix: jnp.dot(mix, jnp.repeat(jnp.eye(HEADS, dtype=f32), HEAD, axis=1), precision=lax.Precision.HIGHEST)
    lines = lambda x, size: jnp.pad(x, ((0, size - x.shape[0]), (0, 0)))
    gains = jnp.concatenate([first_gain, second_gain]).astype(f32)
    small_own = jnp.concatenate(
        [lines(gains, PRE), lines(0.125 * spread(pre_mix[0].T), POST - PRE), lines(spread(post_mix[0]), SMALL_ROWS - POST)]
    )
    smalls = (small_own, swap_section(small_own))
    joints, mixers, ups, downs = (
        (w, swap_section(w)) for w in (joint_weight, mixer_weight, up_weight, down_weight)
    )

    mine = pick(inputs, m)
    pieces = []
    for d in range(1, n):
        target = m ^ (1 if d >= chips else 0)
        pieces.append(xor_permute(pick(pick(inputs, target), s), "ctx", d))
    other_pieces = [swap_section(x) for x in pieces]
    own_half = jnp.stack([pick(mine, s)] + pieces)
    other_half = jnp.stack([pick(mine, 1 - s)] + other_pieces)
    first, second = jnp.where(s == 0, own_half, other_half), jnp.where(s == 0, other_half, own_half)
    x_all = from_xor_order(jnp.stack([first, second], axis=1), ctx).reshape(seq, width)

    length = pick(lengths.reshape(-1), m)
    low_start = core * blk
    high_start = (2 * n - 1 - core) * blk
    bk = min(256, seq)
    places = [
        jnp.stack([length, (s != layer).astype(jnp.int32), low_start, high_start, s]).astype(jnp.int32)
        for layer in range(2)
    ]

    def own_rows(x):
        return jnp.concatenate(
            [
                lax.dynamic_slice_in_dim(x, low_start, blk, 0),
                lax.dynamic_slice_in_dim(x, high_start, blk, 0),
            ]
        )

    def gather_row(x):
        got = [xor_permute(x, "ctx", d) for d in range(1, chips)]
        own = jnp.stack([x] + got)
        other = jnp.stack([swap_section(y) for y in [x] + got])
        first, second = jnp.where(s == 0, own, other), jnp.where(s == 0, other, own)
        cores = from_xor_order(jnp.stack([first, second], axis=1), xi).reshape(n, 2, blk, width)
        return jnp.concatenate([cores[i, 0] for i in range(n)] + [cores[n - 1 - i, 1] for i in range(n)])

    def scatter_row(x, token):
        parts = x.astype(bf16).reshape(2 * n, blk, width)
        cores = jnp.stack([parts[i if h == 0 else 2 * n - 1 - i] for i in range(n) for h in range(2)])
        cores = cores.reshape(chips, 2, 2, blk, width)
        kept = lax.dynamic_index_in_dim(cores, s, 1, keepdims=False)
        got = swap_section(lax.dynamic_index_in_dim(cores, 1 - s, 1, keepdims=False))
        low = (kept.astype(f32) + got.astype(f32)).astype(bf16)
        total = pick(low, xi).astype(f32)
        for d in range(1, chips):
            total = total + xor_permute(pick(low, xi ^ d), "ctx", d).astype(f32)
        return total.reshape(2 * blk, width), low

    def forward(layer, x_all, x_own, extras):
        attended, q, normed_own, token, normed_all, k, v, u, lse = attend(
            places[layer], x_all, 2 * blk, smalls, joints, bk, extras[0]
        )
        weights = [x for pair in (mixers, ups, downs) for x in pair]
        out, hidden, normed_two, upward, active, token = feed(
            places[layer][1:2], x_own, attended, smalls, weights, ff, extras[1]
        )
        rows = [(x, swap_section(x)) for x in (active, normed_two, attended, normed_own)]
        return out, (q, k, v, u, lse, hidden, upward, rows, normed_all)

    def half(x, which):
        return lax.dynamic_slice_in_dim(x, which * (x.shape[1] // 2), x.shape[1] // 2, 1)

    def chip_half(x, token):
        return half(x, s + token), swap_section(half(x, 1 - s - token))

    def product(left, right):
        return (dense_tn(left[0], right[0]) + dense_tn(left[1], right[1])).astype(bf16)

    def blocks_of(grad):
        return grad.reshape(dp_count, n, grad.shape[0] // (dp_count * n), grad.shape[1])

    shard = width // (dp_count * n)

    def backward(layer, dy, x_own, kept, earlier):
        q, k, v, u, lse, hidden, upward, rows, normed_all = kept
        rows_active, rows_two, rows_attended, rows_normed = rows
        here = s == layer
        joint_w = jnp.where(here, joints[0][0], joints[1][0])
        q_w = joint_w[:, :width]
        kv_w = lax.dynamic_slice_in_dim(joint_w, width * (1 + s), width, 1)
        gain_a = jnp.where(here, smalls[0][GAIN_A], smalls[1][GAIN_A])
        down_sum = Summer([blocks_of(product(rows_active, chip_half(dy, zero)))], False)
        extras = down_sum.send() + earlier[0]()
        weights = [x for pair in (mixers, ups, downs) for x in pair]
        dup, dhidden, dhidden_low, datt, gain_b_grad, token = feed_back(
            places[layer][1:2], dy, upward, hidden, smalls, weights, extras
        )
        dup_half = chip_half(dup, zero)
        dhidden_half = chip_half(dhidden_low, zero)
        extras = earlier[1](token)
        up_sum = Summer(
            [blocks_of(product(rows_two, dup_half)), blocks_of(product(rows_attended, dhidden_half))], True
        )
        extras = extras + up_sum.send()
        dq, dkv_keep, dkv_send, pre_rows, post_rows, token = attend_back(
            places[layer], q, datt, u, lse, k, v, smalls, bk, extras
        )
        token = token_after(token, dkv_send, down_sum.got, up_sum.got, *earlier[2]())
        got = swap_section(dkv_send)
        dq_half = chip_half(dq, token)
        for one in (down_sum, up_sum):
            one.add(token)
        earlier[3](token, (down_sum, up_sum))
        dkv = (dkv_keep.astype(f32) + got.astype(f32)).astype(bf16)
        scattered, travels = scatter_row(dense_nt(dkv, kv_w), token)
        cut = 2 * width // 3
        kv_part = dense_tn(normed_all, dkv).astype(bf16)
        q_part = product(rows_normed, dq_half)
        kv_sum = Summer([blocks_of(kv_part)[..., :cut]], False)
        q_sum = Summer([blocks_of(kv_part)[..., cut:], blocks_of(q_part)], True)
        dnormed = scattered + dense_nt(dq, q_w)
        values = x_own.astype(f32)
        inverse = rms_inverse(values)
        unit = values * inverse
        gain_a_grad = jnp.sum(dnormed * unit, axis=0)
        scaled = dnormed * gain_a
        dfront = inverse * (scaled - unit * jnp.mean(scaled * unit, axis=-1, keepdims=True))
        small = (gain_a_grad, gain_b_grad.reshape(-1), pre_rows, post_rows)
        sums = (down_sum, up_sum, kv_sum, q_sum)
        return dhidden + dfront, sums, small, (scattered, travels, kv_part, q_part)

    x0_own = own_rows(x_all)
    x1_own, kept0 = forward(0, x_all, x0_own, ((), ()))
    x1_all = gather_row(x1_own)

    low_chip = ctx < chips
    there = [(i, chips + i) for i in range(chips)] + [(n - 1 - i, i) for i in range(chips)]
    here = [(n - 1 - i, chips + i) for i in range(chips)] + [(i, i) for i in range(chips)]
    first = jnp.where(low_chip, s, 1 - s) + token_after(x1_all)
    halves = lax.dynamic_index_in_dim(cotangent, first, 1, keepdims=False)
    ones, twos = jnp.where(low_chip, halves[1], halves[0]), jnp.where(low_chip, halves[0], halves[1])
    one, two = lax.ppermute(ones, "ctx", there), lax.ppermute(twos, "ctx", here)
    dy1 = jnp.concatenate([jnp.where(m == 0, two, one), jnp.where(m == 0, one, two)])
    y, kept1 = forward(1, x1_all, x1_own, ((ones, twos), (dy1,)))

    def send_home(x):
        x = x.reshape(2, blk, width)
        one = lax.ppermute(jnp.where(m == 0, x[1], x[0]), "ctx", [(b, a) for a, b in there])
        two = lax.ppermute(jnp.where(m == 0, x[0], x[1]), "ctx", [(b, a) for a, b in here])
        return jnp.where(low_chip, jnp.stack([two, one]), jnp.stack([one, two]))

    nothing = lambda *_: []
    dx1, (down1, up1, kv1, q1), small1, (arrived, *_) = backward(
        1, dy1, x1_own, kept1, (nothing, nothing, nothing, nothing)
    )
    dy0 = dx1.astype(bf16)
    arrived = token_after(arrived)
    state = {}

    def at_first():
        return down1.send(arrived) + up1.send(arrived) + kv1.send(arrived) + q1.send(arrived)

    def after_feed(token):
        token = token_after(token, down1.got, up1.got)
        for one in (down1, up1):
            one.rest(token)
        state["last1"] = LastSum([down1, up1], shard)
        return state["last1"].send()

    def after_attention():
        return [kv1.got, q1.got] + state["last1"].got

    def at_last(token, sums):
        for one in (kv1, q1):
            one.add(token)
            one.send()
        for one in sums:
            one.send()

    dx0, (down0, up0, kv0, q0), small0, (scattered, travels, kv_part, q_part) = backward(
        0, dy0, x0_own, kept0, (at_first, after_feed, after_attention, at_last)
    )
    for one in (kv0, q0):
        one.send()
    token = token_after(travels, kv_part, q_part)
    for one in (down0, up0, kv1, q1):
        one.rest(token)
    big = LastSum([down0, up0, kv1, q1], shard)
    sent = big.send()
    token = token_after(*sent)
    for one in (kv0, q0):
        one.add(token)
        one.send()
    dx_home = send_home(dx0.astype(bf16))
    y_home = send_home(y + token.astype(bf16))

    heads_of = jnp.repeat(jnp.eye(HEADS, dtype=f32), HEAD, axis=0)

    def small_sums(gain_a_grad, gain_b_grad, pre_rows, post_rows):
        per_head = lambda rows: jnp.dot(rows, heads_of, precision=lax.Precision.HIGHEST)
        pre, post = 0.125 * per_head(pre_rows).T, per_head(post_rows)
        return jnp.concatenate([gain_a_grad, gain_b_grad, pre.reshape(-1), post.reshape(-1)])

    small0, small1 = small_sums(*small0), small_sums(*small1)
    small_got = swap_section(jnp.where(s == 0, small1, small0))
    small = all_sum(jnp.where(s == 0, small0, small1) + small_got)
    for one in (kv0, q0):
        one.rest(zero)
    joint0 = LastSum([kv0, q0], shard)
    joint0.send()

    got = swap_section(jnp.where(s == 0, y_home, dx_home))
    held = jnp.where(s == 0, dx_home, y_home)
    is_first = jnp.where(low_chip, s, 1 - s) == 0
    ends = jnp.stack([jnp.where(is_first, held, got), jnp.where(is_first, got, held)], axis=1)
    ends = ends.reshape(1, micro_count, row_count, local_len, width)

    at = (lax.axis_index("dp") * n + ctx) * shard
    gain_a_out = lax.dynamic_slice_in_dim(small[:width], at, shard, 0)
    gain_b_out = lax.dynamic_slice_in_dim(small[width : 2 * width], at, shard, 0)
    pre_out = small[2 * width : 2 * width + HEADS * HEADS].reshape(1, HEADS, HEADS)
    post_out = small[2 * width + HEADS * HEADS :].reshape(1, HEADS, HEADS)

    big0_columns = state["last1"].part.shape[-1]
    big = big.finish(zero)
    big0, joint1 = big[:, :big0_columns], big[:, big0_columns:]
    pairs = ((big0, state["last1"].finish(zero)), (joint0.finish(zero), joint1))
    outs = []
    for at_zero, at_one in pairs:
        other = swap_section(jnp.where(s == 0, at_one, at_zero))
        own = jnp.where(s == 0, at_zero, at_one)
        outs.append((jnp.where(s == 0, own, other), jnp.where(s == 0, other, own)))
    (big_a, big_b), (joint_a, joint_b) = outs
    half_d, half_ff, times = width // 2, ff // 2, ff // width
    side = lambda *cuts: jnp.concatenate([x[:, at : at + size] for x, at, size in cuts], axis=1)
    down_out = jnp.concatenate([side((big_a, i * half_d, half_d), (big_b, i * half_d, half_d)) for i in range(times)])
    at = times * half_d
    up_out = side((big_a, at, half_ff), (big_b, at, half_ff))
    mixer_out = side((big_a, at + half_ff, half_d), (big_b, at + half_ff, half_d))
    joint_out = side((joint_a, width, half_d), (joint_b, width, half_d), (joint_a, 0, width), (joint_b, 0, width))
    return (
        ends,
        gain_a_out[None],
        joint_out[None],
        pre_out,
        post_out,
        mixer_out[None],
        gain_b_out[None],
        up_out[None],
        down_out[None],
    )


def solution(mesh):
    in_specs = (
        P(None, "dp", "ctx", None),
        P(None, "dp"),
        P(None, "dp", "ctx", None),
        P("section", None),
        P("section", None, None),
        P("section", None, None),
        P("section", None, None),
        P("section", None, None),
        P("section", None),
        P("section", None, None),
        P("section", None, None),
    )
    out_specs = (
        P("section", None, "dp", "ctx", None),
        P("section", ("dp", "ctx")),
        P("section", ("dp", "ctx"), None),
        P("section", None, None),
        P("section", None, None),
        P("section", ("dp", "ctx"), None),
        P("section", ("dp", "ctx")),
        P("section", ("dp", "ctx"), None),
        P("section", ("dp", "ctx"), None),
    )
    return jax.shard_map(local, mesh=mesh, in_specs=in_specs, out_specs=out_specs, check_vma=False)
```

```python
import functools
import math
import types

import jax
import jax.numpy as jnp
from jax import lax
from jax.experimental import pallas as pl
from jax.experimental.pallas import tpu as pltpu
from jax.sharding import PartitionSpec as P

HEADS = 12
HEAD = 64
eps = 1e-06
MASKED = -1e30
f32 = jnp.float32
bf16 = jnp.bfloat16
MIB = 1024 * 1024
SMALL_VMEM = 36 * MIB
BIG_VMEM = 60 * MIB


def dense(left_side, right_side):
    return jnp.dot(left_side, right_side, preferred_element_type=f32)


def dense_tn(left_side, right_side):
    return lax.dot_general(
        left_side, right_side, (((0,), (0,)), ((), ())), preferred_element_type=f32
    )


def dense_nt(left_side, right_side):
    return lax.dot_general(
        left_side, right_side, (((1,), (1,)), ((), ())), preferred_element_type=f32
    )


GAIN_A, GAIN_B, PRE, POST = 0, 1, 8, 24
SMALL_ROWS = 40


def small_of(own, got, which):
    return lambda at, size: jnp.where(which == 0, own[at : at + size, :], got[at : at + size, :])


def rms_inverse(values):
    return lax.rsqrt(jnp.mean(values * values, axis=-1, keepdims=True) + eps)


def lane_parts(x):
    return [x[:, i : i + 128] for i in range(0, x.shape[1], 128)]


def bias_of(q_start, k_start, length, bq, bk):
    rows = q_start + lax.broadcasted_iota(jnp.int32, (bq, bk), 0)
    cols = k_start + lax.broadcasted_iota(jnp.int32, (bq, bk), 1)
    return jnp.where((cols <= rows) & (cols < length), 0.0, MASKED).astype(f32)


def attend_kernel(place, small_own, small_got, joint_own, joint_got, *rest, bk, count_in):
    (
        att_ref, q_ref, own_ref, x_ref, token_ref, normed_hbm, k_hbm, v_hbm, u_hbm, lse_hbm,
        joint, raw, normed, k, v, u, lse, qp, logit, total, top, norm, sems,
    ) = rest[count_in:]
    token_ref[0] = 0
    length, which = place[0], place[1]
    fetch((joint_own, joint_got), which, joint, sems.at[0])
    seq, width = normed.shape
    count = att_ref.shape[0]
    bq = count // 2
    small = small_of(small_own, small_got, which)
    gain, pre, post = small(GAIN_A, 1), small(PRE, HEADS), small(POST, HEADS)
    at = 5
    for piece in rest[:count_in]:
        for j in range(piece.shape[0] // bq):
            x = piece[j * bq : (j + 1) * bq, :]
            span = pl.ds(pl.multiple_of(place[at] * bq, bq), bq)
            raw[span, :] = x
            x = x.astype(f32)
            normed[span, :] = (x * rms_inverse(x) * gain).astype(bf16)
            at += 1
    for i in range(2):
        span = pl.ds(pl.multiple_of(place[2 + i], bq), bq)
        own_ref[i * bq : (i + 1) * bq, :] = normed[span, :]
        x_ref[i * bq : (i + 1) * bq, :] = raw[span, :]
    fetched((joint_own, joint_got), joint, sems.at[0])
    cut = width // 3
    for i in range(3):
        cols = slice(width + i * cut, width + (i + 1) * cut)
        k[:, i * cut : (i + 1) * cut] = dense(normed[...], joint[:, cols]).astype(bf16)
    for i in range(3):
        cols = slice(2 * width + i * cut, 2 * width + (i + 1) * cut)
        v[:, i * cut : (i + 1) * cut] = dense(normed[...], joint[:, cols]).astype(bf16)
    q_ref[...] = dense(own_ref[...], joint[:, :width]).astype(bf16)
    outs = [
        pltpu.make_async_copy(a, b, sems.at[1 + i])
        for i, (a, b) in enumerate(((normed, normed_hbm), (k, k_hbm), (v, v_hbm)))
    ]
    for out in outs:
        out.start()

    def rows_step(step, carry):
        q_start = place[2 + step]
        mine = pl.ds(pl.multiple_of(step * bq, bq), bq)
        q32 = q_ref[mine, :].astype(f32)
        for h in range(HEADS):
            qp[h * bq : (h + 1) * bq, :] = (q32 * pre[h : h + 1, :]).astype(bf16)
        blocks = (jnp.minimum(q_start + bq, length) + bk - 1) // bk
        top[...] = jnp.full_like(top, MASKED)
        total[...] = jnp.zeros_like(total)
        norm[...] = jnp.zeros_like(norm)

        def score(kb, c):
            bias = bias_of(q_start, kb * bk, length, bq, bk)
            tile = dense_nt(qp[...], k[pl.ds(pl.multiple_of(kb * bk, bk), bk), :])
            tile = (tile.reshape(HEADS, bq, bk) + bias[None]).reshape(HEADS * bq, bk)
            logit[kb] = tile
            top[...] = functools.reduce(jnp.maximum, lane_parts(tile), top[...])
            return c

        lax.fori_loop(0, blocks, score, 0)
        highest = jnp.max(top[...], axis=-1, keepdims=True)
        top[...] = jnp.broadcast_to(highest, top.shape)

        def apply(kb, c):
            high = top[...]
            parts = [jnp.exp(x - high) for x in lane_parts(logit[kb])]
            norm[...] = functools.reduce(jnp.add, parts, norm[...])
            e = jnp.concatenate([x.astype(bf16) for x in parts], axis=1)
            total[...] += dense(e, v[pl.ds(pl.multiple_of(kb * bk, bk), bk), :])
            return c

        lax.fori_loop(0, blocks, apply, 0)
        sums = jnp.sum(norm[...], axis=-1, keepdims=True)
        scale = 1.0 / sums
        rows = pl.ds(pl.multiple_of(step * HEADS * bq, HEADS * bq), HEADS * bq)
        lse[rows, :] = jnp.broadcast_to(highest + jnp.log(sums), top.shape)
        att = jnp.zeros((bq, width), f32)
        for g in range(HEADS):
            part = total[g * bq : (g + 1) * bq, :] * scale[g * bq : (g + 1) * bq]
            u[pl.ds(pl.multiple_of(step * HEADS * bq + g * bq, bq), bq), :] = part.astype(bf16)
            att = att + part * post[g : g + 1, :]
        att_ref[mine, :] = att.astype(bf16)
        return carry

    lax.fori_loop(0, 2, rows_step, 0)
    outs += [pltpu.make_async_copy(u, u_hbm, sems.at[4]), pltpu.make_async_copy(lse, lse_hbm, sems.at[5])]
    for out in outs[3:]:
        out.start()
    for out in outs:
        out.wait()


VMEM_SPEC = pl.BlockSpec(memory_space=pltpu.VMEM)
ANY_SPEC = pl.BlockSpec(memory_space=pl.ANY)
HBM_SPEC = pl.BlockSpec(memory_space=pltpu.HBM)
SMEM_SPEC = pl.BlockSpec(memory_space=pltpu.SMEM)
TOKEN = jax.ShapeDtypeStruct((1,), jnp.int32)

LARGE = 64 * 1024
SMALL_COST = pl.CostEstimate(flops=0, bytes_accessed=0, transcendentals=0)


def in_hbm(spec, x):
    return spec in (VMEM_SPEC, HBM_SPEC) and math.prod(x.shape) >= LARGE


def from_hbm(spec, x):
    return pltpu.with_memory_space_constraint(x, pltpu.HBM) if in_hbm(spec, x) else x


def result_in_hbm(spec, x):
    return pltpu.HBM(x.shape, x.dtype) if in_hbm(spec, x) else x


def one_step(kernel, *, in_specs, out_specs, out_shape, **rest):
    def whole(spec, x):
        if spec is not VMEM_SPEC:
            return spec
        zeros = (0,) * len(x.shape)
        return pl.BlockSpec(x.shape, lambda i: zeros, pipeline_mode=pl.Buffered(1))

    def run(*args):
        return pl.pallas_call(
            kernel,
            cost_estimate=SMALL_COST,
            grid=(1,),
            in_specs=[whole(*x) for x in zip(in_specs, args, strict=True)],
            out_specs=[whole(*x) for x in zip(out_specs, out_shape, strict=True)],
            out_shape=[result_in_hbm(*x) for x in zip(out_specs, out_shape)],
            **rest,
        )(*[from_hbm(*x) for x in zip(in_specs, args)])

    return run


def attend(place, pieces, count, smalls, joints, bk):
    width = pieces[0].shape[1]
    seq = sum(x.shape[0] for x in pieces)
    bq = count // 2
    shape = jax.ShapeDtypeStruct
    return one_step(
        functools.partial(attend_kernel, bk=bk, count_in=len(pieces)),
        in_specs=[SMEM_SPEC] + [VMEM_SPEC] * 2 + [HBM_SPEC] * 2 + [VMEM_SPEC] * len(pieces),
        out_specs=[VMEM_SPEC] * 4 + [SMEM_SPEC] + [HBM_SPEC] * 5,
        out_shape=[shape((count, width), bf16)] * 4
        + [TOKEN]
        + [shape((seq, width), bf16)] * 3
        + [shape((HEADS * count, width), bf16), shape((HEADS * count, 128), f32)],
        scratch_shapes=[
            pltpu.VMEM((width, 3 * width), bf16),
            pltpu.VMEM((seq, width), bf16),
            pltpu.VMEM((seq, width), bf16),
            pltpu.VMEM((seq, width), bf16),
            pltpu.VMEM((seq, width), bf16),
            pltpu.VMEM((HEADS * count, width), bf16),
            pltpu.VMEM((HEADS * count, 128), f32),
            pltpu.VMEM((HEADS * bq, width), bf16),
            pltpu.VMEM((seq // bk, HEADS * bq, bk), f32),
            pltpu.VMEM((HEADS * bq, width), f32),
            pltpu.VMEM((HEADS * bq, 128), f32),
            pltpu.VMEM((HEADS * bq, 128), f32),
            pltpu.SemaphoreType.DMA((6,)),
        ],
        compiler_params=pltpu.CompilerParams(vmem_limit_bytes=BIG_VMEM),
    )(place, *smalls, *joints, *pieces)


def feed_kernel(
    which, x_ref, att_ref, small_own, small_got,
    mixer_own, mixer_got, up_own, up_got, down_own, down_got, *rest, tile, extra,
):
    (
        out_ref, hidden_ref, two_ref, upward_hbm, active_hbm, token_ref,
        mixer, up, down, upward, active, sems,
    ) = rest[extra:]
    token_ref[0] = 0
    pairs = ((mixer_own, mixer_got), (up_own, up_got), (down_own, down_got))
    buffers = (mixer, up, down)
    for i in range(3):
        fetch(pairs[i], which[0], buffers[i], sems.at[i])
    gain = small_of(small_own, small_got, which[0])(GAIN_B, 1)
    fetched(pairs[0], mixer, sems.at[0])
    hidden = x_ref[...].astype(f32) + dense(att_ref[...], mixer[...])
    hidden_ref[...] = hidden
    two = (hidden * rms_inverse(hidden) * gain).astype(bf16)
    two_ref[...] = two
    fetched(pairs[1], up, sems.at[1])
    result, outs = hidden, []
    for j in range(down.shape[0] // tile):
        span = slice(j * tile, (j + 1) * tile)
        u = dense(two, up[:, span])
        upward[:, span] = u
        act = (0.5 * u * (1.0 + jnp.tanh(0.7978845608 * (u + 0.044715 * (u * u * u))))).astype(bf16)
        active[:, span] = act
        if j == 0:
            fetched(pairs[2], down, sems.at[2])
        result = result + dense(act, down[span, :])
    outs = [pltpu.make_async_copy(upward, upward_hbm, sems.at[3]), pltpu.make_async_copy(active, active_hbm, sems.at[4])]
    for out in outs:
        out.start()
    out_ref[...] = result.astype(bf16)
    for out in outs:
        out.wait()


def feed(which, x, attended, smalls, weights, ff, extras):
    count, width = x.shape
    shape = jax.ShapeDtypeStruct
    return one_step(
        functools.partial(feed_kernel, tile=width, extra=len(extras)),
        in_specs=[SMEM_SPEC] + [VMEM_SPEC] * 4 + [HBM_SPEC] * (6 + len(extras)),
        out_specs=[VMEM_SPEC] * 3 + [HBM_SPEC] * 2 + [SMEM_SPEC],
        out_shape=[
            shape((count, width), bf16),
            shape((count, width), f32),
            shape((count, width), bf16),
            shape((count, ff), f32),
            shape((count, ff), bf16),
            TOKEN,
        ],
        scratch_shapes=[
            pltpu.VMEM((width, width), bf16),
            pltpu.VMEM((width, ff), bf16),
            pltpu.VMEM((ff, width), bf16),
            pltpu.VMEM((count, ff), f32),
            pltpu.VMEM((count, ff), bf16),
            pltpu.SemaphoreType.DMA((5,)),
        ],
        compiler_params=pltpu.CompilerParams(vmem_limit_bytes=SMALL_VMEM),
    )(which, x, attended, *smalls, *weights, *extras)


def fetch(pair, which, buffer, semaphore):
    for i, ref in enumerate(pair):

        @pl.when(which == i)
        def _(ref=ref):
            pltpu.make_async_copy(ref.at[0], buffer, semaphore).start()


def fetched(pair, buffer, semaphore):
    pltpu.make_async_copy(pair[0].at[0], buffer, semaphore).wait()


def gelu_slope(u):
    inner = 0.7978845608 * (u + 0.044715 * (u * u * u))
    t = jnp.tanh(inner)
    return 0.5 * (1.0 + t) + 0.5 * u * (1.0 - t * t) * (0.7978845608 + 0.1070322243 * (u * u))


def feed_back_kernel(
    which, dy_ref, upward_ref, hidden_ref, small_own, small_got,
    mixer_own, mixer_got, up_own, up_got, down_own, down_got, *rest, tile, extra,
):
    (
        keep_ref, send_ref, dhidden_ref, datt_ref, gain_grad_ref, token_ref,
        mixer, up, down, sems,
    ) = rest[extra:]
    token_ref[0] = 0
    width = dy_ref.shape[1]
    half_ff, half = down.shape[0] // 2, width // 2

    def put(value, number, at):
        for ref, equal in ((keep_ref, True), (send_ref, False)):

            @pl.when((which[1] == number) == equal)
            def _(ref=ref):
                ref[:, at : at + value.shape[1]] = value

    pairs = ((down_own, down_got), (up_own, up_got), (mixer_own, mixer_got))
    for i, (pair, buffer) in enumerate(zip(pairs, (down, up, mixer))):
        fetch(pair, which[0], buffer, sems.at[i])
    gain = small_of(small_own, small_got, which[0])(GAIN_B, 1)
    dy = dy_ref[...]
    fetched(pairs[0], down, sems.at[0])
    grad = jnp.zeros(hidden_ref.shape, f32)
    for j in range(down.shape[0] // tile):
        span = slice(j * tile, (j + 1) * tile)
        dactive = dense_nt(dy, down[span, :])
        dup = (dactive * gelu_slope(upward_ref[:, span])).astype(bf16)
        put(dup, j * tile // half_ff, j * tile % half_ff)
        if j == 0:
            fetched(pairs[1], up, sems.at[1])
        grad = grad + dense_nt(dup, up[:, span])
    hidden = hidden_ref[...]
    inverse = rms_inverse(hidden)
    unit = hidden * inverse
    gain_grad_ref[...] = jnp.sum(grad * unit, axis=0, keepdims=True)
    scaled = grad * gain
    dhidden = dy.astype(f32) + inverse * (scaled - unit * jnp.mean(scaled * unit, axis=-1, keepdims=True))
    dhidden_ref[...] = dhidden
    low = dhidden.astype(bf16)
    for i in range(2):
        put(low[:, i * half : (i + 1) * half], i, half_ff)
    fetched(pairs[2], mixer, sems.at[2])
    datt_ref[...] = dense_nt(low, mixer[...]).astype(bf16)


def feed_back(which, dy, upward, hidden, smalls, weights, extras):
    count, width = dy.shape
    ff = upward.shape[1]
    shape = jax.ShapeDtypeStruct
    return one_step(
        functools.partial(feed_back_kernel, tile=width, extra=len(extras)),
        in_specs=[SMEM_SPEC] + [VMEM_SPEC] * 5 + [HBM_SPEC] * (6 + len(extras)),
        out_specs=[VMEM_SPEC] * 5 + [SMEM_SPEC],
        out_shape=[
            shape((count, (ff + width) // 2), bf16),
            shape((count, (ff + width) // 2), bf16),
            shape((count, width), f32),
            shape((count, width), bf16),
            shape((1, width), f32),
            TOKEN,
        ],
        scratch_shapes=[
            pltpu.VMEM((width, width), bf16),
            pltpu.VMEM((width, ff), bf16),
            pltpu.VMEM((ff, width), bf16),
            pltpu.SemaphoreType.DMA((3,)),
        ],
        compiler_params=pltpu.CompilerParams(vmem_limit_bytes=SMALL_VMEM),
    )(which, dy, upward, hidden, *smalls, *weights, *extras)


def attend_back_kernel(
    place, q_ref, datt_ref, u_ref, lse_ref, k_ref, v_ref, small_own, small_got, *rest, bq, bk, extra
):
    (
        dq_ref, keep_ref, send_ref, pre_grad_ref, post_grad_ref, token_ref,
        qp, dp, dk, dv, w, delta,
    ) = rest[extra:]
    token_ref[0] = 0
    step = pl.program_id(0)
    length, which, q_start = place[0], place[1], place[2 + step]
    small = small_of(small_own, small_got, which)
    pre, post = small(PRE, HEADS), small(POST, HEADS)

    @pl.when(step == 0)
    def _():
        dk[...] = jnp.zeros_like(dk)
        dv[...] = jnp.zeros_like(dv)
        pre_grad_ref[...] = jnp.zeros_like(pre_grad_ref)
        post_grad_ref[...] = jnp.zeros_like(post_grad_ref)

    q32 = q_ref[...].astype(f32)
    datt = datt_ref[...].astype(f32)
    for h in range(HEADS):
        part = slice(h * bq, (h + 1) * bq)
        qp[part, :] = (q32 * pre[h : h + 1, :]).astype(bf16)
        scaled = datt * post[h : h + 1, :]
        dp[part, :] = scaled.astype(bf16)
        u = u_ref[part, :].astype(f32)
        delta[part, :] = jnp.broadcast_to(jnp.sum(scaled * u, axis=-1, keepdims=True), (bq, 128))
        post_grad_ref[h : h + 1, :] += jnp.sum(datt * u, axis=0, keepdims=True)
    w[...] = jnp.zeros_like(w)
    blocks = (jnp.minimum(q_start + bq, length) + bk - 1) // bk

    def block(kb, c):
        span = pl.ds(pl.multiple_of(kb * bk, bk), bk)
        bias = bias_of(q_start, kb * bk, length, bq, bk)
        k_blk, v_blk = k_ref[span, :], v_ref[span, :]
        logits = dense_nt(qp[...], k_blk)
        logits = (logits.reshape(HEADS, bq, bk) + bias[None]).reshape(HEADS * bq, bk)
        grad = dense_nt(dp[...], v_blk)
        lse, spread = lse_ref[...], delta[...]
        attention, dlog = [], []
        for x, g in zip(lane_parts(logits), lane_parts(grad)):
            a = jnp.exp(x - lse)
            attention.append(a.astype(bf16))
            dlog.append((a * (g - spread)).astype(bf16))
        attention, dlog = jnp.concatenate(attention, axis=1), jnp.concatenate(dlog, axis=1)
        dv[span, :] += dense_tn(attention, dp[...])
        dk[span, :] += dense_tn(dlog, qp[...])
        w[...] += dense(dlog, k_blk)
        return c

    lax.fori_loop(0, blocks, block, 0)
    dq = jnp.zeros_like(q32)
    for h in range(HEADS):
        part = w[h * bq : (h + 1) * bq, :]
        dq = dq + part * pre[h : h + 1, :]
        pre_grad_ref[h : h + 1, :] += jnp.sum(part * q32, axis=0, keepdims=True)
    dq_ref[...] = dq.astype(bf16)

    for section, (kept, sent) in enumerate(((dk, dv), (dv, dk))):

        @pl.when((step == pl.num_programs(0) - 1) & (place[4] == section))
        def _(kept=kept, sent=sent):
            keep_ref[...] = kept[...].astype(bf16)
            send_ref[...] = sent[...].astype(bf16)


def attend_back(place, q, datt, u, lse, k, v, smalls, bk, extras):
    count, width = q.shape
    seq = k.shape[0]
    bq = count // 2
    full = lambda i, place: (0, 0)
    row = lambda i, place: (i, 0)
    shape = jax.ShapeDtypeStruct
    return pl.pallas_call(
        cost_estimate=SMALL_COST,
        kernel=functools.partial(attend_back_kernel, bq=bq, bk=bk, extra=len(extras)),
        grid_spec=pltpu.PrefetchScalarGridSpec(
            num_scalar_prefetch=1,
            grid=(2,),
            in_specs=[
                pl.BlockSpec((bq, width), row),
                pl.BlockSpec((bq, width), row),
                pl.BlockSpec((HEADS * bq, width), row),
                pl.BlockSpec((HEADS * bq, 128), row),
                pl.BlockSpec((seq, width), full),
                pl.BlockSpec((seq, width), full),
                pl.BlockSpec((SMALL_ROWS, width), full),
                pl.BlockSpec((SMALL_ROWS, width), full),
            ]
            + [HBM_SPEC] * len(extras),
            out_specs=[
                pl.BlockSpec((bq, width), row),
                pl.BlockSpec((seq, width), full),
                pl.BlockSpec((seq, width), full),
                pl.BlockSpec((HEADS, width), full),
                pl.BlockSpec((HEADS, width), full),
                SMEM_SPEC,
            ],
            scratch_shapes=[
                pltpu.VMEM((HEADS * bq, width), bf16),
                pltpu.VMEM((HEADS * bq, width), bf16),
                pltpu.VMEM((seq, width), f32),
                pltpu.VMEM((seq, width), f32),
                pltpu.VMEM((HEADS * bq, width), f32),
                pltpu.VMEM((HEADS * bq, 128), f32),
            ],
        ),
        out_shape=[
            shape((count, width), bf16),
            shape((seq, width), bf16),
            shape((seq, width), bf16),
            shape((HEADS, width), f32),
            shape((HEADS, width), f32),
            TOKEN,
        ],
        compiler_params=pltpu.CompilerParams(vmem_limit_bytes=BIG_VMEM),
    )(place, q, datt, u, lse, k, v, *smalls, *extras)


def swap_section(x):
    return lax.ppermute(x, "section", [(0, 1), (1, 0)])


def xor_permute(x, axis, by):
    return lax.ppermute(x, axis, [(i, i ^ by) for i in range(lax.axis_size(axis))])


def from_xor_order(x, index):
    places = range(x.shape[0])
    return jnp.concatenate([lax.dynamic_index_in_dim(x, index ^ i, 0) for i in places])


def token_kernel(*refs):
    refs[-1][0] = 0


def token_after(*arrays):
    arrays = [x if x.ndim == 1 else x[(0,) * (x.ndim - 2)][:16, :128] for x in arrays]
    return pl.pallas_call(
        token_kernel,
        cost_estimate=SMALL_COST,
        in_specs=[SMEM_SPEC if x.ndim == 1 else VMEM_SPEC for x in arrays],
        out_specs=SMEM_SPEC,
        out_shape=TOKEN,
    )(*arrays)[0]


def half_columns(ref, which, size):
    return ref[:, pl.ds(pl.multiple_of(which * size, size), size)]


def split_blocks(blocks, kept, sent, mine):
    for i in range(kept.shape[0]):
        kept[i] = blocks[2 * i + mine]
        sent[i] = blocks[2 * i + 1 - mine]


def split_blocks_first(blocks, kept, sent, mine):
    for i in range(kept.shape[0]):
        at = 4 * (i // 2) + i % 2
        kept[i] = blocks[at + 2 * mine]
        sent[i] = blocks[at + 2 * (1 - mine)]


def down_kernel(seat, active, active_other, dy, dy_other, kept, sent, token_ref, blocks):
    token_ref[0] = 0
    rows, size = blocks.shape[1:]
    right, right_other = (half_columns(x, seat[0], size) for x in (dy, dy_other))
    tile = dy.shape[1]
    for j in range(active.shape[1] // tile):
        cols = slice(j * tile, (j + 1) * tile)
        grad = dense_tn(active[:, cols], right) + dense_tn(active_other[:, cols], right_other)
        each = tile // rows
        blocks[j * each : (j + 1) * each] = grad.astype(bf16).reshape(each, rows, size)
    split_blocks(blocks, kept, sent, seat[1] % 2)


def up_kernel(seat, two, two_other, att, att_other, right, right_other, kept, sent, token_ref, blocks):
    token_ref[0] = 0
    rows, size = blocks.shape[1:]
    cut = size - att.shape[1] // 2
    tile = cut // 2
    for j in range(2):
        cols = slice(j * tile, (j + 1) * tile)
        grad = dense_tn(two[...], right[:, cols]) + dense_tn(two_other[...], right_other[:, cols])
        blocks[:, :, cols] = grad.astype(bf16).reshape(-1, rows, tile)
    grad = dense_tn(att[...], right[:, cut:]) + dense_tn(att_other[...], right_other[:, cut:])
    blocks[:, :, cut:] = grad.astype(bf16).reshape(-1, rows, size - cut)
    split_blocks_first(blocks, kept, sent, seat[1] // 2)


def halves_of(kernel, seat, arrays, count, rows, size, flops):
    shape = jax.ShapeDtypeStruct((count // 2, rows, size), bf16)
    return one_step(
        kernel,
        in_specs=[SMEM_SPEC] + [VMEM_SPEC] * len(arrays),
        out_specs=[VMEM_SPEC, VMEM_SPEC, SMEM_SPEC],
        out_shape=[shape, shape, TOKEN],
        scratch_shapes=[pltpu.VMEM((count, rows, size), bf16)],
        compiler_params=pltpu.CompilerParams(vmem_limit_bytes=SMALL_VMEM),
    )(seat, *arrays)


def second_kernel(seat, token_in, *refs, bits, passing, closing):
    count = len(bits)
    refs = refs[passing:]
    parts, refs = refs[2 * count : 2 * count + closing], refs[: 2 * count] + refs[2 * count + closing :]
    refs[4 * count][0] = token_in[0]
    if closing:
        refs[4 * count + 1][...] = functools.reduce(jnp.add, [x[...].astype(f32) for x in parts])
    for i, bit in enumerate(bits):
        kept, got = refs[2 * i], refs[2 * i + 1]
        kept_out, sent_out = refs[2 * count + 2 * i], refs[2 * count + 2 * i + 1]
        mine = (seat[1] // bit) % 2
        for j in range(kept_out.shape[0]):
            for out, at in ((kept_out, 2 * j + mine), (sent_out, 2 * j + 1 - mine)):
                out[j] = (kept[at].astype(f32) + got[at].astype(f32)).astype(bf16)


def last_kernel(seat, token_in, *refs, count, rows, dp_count, passing):
    refs = refs[passing:]
    total, outs, token_ref = refs[2 * count], refs[2 * count + 1 : 2 * count + dp_count], refs[2 * count + dp_count]
    token_ref[0] = token_in[0]
    at = 0
    for i in range(count):
        kept, got = refs[2 * i], refs[2 * i + 1]
        size = kept.shape[2]
        for j in range(kept.shape[1] // rows):
            part = slice(j * rows, (j + 1) * rows)
            for by in range(len(outs) + 1):
                z = seat[2] ^ by
                value = kept[z, part, :].astype(f32) + got[z, part, :].astype(f32)
                if by == 0:
                    total[:, at : at + size] = value
                else:
                    outs[by - 1][:, at : at + size] = value.astype(bf16)
            at += size


def halved_kernel(seat, token_in, *refs, count, rows, passing):
    refs = refs[passing:]
    kept_out, sent_out, token_ref = refs[2 * count : 2 * count + 3]
    token_ref[0] = token_in[0]
    mine = seat[2] % 2
    at = 0
    for i in range(count):
        kept, got = refs[2 * i], refs[2 * i + 1]
        size = kept.shape[2]
        for j in range(kept.shape[1] // rows):
            part = slice(j * rows, (j + 1) * rows)
            for b in range(2):
                for out, z in ((kept_out, 2 * b + mine), (sent_out, 2 * b + 1 - mine)):
                    value = kept[z, part, :].astype(f32) + got[z, part, :].astype(f32)
                    out[b, :, at : at + size] = value.astype(bf16)
            at += size


def middle_kernel(seat, token_in, *refs, passing):
    kept, got, total, sent, token_ref = refs[passing : passing + 5]
    token_ref[0] = token_in[0]
    mine = seat[2] // 2
    total[...] = kept[mine].astype(f32) + got[mine].astype(f32)
    sent[...] = (kept[1 - mine].astype(f32) + got[1 - mine].astype(f32)).astype(bf16)


class Halved:
    def __init__(self, kept, sent):
        self.kept, self.got = kept, xor_permute(sent, "dp", 1)


def halved_step(seat, token, sums, rows, passing):
    specs_in, specs_out, shapes, aliases = handed_on(passing, 2, 3)
    size = sum(x.kept.shape[1] // rows * x.kept.shape[2] for x in sums)
    shape = jax.ShapeDtypeStruct((2, rows, size), bf16)
    kept, sent, token, *passing = one_step(
        functools.partial(halved_kernel, count=len(sums), rows=rows, passing=len(passing)),
        in_specs=[SMEM_SPEC] * 2 + specs_in + [VMEM_SPEC] * (2 * len(sums)),
        out_specs=[VMEM_SPEC] * 2 + [SMEM_SPEC] + specs_out,
        out_shape=[shape, shape, TOKEN] + shapes,
        input_output_aliases=aliases,
        compiler_params=pltpu.CompilerParams(vmem_limit_bytes=SMALL_VMEM),
    )(seat, token, *passing, *[y for x in sums for y in (x.kept, x.got)])
    return Halved(kept, sent), token, tuple(passing)


def middle_step(seat, token, halved, passing):
    specs_in, specs_out, shapes, aliases = handed_on(passing, 2, 3)
    shape = jax.ShapeDtypeStruct
    total, sent, token, *passing = one_step(
        functools.partial(middle_kernel, passing=len(passing)),
        in_specs=[SMEM_SPEC] * 2 + specs_in + [VMEM_SPEC] * 2,
        out_specs=[VMEM_SPEC] * 2 + [SMEM_SPEC] + specs_out,
        out_shape=[shape(halved.kept.shape[1:], f32), shape(halved.kept.shape[1:], bf16), TOKEN] + shapes,
        input_output_aliases=aliases,
        compiler_params=pltpu.CompilerParams(vmem_limit_bytes=SMALL_VMEM),
    )(seat, token, *passing, halved.kept, halved.got)
    halved.parts = (total, xor_permute(sent, "dp", 2))
    return token, tuple(passing)


class FastSum:
    def __init__(self, kept, sent, bits, token=None):
        self.kept, self.bits, self.token = kept, bits, token
        self.got = xor_permute(sent, "ctx", bits[0])

    def start(self):
        self.got = xor_permute(self.sent, "ctx", self.bits[1])


def handed_on(passing, before, after):
    specs = [ANY_SPEC] * len(passing)
    shapes = [jax.ShapeDtypeStruct(x.shape, x.dtype) for x in passing]
    return specs, specs, shapes, {before + i: after + i for i in range(len(passing))}


def hand_on_kernel(token_in, *refs, meanwhile, passing):
    refs[meanwhile + passing][0] = token_in[0]


def hand_on(token, meanwhile, passing):
    specs_in, specs_out, shapes, aliases = handed_on(passing, 1 + len(meanwhile), 1)
    outs = one_step(
        functools.partial(hand_on_kernel, meanwhile=len(meanwhile), passing=len(passing)),
        in_specs=[SMEM_SPEC] + [VMEM_SPEC] * len(meanwhile) + specs_in,
        out_specs=[SMEM_SPEC] + specs_out,
        out_shape=[TOKEN] + shapes,
        input_output_aliases=aliases,
    )(token, *meanwhile, *passing)
    return outs[0], outs[1:]


def second_step(seat, token, sums, passing, closing):
    closed = [jax.ShapeDtypeStruct(x.shape, f32) for x in closing[:1]]
    specs_in, specs_out, shapes, aliases = handed_on(passing, 2, 2 * len(sums) + 1 + len(closed))
    shape = lambda x: jax.ShapeDtypeStruct((x.shape[0] // 2,) + x.shape[1:], bf16)
    outs = one_step(
        functools.partial(second_kernel, bits=[x.bits[1] for x in sums], passing=len(passing), closing=len(closing)),
        in_specs=[SMEM_SPEC] * 2 + specs_in + [VMEM_SPEC] * (2 * len(sums) + len(closing)),
        out_specs=[VMEM_SPEC] * (2 * len(sums)) + [SMEM_SPEC] + [VMEM_SPEC] * len(closed) + specs_out,
        out_shape=[shape(x.kept) for x in sums for _ in range(2)] + [TOKEN] + closed + shapes,
        input_output_aliases=aliases,
        compiler_params=pltpu.CompilerParams(vmem_limit_bytes=SMALL_VMEM),
    )(seat, token, *passing, *[y for x in sums for y in (x.kept, x.got)], *closing)
    for i, x in enumerate(sums):
        x.kept, x.sent = outs[2 * i], outs[2 * i + 1]
    outs = outs[2 * len(sums) :]
    return outs[0], outs[1 + len(closed) :], outs[1] if closed else None


def last_step(seat, token, sums, rows, passing):
    dp_count = sums[0].kept.shape[0]
    specs_in, specs_out, shapes, aliases = handed_on(passing, 2, dp_count + 1)
    size = sum(x.kept.shape[1] // rows * x.kept.shape[2] for x in sums)
    shape = jax.ShapeDtypeStruct((rows, size), bf16)
    outs = one_step(
        functools.partial(last_kernel, count=len(sums), rows=rows, dp_count=dp_count, passing=len(passing)),
        in_specs=[SMEM_SPEC] * 2 + specs_in + [VMEM_SPEC] * (2 * len(sums)),
        out_specs=[VMEM_SPEC] * dp_count + [SMEM_SPEC] + specs_out,
        out_shape=[jax.ShapeDtypeStruct((rows, size), f32)] + [shape] * (dp_count - 1) + [TOKEN] + shapes,
        input_output_aliases=aliases,
        compiler_params=pltpu.CompilerParams(vmem_limit_bytes=SMALL_VMEM),
    )(seat, token, *passing, *[y for x in sums for y in (x.kept, x.got)])
    gots = [xor_permute(x, "dp", by) for by, x in enumerate(outs[1:dp_count], 1)]
    return outs[0], gots, outs[dp_count], outs[dp_count + 1 :]


def final_parts_kernel(seat, *refs, counts):
    *refs, keep, send = refs
    sums, at = [], 0
    for count in counts:
        sums.append(functools.reduce(jnp.add, [x[...].astype(f32) for x in refs[at : at + count]]))
        at += count
    cut = sums[0].shape[1]
    for section in range(2):

        @pl.when(seat[0] == section)
        def _(section=section):
            for out, layer in ((keep, section), (send, 1 - section)):
                out[:, :cut] = sums[2 * layer]
                out[:, cut:] = sums[2 * layer + 1]


def final_parts(seat, groups):
    parts = [x for group in groups for x in group]
    rows = parts[0].shape[0]
    out = jax.ShapeDtypeStruct((rows, groups[0][0].shape[1] + groups[1][0].shape[1]), f32)
    return one_step(
        functools.partial(final_parts_kernel, counts=[len(x) for x in groups]),
        in_specs=[SMEM_SPEC] + [VMEM_SPEC] * len(parts),
        out_specs=[VMEM_SPEC] * 2,
        out_shape=[out, out],
        compiler_params=pltpu.CompilerParams(vmem_limit_bytes=SMALL_VMEM),
    )(seat, *parts)


def final_outs_kernel(seat, keep, got, joint, mixer, up, down):
    half, half_up, rows = mixer.shape[1] // 2, up.shape[1] // 2, mixer.shape[0]
    width = 2 * half
    for section in range(2):

        @pl.when(seat[0] == section)
        def _(section=section):
            for i, ref in enumerate((keep, got) if section == 0 else (got, keep)):
                times = down.shape[0] // rows
                for j in range(times):
                    down[j * rows : (j + 1) * rows, i * half : (i + 1) * half] = ref[:, j * half : (j + 1) * half]
                at = times * half
                up[:, i * half_up : (i + 1) * half_up] = ref[:, at : at + half_up]
                at += half_up
                mixer[:, i * half : (i + 1) * half] = ref[:, at : at + half]
                at += half
                joint[:, (1 + i) * width : (2 + i) * width] = ref[:, at : at + width]
                joint[:, i * half : (i + 1) * half] = ref[:, at + width : at + width + half]


def final_outs(seat, keep, got, width, ff):
    rows = keep.shape[0]
    shape = lambda *x: jax.ShapeDtypeStruct(x, f32)
    return one_step(
        final_outs_kernel,
        in_specs=[SMEM_SPEC] + [VMEM_SPEC] * 2,
        out_specs=[VMEM_SPEC] * 4,
        out_shape=[shape(rows, 3 * width), shape(rows, width), shape(rows, ff), shape(rows * (ff // width), width)],
        compiler_params=pltpu.CompilerParams(vmem_limit_bytes=SMALL_VMEM),
    )(seat, keep, got)


def mix_grads_kernel(small, pre, post):
    rows = lax.broadcasted_iota(jnp.int32, (HEADS, small.shape[1]), 0)
    cols = lax.broadcasted_iota(jnp.int32, (HEADS, small.shape[1]), 1)
    heads = jnp.where(cols // HEAD == rows, 1.0, 0.0).astype(f32)
    dot = lambda a, b: lax.dot_general(
        a, b, (((1,), (1,)), ((), ())), precision=lax.Precision.HIGHEST, preferred_element_type=f32
    )
    pre[...] = 0.125 * dot(heads, small[2 : 2 + HEADS, :])
    post[...] = dot(small[2 + HEADS : 2 + 2 * HEADS, :], heads)


def mix_grads(small):
    out = jax.ShapeDtypeStruct((HEADS, HEADS), f32)
    return one_step(mix_grads_kernel, in_specs=[VMEM_SPEC], out_specs=[VMEM_SPEC] * 2, out_shape=[out, out])(small)


def total_of(part, gots):
    for got in gots:
        part = part + got.astype(f32)
    return part


def join_kernel(
    seat, token_in, keep_ref, got_ref, normed_ref, own, own_other, dq, dq_other, joint_own, joint_got,
    small_own, small_got, dn_kept, dn_sent, dnq_ref, a_kept, a_sent, b_kept, b_sent, gain_grad_ref, token_ref,
    kv_w, q_w, dkv, dn, a_blocks, b_blocks, sems,
):
    token_ref[0] = token_in[0]
    width = dkv.shape[1]
    section, which = seat[0], seat[3]
    for i, ref in enumerate((joint_own, joint_got)):

        @pl.when(which == i)
        def _(ref=ref):
            cols = pl.ds(pl.multiple_of((1 + section) * width, width), width)
            pltpu.make_async_copy(ref.at[0, :, cols], kv_w, sems.at[0]).start()
            pltpu.make_async_copy(ref.at[0, :, pl.ds(0, width)], q_w, sems.at[1]).start()

    dkv[...] = (keep_ref[...].astype(f32) + got_ref[...].astype(f32)).astype(bf16)
    rows, size_a, size_b = a_blocks.shape[1], a_blocks.shape[2], b_blocks.shape[2]
    grad = dense_tn(normed_ref[...], dkv[:, :size_a])
    a_blocks[...] = grad.astype(bf16).reshape(-1, rows, size_a)
    grad = dense_tn(normed_ref[...], dkv[:, size_a:])
    b_blocks[:, :, : width - size_a] = grad.astype(bf16).reshape(-1, rows, width - size_a)
    half = width // 2
    grad = dense_tn(own[...], half_columns(dq, section, half)) + dense_tn(
        own_other[...], half_columns(dq_other, section, half)
    )
    b_blocks[:, :, width - size_a :] = grad.astype(bf16).reshape(-1, rows, half)
    split_blocks(a_blocks, a_kept, a_sent, seat[1] % 2)
    split_blocks_first(b_blocks, b_kept, b_sent, seat[1] // 2)
    for i in range(2):
        pltpu.make_async_copy(joint_own.at[0, :, pl.ds(0, width)], (kv_w, q_w)[i], sems.at[i]).wait()
    back = dense_nt(dkv[...], kv_w[...])
    dn[...] = back.astype(bf16)
    back_q = dense_nt(dq[...], q_w[...])
    dnq_ref[...] = back_q
    gain_grad = jnp.sum(back * normed_ref[...].astype(f32), axis=0, keepdims=True)
    gain_grad = gain_grad + jnp.sum(back_q * own[...].astype(f32), axis=0, keepdims=True)
    gain_grad_ref[...] = gain_grad / small_of(small_own, small_got, which)(GAIN_A, 1)
    blk = own.shape[0] // 2
    last = dn.shape[0] // blk - 1
    for i in range(dn_kept.shape[0] // blk):
        for out, side in ((dn_kept, section), (dn_sent, 1 - section)):
            core = (i // 2) * 2 + side
            at = core if i % 2 == 0 else last - core
            out[i * blk : (i + 1) * blk, :] = dn[pl.ds(pl.multiple_of(at * blk, blk), blk), :]


def join(seat, token, arrays, joints, smalls, count, rows):
    seq, width = arrays[0].shape
    own_count = arrays[3].shape[0]
    size_a = 2 * width // 3
    size_b = width - size_a + width // 2
    shape = jax.ShapeDtypeStruct
    a_shape, b_shape = (shape((count // 2, rows, size), bf16) for size in (size_a, size_b))
    half_rows = shape((seq // 2, width), bf16)
    return one_step(
        join_kernel,
        in_specs=[SMEM_SPEC] * 2 + [VMEM_SPEC] * 7 + [HBM_SPEC] * 2 + [VMEM_SPEC] * 2,
        out_specs=[VMEM_SPEC] * 8 + [SMEM_SPEC],
        out_shape=[half_rows, half_rows, shape((own_count, width), f32)]
        + [a_shape, a_shape, b_shape, b_shape, shape((1, width), f32), TOKEN],
        scratch_shapes=[
            pltpu.VMEM((width, width), bf16),
            pltpu.VMEM((width, width), bf16),
            pltpu.VMEM((seq, width), bf16),
            pltpu.VMEM((seq, width), bf16),
            pltpu.VMEM((count, rows, size_a), bf16),
            pltpu.VMEM((count, rows, size_b), bf16),
            pltpu.SemaphoreType.DMA((2,)),
        ],
        compiler_params=pltpu.CompilerParams(vmem_limit_bytes=SMALL_VMEM),
    )(seat, token, *arrays, *joints, *smalls)


class Summer:
    def __init__(self, blocks, backwards):
        self.dp_count, ctx_count = blocks[0].shape[:2]
        bits = [1 << i for i in range(ctx_count.bit_length() - 1)]
        self.left = bits[::-1]
        self.order = bits[::-1] if backwards else bits
        self.parts = [x.reshape((self.dp_count,) + (2,) * len(bits) + x.shape[2:]) for x in blocks]

    def send(self, token=0):
        bit, self.order = self.order[0], self.order[1:]
        self.axis = 1 + self.left.index(bit)
        self.left = [b for b in self.left if b != bit]
        self.mine = (lax.axis_index("ctx") // bit) % 2
        at = 1 - self.mine + token
        sent = [lax.dynamic_index_in_dim(x, at, self.axis, keepdims=False) for x in self.parts]
        sent = sent[0] if len(sent) == 1 else jnp.concatenate(sent, axis=-1)
        self.got = xor_permute(sent, "ctx", bit)
        return [sent]

    def add(self, token):
        at, parts = 0, []
        for x in self.parts:
            kept = lax.dynamic_index_in_dim(x, self.mine + token, self.axis, keepdims=False)
            got = self.got[..., at : at + x.shape[-1]]
            at += x.shape[-1]
            parts.append((kept.astype(f32) + got.astype(f32)).astype(bf16))
        self.parts = parts

    def rest(self, token):
        self.add(token)
        while self.order:
            self.send()
            self.add(0)


class LastSum:
    def __init__(self, summers, rows):
        pieces = []
        for x in [x for one in summers for x in one.parts]:
            pieces += [x[:, i : i + rows] for i in range(0, x.shape[1], rows)]
        self.part = jnp.concatenate(pieces, axis=-1)

    def send(self):
        dp = lax.axis_index("dp")
        sent = [
            lax.dynamic_index_in_dim(self.part, dp ^ by, 0, keepdims=False)
            for by in range(1, self.part.shape[0])
        ]
        self.got = [xor_permute(x, "dp", by) for by, x in enumerate(sent, 1)]
        return sent

    @property
    def total(self):
        return lax.dynamic_index_in_dim(self.part, lax.axis_index("dp"), 0, keepdims=False).astype(f32)


def all_sum(x, tokens):
    steps = [(axis, 1 << i) for axis in ("ctx", "dp") for i in range(lax.axis_size(axis).bit_length() - 1)]
    for i, (axis, bit) in enumerate(steps):
        got = xor_permute(x, axis, bit)
        x = x + tokens[min(i, len(tokens) - 1)].astype(f32) + got
    return x


def local(
    inputs, lengths, cotangent, first_gain, joint_weight, pre_mix, post_mix,
    mixer_weight, second_gain, up_weight, down_weight,
):
    s = lax.axis_index("section")
    ctx = lax.axis_index("ctx")
    n = lax.axis_size("ctx")
    dp_count = lax.axis_size("dp")
    chips = n // 2
    micro_count, row_count, local_len, width = inputs.shape
    ff = up_weight.shape[2]
    seq = local_len * n
    blk = local_len // 2
    m = ctx // chips
    xi = ctx % chips
    core = xi * 2 + s
    zero = jnp.zeros((), jnp.int32)
    inputs = inputs.reshape(micro_count, 2, blk, width)
    cotangent = cotangent.reshape(micro_count, 2, blk, width)
    pick = lambda arr, i: lax.dynamic_index_in_dim(arr, i, 0, keepdims=False)

    spread = lambda mix: jnp.dot(mix, jnp.repeat(jnp.eye(HEADS, dtype=f32), HEAD, axis=1), precision=lax.Precision.HIGHEST)
    lines = lambda x, size: jnp.pad(x, ((0, size - x.shape[0]), (0, 0)))
    gains = jnp.concatenate([first_gain, second_gain]).astype(f32)
    small_own = jnp.concatenate(
        [lines(gains, PRE), lines(0.125 * spread(pre_mix[0].T), POST - PRE), lines(spread(post_mix[0]), SMALL_ROWS - POST)]
    )
    smalls = (small_own, swap_section(small_own))
    joints, mixers, ups, downs = (
        (w, swap_section(w)) for w in (joint_weight, mixer_weight, up_weight, down_weight)
    )

    mine = pick(inputs, m)
    pieces = []
    for d in range(1, n):
        target = m ^ (1 if d >= chips else 0)
        pieces.append(xor_permute(pick(pick(inputs, target), s), "ctx", d))
    other_pieces = [swap_section(jnp.concatenate(pieces))]
    chip_of = [ctx ^ d for d in range(1, n)]
    blocks0 = [2 * ctx, 2 * ctx + 1] + [2 * c + s for c in chip_of] + [2 * c + 1 - s for c in chip_of]
    pieces0 = [mine.reshape(2 * blk, width)] + pieces + other_pieces

    length = pick(lengths.reshape(-1), m)
    low_start = core * blk
    high_start = (2 * n - 1 - core) * blk
    bk = min(256, seq)
    places = [
        jnp.stack([length, (s != layer).astype(jnp.int32), low_start, high_start, s]).astype(jnp.int32)
        for layer in range(2)
    ]

    def gather_row(x):
        got = [x] + [xor_permute(x, "ctx", d) for d in range(1, chips)]
        cores = [(xi ^ d) * 2 + side for side in (s, 1 - s) for d in range(chips)]
        return got + [swap_section(y) for y in got], [b for c in cores for b in (c, 2 * n - 1 - c)]

    def forward(layer, pieces, blocks, meanwhile):
        place = jnp.concatenate([places[layer], jnp.stack(blocks).astype(jnp.int32)])
        attended, q, normed_own, x_own, token, normed_all, k, v, u, lse = attend(
            place, pieces, 2 * blk, smalls, joints, bk
        )
        weights = [x for pair in (mixers, ups, downs) for x in pair]
        out, hidden, normed_two, upward, active, token = feed(
            places[layer][1:2], x_own, attended, smalls, weights, ff, meanwhile
        )
        rows = [(x, swap_section(x)) for x in (active, normed_two, attended, normed_own)]
        return out, (x_own, q, k, v, u, lse, hidden, upward, rows, normed_all)

    def half(x, which):
        return lax.dynamic_slice_in_dim(x, which * (x.shape[1] // 2), x.shape[1] // 2, 1)

    def product(left, right):
        return (dense_tn(left[0], right[0]) + dense_tn(left[1], right[1])).astype(bf16)

    def blocks_of(grad):
        return grad.reshape(dp_count, n, grad.shape[0] // (dp_count * n), grad.shape[1])

    shard = width // (dp_count * n)

    fast = n == 4 and dp_count == 4 and shard % 16 == 0
    count = dp_count * n
    seats = [jnp.stack([s, ctx, lax.axis_index("dp"), s != layer]).astype(jnp.int32) for layer in range(2)]

    class Slow:
        def first(left, right, backwards):
            one = Summer([blocks_of(product(a, b)) for a, b in zip(left, right)], backwards)
            one.token = token_after(*one.send()).reshape(1)
            return one

        def second(token, sums, passing=(), closing=()):
            for one in sums:
                one.add(token[0])
            return token, passing, total_of(closing[0], closing[1:]) if closing else None

        def last(token, sums, passing=()):
            for one in sums:
                one.rest(token[0])
            one = LastSum(sums, shard)
            one.send()
            one.parts = (one.total, *one.got)
            return one, token, passing

        halved = last

        def middle(token, one, passing=()):
            return token, passing

    class Fast:
        def first(left, right, backwards):
            flat = [x for pair in left for x in pair]
            if backwards:
                arrays, size, rows = flat + list(right), (ff + width) // 2, shard
            else:
                arrays, size, rows = flat + list(right), width // 2, ff // count
            flops = 4 * flat[0].shape[0] * rows * count * size
            kernel = up_kernel if backwards else down_kernel
            kept, sent, token = halves_of(kernel, seats[0], arrays, count, rows, size, flops)
            return FastSum(kept, sent, (2, 1) if backwards else (1, 2), token)

        def second(token, sums, passing=(), closing=()):
            return second_step(seats[0], token, sums, passing, closing)

        def last(token, sums, passing=()):
            part, gots, token, passing = last_step(seats[0], token, sums, shard, passing)
            one = types.SimpleNamespace(parts=(part, *gots))
            return one, token, passing

        def halved(token, sums, passing=()):
            return halved_step(seats[0], token, sums, shard, passing)

        def middle(token, one, passing=()):
            return middle_step(seats[0], token, one, passing)

    steps = Fast if fast else Slow

    def backward(layer, dy, kept, earlier):
        x_own, q, k, v, u, lse, hidden, upward, rows, normed_all = kept
        rows_active, rows_two, rows_attended, rows_normed = rows
        here = s == layer
        gain_a = jnp.where(here, smalls[0][GAIN_A], smalls[1][GAIN_A])
        dy_other = swap_section(dy)
        if fast:
            down_sum = steps.first([rows_active], (dy, dy_other), False)
        else:
            down_sum = steps.first([rows_active], [(half(dy, s), half(dy_other, s))], False)
        earlier[0]()
        weights = [x for pair in (mixers, ups, downs) for x in pair]
        keep, send, dhidden, datt, gain_b_grad, token = feed_back(
            jnp.stack([s != layer, s]).astype(jnp.int32), dy, upward, hidden, smalls, weights, (down_sum.token,)
        )
        token, (send,) = earlier[1](token, (send,))
        other = swap_section(send)
        if fast:
            up_sum = steps.first([rows_two, rows_attended], (keep, other), True)
        else:
            cut = ff // 2
            pairs = [(keep[:, :cut], other[:, :cut]), (keep[:, cut:], other[:, cut:])]
            up_sum = steps.first([rows_two, rows_attended], pairs, True)
        dq, dkv_keep, dkv_send, pre_rows, post_rows, token = attend_back(
            places[layer], q, datt, u, lse, k, v, smalls, bk, (token, up_sum.token)
        )
        token, (dkv_send, dq) = earlier[2](token, (down_sum, up_sum), (dkv_send, dq))
        got, dq_other = swap_section(dkv_send), swap_section(dq)
        if fast:
            dn_kept, dn_sent, dnq, a_kept, a_sent, b_kept, b_sent, gain_a_grad, token = join(
                seats[layer], token, (dkv_keep, got, normed_all, *rows_normed, dq, dq_other), joints, smalls, count, shard
            )
            kv_sum, q_sum = FastSum(a_kept, a_sent, (1, 2)), FastSum(b_kept, b_sent, (2, 1))
            dn_kept, dn_sent = (x.reshape(chips, 2, blk, width) for x in (dn_kept, dn_sent))
        else:
            joint_w = jnp.where(here, joints[0][0], joints[1][0])
            kv_w = lax.dynamic_slice_in_dim(joint_w, width * (1 + s), width, 1)
            dkv = (dkv_keep.astype(f32) + got.astype(f32)).astype(bf16)
            dn = dense_nt(dkv, kv_w)
            gain_a_grad = jnp.sum(dn * normed_all.astype(f32), axis=0)
            dn = dn.astype(bf16).reshape(2 * n, blk, width)
            dn = jnp.stack([dn[i if h == 0 else 2 * n - 1 - i] for i in range(n) for h in range(2)])
            dn = dn.reshape(chips, 2, 2, blk, width)
            dn_kept = lax.dynamic_index_in_dim(dn, s, 1, keepdims=False)
            dn_sent = lax.dynamic_index_in_dim(dn, 1 - s, 1, keepdims=False)
            dnq = dense_nt(dq, joint_w[:, :width])
            gain_a_grad = (gain_a_grad + jnp.sum(dnq * rows_normed[0].astype(f32), axis=0)) / gain_a
            kv_part = blocks_of(dense_tn(normed_all, dkv).astype(bf16))
            q_part = blocks_of(product(rows_normed, (half(dq, s), half(dq_other, s))))
            cut = 2 * width // 3
            kv_sum = Summer([kv_part[..., :cut]], False)
            q_sum = Summer([kv_part[..., cut:], q_part], True)
            kv_sum.send()
            q_sum.send()
        token, (dn_sent,) = earlier[3](token, (dn_sent,), (down_sum, up_sum))
        low = (dn_kept.astype(f32) + swap_section(dn_sent).astype(f32)).astype(bf16)
        gots = [xor_permute(pick(low, xi ^ d), "ctx", d) for d in range(1, chips)]
        sums = (down_sum, up_sum, kv_sum, q_sum)
        token = earlier[4](token, low, sums)
        scattered = pick(low, xi + token[0]).astype(f32)
        for x in gots:
            scattered = scattered + x.astype(f32)
        scaled = (scattered.reshape(2 * blk, width) + dnq) * gain_a
        values = x_own.astype(f32)
        inverse = rms_inverse(values)
        unit = values * inverse
        dfront = inverse * (scaled - unit * jnp.mean(scaled * unit, axis=-1, keepdims=True))
        small = jnp.concatenate([gain_a_grad.reshape(1, -1), gain_b_grad.reshape(1, -1), pre_rows, post_rows])
        return dhidden + dfront, sums, small, token

    low_chip = ctx < chips
    there = [(i, chips + i) for i in range(chips)] + [(n - 1 - i, i) for i in range(chips)]
    here = [(n - 1 - i, chips + i) for i in range(chips)] + [(i, i) for i in range(chips)]
    first = jnp.where(low_chip, s, 1 - s)
    halves = lax.dynamic_index_in_dim(cotangent, first, 1, keepdims=False)
    ones, twos = jnp.where(low_chip, halves[1], halves[0]), jnp.where(low_chip, halves[0], halves[1])
    one, two = lax.ppermute(ones, "ctx", there), lax.ppermute(twos, "ctx", here)
    dy1 = jnp.concatenate([jnp.where(m == 0, two, one), jnp.where(m == 0, one, two)])
    x1, kept0 = forward(0, pieces0, blocks0, (one, two))
    y, kept1 = forward(1, *gather_row(x1), ())

    def send_home(x):
        x = x.reshape(2, blk, width)
        one = lax.ppermute(jnp.where(m == 0, x[1], x[0]), "ctx", [(b, a) for a, b in there])
        two = lax.ppermute(jnp.where(m == 0, x[0], x[1]), "ctx", [(b, a) for a, b in here])
        return one, two

    def at_home(one, two):
        return jnp.where(low_chip, jnp.stack([two, one]), jnp.stack([one, two]))

    def start(sums):
        for one in sums:
            one.start() if fast else one.send()

    def no_step():
        return None

    state = {}

    def after_attention(token, sums, passing):
        token, passing, _ = steps.second(token, sums, passing)
        start(sums)
        return token, passing

    def after_join(token, passing, sums):
        state["big"], token, passing = steps.halved(token, sums, passing)
        return token, passing

    def after_low(token, low, sums):
        token = token_after(token, low).reshape(1)
        token, _, _ = steps.second(token, sums[2:])
        start(sums[2:])
        return token

    first_steps = (no_step, lambda token, passing: (token, passing), after_attention, after_join, after_low)
    dx1, (_, _, kv1, q1), small1, _ = backward(1, dy1, kept1, first_steps)
    dy0 = dx1.astype(bf16)
    y_sent = send_home(y)

    def after_feed(token, passing):
        state["joint1"], token, passing = steps.halved(token, [kv1, q1], (*passing, *y_sent))
        token, (passing, *state["y"]) = steps.middle(token, state["big"], passing)
        return token, (passing,)

    def after_attention(token, sums, passing):
        token, passing, state["big1"] = steps.second(token, sums, passing, state["big"].parts)
        start(sums)
        token, passing = steps.middle(token, state["joint1"], passing)
        return token, passing

    def after_join(token, passing, sums):
        state["big0"], token, passing = steps.halved(token, sums, passing)
        state["token"] = token
        return token, passing

    def after_low(token, low, sums):
        token = token_after(token, low).reshape(1)
        token, _, _ = steps.second(token, sums[2:])
        start(sums[2:])
        return steps.middle(token, state["big0"])[0]

    dx0, (down0, up0, kv0, q0), small0, token = backward(
        0, dy0, kept0, (no_step, after_feed, after_attention, after_join, after_low)
    )
    early = token
    dx0 = dx0.astype(bf16)
    dx_home = at_home(*send_home(dx0))
    y_home = at_home(*state["y"])
    token = token_after(dx0).reshape(1)

    small_got = swap_section(jnp.where(s == 0, small1, small0))
    small = jnp.where(s == 0, small0, small1) + small_got
    joint0, last_token, _ = steps.last(token, [kv0, q0])
    small = all_sum(small, (state["token"][0], early[0], token[0], last_token[0]))

    got = swap_section(jnp.where(s == 0, y_home, dx_home))
    held = jnp.where(s == 0, dx_home, y_home)
    is_first = jnp.where(low_chip, s, 1 - s) == 0
    ends = jnp.stack([jnp.where(is_first, held, got), jnp.where(is_first, got, held)], axis=1)
    ends = ends.reshape(1, micro_count, row_count, local_len, width)

    at = (lax.axis_index("dp") * n + ctx) * shard
    gain_a_out, gain_b_out = (lax.dynamic_slice_in_dim(small[i], at, shard, 0) for i in range(2))
    pre_out, post_out = mix_grads(small)
    half_d, half_ff, times = width // 2, ff // 2, ff // width
    if fast:
        groups = (state["big0"].parts, joint0.parts, (state["big1"],), state["joint1"].parts)
        keep, send = final_parts(seats[0], groups)
        joint_out, mixer_out, up_out, down_out = final_outs(seats[0], keep, swap_section(send), width, ff)
    else:
        big0, joint0, joint1 = (total_of(x.parts[0], x.parts[1:]) for x in (state["big0"], joint0, state["joint1"]))
        pairs = ((big0, state["big1"]), (joint0, joint1))
        outs = []
        for at_zero, at_one in pairs:
            other = swap_section(jnp.where(s == 0, at_one, at_zero))
            own = jnp.where(s == 0, at_zero, at_one)
            outs.append((jnp.where(s == 0, own, other), jnp.where(s == 0, other, own)))
        (big_a, big_b), (joint_a, joint_b) = outs
        side = lambda *cuts: jnp.concatenate([x[:, at : at + size] for x, at, size in cuts], axis=1)
        down_out = jnp.concatenate(
            [side((big_a, i * half_d, half_d), (big_b, i * half_d, half_d)) for i in range(times)]
        )
        at = times * half_d
        up_out = side((big_a, at, half_ff), (big_b, at, half_ff))
        mixer_out = side((big_a, at + half_ff, half_d), (big_b, at + half_ff, half_d))
        joint_out = side((joint_a, width, half_d), (joint_b, width, half_d), (joint_a, 0, width), (joint_b, 0, width))
    return (
        ends,
        gain_a_out[None],
        joint_out[None],
        pre_out[None],
        post_out[None],
        mixer_out[None],
        gain_b_out[None],
        up_out[None],
        down_out[None],
    )


def solution(mesh):
    in_specs = (
        P(None, "dp", "ctx", None),
        P(None, "dp"),
        P(None, "dp", "ctx", None),
        P("section", None),
        P("section", None, None),
        P("section", None, None),
        P("section", None, None),
        P("section", None, None),
        P("section", None),
        P("section", None, None),
        P("section", None, None),
    )
    out_specs = (
        P("section", None, "dp", "ctx", None),
        P("section", ("dp", "ctx")),
        P("section", ("dp", "ctx"), None),
        P("section", None, None),
        P("section", None, None),
        P("section", ("dp", "ctx"), None),
        P("section", ("dp", "ctx")),
        P("section", ("dp", "ctx"), None),
        P("section", ("dp", "ctx"), None),
    )
    return jax.shard_map(local, mesh=mesh, in_specs=in_specs, out_specs=out_specs, check_vma=False)
```

```python
import functools
import math
import types

import jax
import jax.numpy as jnp
from jax import lax
from jax.experimental import pallas as pl
from jax.experimental.pallas import tpu as pltpu
from jax.sharding import PartitionSpec as P

HEADS = 12
HEAD = 64
eps = 1e-06
MASKED = -1e30
f32 = jnp.float32
bf16 = jnp.bfloat16
MIB = 1024 * 1024
SMALL_VMEM = 36 * MIB
BIG_VMEM = 60 * MIB


def dense(left_side, right_side):
    return jnp.dot(left_side, right_side, preferred_element_type=f32)


def dense_tn(left_side, right_side):
    return lax.dot_general(
        left_side, right_side, (((0,), (0,)), ((), ())), preferred_element_type=f32
    )


def dense_nt(left_side, right_side):
    return lax.dot_general(
        left_side, right_side, (((1,), (1,)), ((), ())), preferred_element_type=f32
    )


GAIN_A, GAIN_B, PRE, POST = 0, 1, 8, 24
SECTION, CTX, DP, LENGTH, STARTS, WHICH, BLOCKS = 0, 1, 2, 3, 4, 6, 8
SMALL_ROWS = 40


def small_of(own, got, which):
    return lambda at, size: jnp.where(which == 0, own[at : at + size, :], got[at : at + size, :])


def rms_inverse(values):
    return lax.rsqrt(jnp.mean(values * values, axis=-1, keepdims=True) + eps)


def lane_parts(x):
    return [x[:, i : i + 128] for i in range(0, x.shape[1], 128)]


def bias_of(q_start, k_start, length, bq, bk):
    rows = q_start + lax.broadcasted_iota(jnp.int32, (bq, bk), 0)
    cols = k_start + lax.broadcasted_iota(jnp.int32, (bq, bk), 1)
    return jnp.where((cols <= rows) & (cols < length), 0.0, MASKED).astype(f32)


def attend_kernel(info, small_own, small_got, joint_own, joint_got, *rest, bk, count_in, layer):
    (
        att_ref, q_ref, own_ref, x_ref, token_ref, normed_hbm, k_hbm, v_hbm, u_hbm, lse_hbm,
        joint, raw, normed, k, v, u, lse, qp, logit, total, top, norm, sems,
    ) = rest[count_in:]
    token_ref[0] = 0
    length, which = info[LENGTH], info[WHICH + layer]
    fetch((joint_own, joint_got), which, joint, sems.at[0])
    seq, width = normed.shape
    count = att_ref.shape[0]
    bq = count // 2
    small = small_of(small_own, small_got, which)
    gain, pre, post = small(GAIN_A, 1), small(PRE, HEADS), small(POST, HEADS)
    at = BLOCKS + layer * (seq // bq)
    for piece in rest[:count_in]:
        for j in range(piece.shape[0] // bq):
            x = piece[j * bq : (j + 1) * bq, :]
            span = pl.ds(pl.multiple_of(info[at] * bq, bq), bq)
            raw[span, :] = x
            x = x.astype(f32)
            normed[span, :] = (x * rms_inverse(x) * gain).astype(bf16)
            at += 1
    for i in range(2):
        span = pl.ds(pl.multiple_of(info[STARTS + i], bq), bq)
        own_ref[i * bq : (i + 1) * bq, :] = normed[span, :]
        x_ref[i * bq : (i + 1) * bq, :] = raw[span, :]
    fetched((joint_own, joint_got), joint, sems.at[0])
    cut = width // 3
    for i in range(3):
        cols = slice(width + i * cut, width + (i + 1) * cut)
        k[:, i * cut : (i + 1) * cut] = dense(normed[...], joint[:, cols]).astype(bf16)
    for i in range(3):
        cols = slice(2 * width + i * cut, 2 * width + (i + 1) * cut)
        v[:, i * cut : (i + 1) * cut] = dense(normed[...], joint[:, cols]).astype(bf16)
    q_ref[...] = dense(own_ref[...], joint[:, :width]).astype(bf16)
    outs = [
        pltpu.make_async_copy(a, b, sems.at[1 + i])
        for i, (a, b) in enumerate(((normed, normed_hbm), (k, k_hbm), (v, v_hbm)))
    ]
    for out in outs:
        out.start()

    def rows_step(step, carry):
        q_start = info[STARTS + step]
        mine = pl.ds(pl.multiple_of(step * bq, bq), bq)
        q32 = q_ref[mine, :].astype(f32)
        for h in range(HEADS):
            qp[h * bq : (h + 1) * bq, :] = (q32 * pre[h : h + 1, :]).astype(bf16)
        blocks = (jnp.minimum(q_start + bq, length) + bk - 1) // bk
        top[...] = jnp.full_like(top, MASKED)
        total[...] = jnp.zeros_like(total)
        norm[...] = jnp.zeros_like(norm)

        def score(kb, c):
            bias = bias_of(q_start, kb * bk, length, bq, bk)
            tile = dense_nt(qp[...], k[pl.ds(pl.multiple_of(kb * bk, bk), bk), :])
            tile = (tile.reshape(HEADS, bq, bk) + bias[None]).reshape(HEADS * bq, bk)
            logit[kb] = tile
            top[...] = functools.reduce(jnp.maximum, lane_parts(tile), top[...])
            return c

        lax.fori_loop(0, blocks, score, 0)
        highest = jnp.max(top[...], axis=-1, keepdims=True)
        top[...] = jnp.broadcast_to(highest, top.shape)

        def apply(kb, c):
            high = top[...]
            parts = [jnp.exp(x - high) for x in lane_parts(logit[kb])]
            norm[...] = functools.reduce(jnp.add, parts, norm[...])
            e = jnp.concatenate([x.astype(bf16) for x in parts], axis=1)
            total[...] += dense(e, v[pl.ds(pl.multiple_of(kb * bk, bk), bk), :])
            return c

        lax.fori_loop(0, blocks, apply, 0)
        sums = jnp.sum(norm[...], axis=-1, keepdims=True)
        scale = 1.0 / sums
        rows = pl.ds(pl.multiple_of(step * HEADS * bq, HEADS * bq), HEADS * bq)
        lse[rows, :] = jnp.broadcast_to(highest + jnp.log(sums), top.shape)
        att = jnp.zeros((bq, width), f32)
        for g in range(HEADS):
            part = total[g * bq : (g + 1) * bq, :] * scale[g * bq : (g + 1) * bq]
            u[pl.ds(pl.multiple_of(step * HEADS * bq + g * bq, bq), bq), :] = part.astype(bf16)
            att = att + part * post[g : g + 1, :]
        att_ref[mine, :] = att.astype(bf16)
        return carry

    lax.fori_loop(0, 2, rows_step, 0)
    outs += [pltpu.make_async_copy(u, u_hbm, sems.at[4]), pltpu.make_async_copy(lse, lse_hbm, sems.at[5])]
    for out in outs[3:]:
        out.start()
    for out in outs:
        out.wait()


VMEM_SPEC = pl.BlockSpec(memory_space=pltpu.VMEM)
FAR_SPEC = pl.BlockSpec(memory_space=pltpu.VMEM)
ANY_SPEC = pl.BlockSpec(memory_space=pl.ANY)
HBM_SPEC = pl.BlockSpec(memory_space=pltpu.HBM)
SMEM_SPEC = pl.BlockSpec(memory_space=pltpu.SMEM)
TOKEN = jax.ShapeDtypeStruct((1,), jnp.int32)

LARGE = 64 * 1024
SMALL_COST = pl.CostEstimate(flops=0, bytes_accessed=0, transcendentals=0)


def in_hbm(spec, x):
    return (spec is FAR_SPEC or spec is HBM_SPEC) and math.prod(x.shape) >= LARGE


def from_hbm(spec, x):
    return pltpu.with_memory_space_constraint(x, pltpu.HBM) if in_hbm(spec, x) else x


def result_in_hbm(spec, x):
    return pltpu.HBM(x.shape, x.dtype) if in_hbm(spec, x) else x


def one_step(kernel, *, in_specs, out_specs, out_shape, **rest):
    def whole(spec, x):
        if spec is not VMEM_SPEC and spec is not FAR_SPEC:
            return spec
        zeros = (0,) * len(x.shape)
        return pl.BlockSpec(x.shape, lambda i: zeros, pipeline_mode=pl.Buffered(1))

    def run(*args):
        return pl.pallas_call(
            kernel,
            cost_estimate=SMALL_COST,
            grid=(1,),
            in_specs=[whole(*x) for x in zip(in_specs, args, strict=True)],
            out_specs=[whole(*x) for x in zip(out_specs, out_shape, strict=True)],
            out_shape=[result_in_hbm(*x) for x in zip(out_specs, out_shape)],
            **rest,
        )(*[from_hbm(*x) for x in zip(in_specs, args)])

    return run


def attend(info, layer, pieces, count, smalls, joints, bk):
    width = pieces[0].shape[1]
    seq = sum(x.shape[0] for x in pieces)
    bq = count // 2
    shape = jax.ShapeDtypeStruct
    return one_step(
        functools.partial(attend_kernel, bk=bk, count_in=len(pieces), layer=layer),
        in_specs=[SMEM_SPEC] + [VMEM_SPEC] * 2 + [HBM_SPEC] * 2 + [VMEM_SPEC] * len(pieces),
        out_specs=[VMEM_SPEC, FAR_SPEC, FAR_SPEC, VMEM_SPEC, SMEM_SPEC] + [HBM_SPEC] * 5,
        out_shape=[shape((count, width), bf16)] * 4
        + [TOKEN]
        + [shape((seq, width), bf16)] * 3
        + [shape((HEADS * count, width), bf16), shape((HEADS * count, 128), f32)],
        scratch_shapes=[
            pltpu.VMEM((width, 3 * width), bf16),
            pltpu.VMEM((seq, width), bf16),
            pltpu.VMEM((seq, width), bf16),
            pltpu.VMEM((seq, width), bf16),
            pltpu.VMEM((seq, width), bf16),
            pltpu.VMEM((HEADS * count, width), bf16),
            pltpu.VMEM((HEADS * count, 128), f32),
            pltpu.VMEM((HEADS * bq, width), bf16),
            pltpu.VMEM((seq // bk, HEADS * bq, bk), f32),
            pltpu.VMEM((HEADS * bq, width), f32),
            pltpu.VMEM((HEADS * bq, 128), f32),
            pltpu.VMEM((HEADS * bq, 128), f32),
            pltpu.SemaphoreType.DMA((6,)),
        ],
        compiler_params=pltpu.CompilerParams(vmem_limit_bytes=BIG_VMEM),
    )(info, *smalls, *joints, *pieces)


def feed_kernel(
    info, x_ref, att_ref, small_own, small_got,
    mixer_own, mixer_got, up_own, up_got, down_own, down_got, *rest, tile, extra, layer,
):
    (
        out_ref, hidden_ref, two_ref, upward_hbm, active_hbm, token_ref,
        mixer, up, down, upward, active, sems,
    ) = rest[extra:]
    token_ref[0] = 0
    which = info[WHICH + layer]
    pairs = ((mixer_own, mixer_got), (up_own, up_got), (down_own, down_got))
    buffers = (mixer, up, down)
    for i in range(3):
        fetch(pairs[i], which, buffers[i], sems.at[i])
    gain = small_of(small_own, small_got, which)(GAIN_B, 1)
    fetched(pairs[0], mixer, sems.at[0])
    hidden = x_ref[...].astype(f32) + dense(att_ref[...], mixer[...])
    hidden_ref[...] = hidden
    two = (hidden * rms_inverse(hidden) * gain).astype(bf16)
    two_ref[...] = two
    fetched(pairs[1], up, sems.at[1])
    result, outs = hidden, []
    for j in range(down.shape[0] // tile):
        span = slice(j * tile, (j + 1) * tile)
        u = dense(two, up[:, span])
        upward[:, span] = u
        act = (0.5 * u * (1.0 + jnp.tanh(0.7978845608 * (u + 0.044715 * (u * u * u))))).astype(bf16)
        active[:, span] = act
        if j == 0:
            fetched(pairs[2], down, sems.at[2])
        result = result + dense(act, down[span, :])
    outs = [pltpu.make_async_copy(upward, upward_hbm, sems.at[3]), pltpu.make_async_copy(active, active_hbm, sems.at[4])]
    for out in outs:
        out.start()
    out_ref[...] = result.astype(bf16)
    for out in outs:
        out.wait()


def feed(info, layer, x, attended, smalls, weights, ff, extras):
    count, width = x.shape
    shape = jax.ShapeDtypeStruct
    return one_step(
        functools.partial(feed_kernel, tile=width, extra=len(extras), layer=layer),
        in_specs=[SMEM_SPEC] + [VMEM_SPEC] * 4 + [HBM_SPEC] * (6 + len(extras)),
        out_specs=[VMEM_SPEC, FAR_SPEC, FAR_SPEC] + [HBM_SPEC] * 2 + [SMEM_SPEC],
        out_shape=[
            shape((count, width), bf16),
            shape((count, width), f32),
            shape((count, width), bf16),
            shape((count, ff), f32),
            shape((count, ff), bf16),
            TOKEN,
        ],
        scratch_shapes=[
            pltpu.VMEM((width, width), bf16),
            pltpu.VMEM((width, ff), bf16),
            pltpu.VMEM((ff, width), bf16),
            pltpu.VMEM((count, ff), f32),
            pltpu.VMEM((count, ff), bf16),
            pltpu.SemaphoreType.DMA((5,)),
        ],
        compiler_params=pltpu.CompilerParams(vmem_limit_bytes=SMALL_VMEM),
    )(info, x, attended, *smalls, *weights, *extras)


def fetch(pair, which, buffer, semaphore):
    for i, ref in enumerate(pair):

        @pl.when(which == i)
        def _(ref=ref):
            pltpu.make_async_copy(ref.at[0], buffer, semaphore).start()


def fetched(pair, buffer, semaphore):
    pltpu.make_async_copy(pair[0].at[0], buffer, semaphore).wait()


def gelu_slope(u):
    inner = 0.7978845608 * (u + 0.044715 * (u * u * u))
    t = jnp.tanh(inner)
    return 0.5 * (1.0 + t) + 0.5 * u * (1.0 - t * t) * (0.7978845608 + 0.1070322243 * (u * u))


def feed_back_kernel(
    info, dy_ref, upward_hbm, hidden_hbm, small_own, small_got,
    mixer_own, mixer_got, up_own, up_got, down_own, down_got, *rest, tile, extra, layer,
):
    (
        keep_ref, send_ref, dhidden_ref, datt_ref, gain_grad_ref, token_ref,
        mixer, up, down, upward_ref, hidden_ref, sems,
    ) = rest[extra:]
    token_ref[0] = 0
    which = info[WHICH + layer]
    width = dy_ref.shape[1]
    half_ff, half = down.shape[0] // 2, width // 2

    def put(value, number, at):
        for ref, equal in ((keep_ref, True), (send_ref, False)):

            @pl.when((info[SECTION] == number) == equal)
            def _(ref=ref):
                ref[:, at : at + value.shape[1]] = value

    pairs = ((down_own, down_got), (up_own, up_got), (mixer_own, mixer_got))
    for i, (pair, buffer) in enumerate(zip(pairs, (down, up, mixer))):
        fetch(pair, which, buffer, sems.at[i])
        if i == 0:
            upward_copy = pltpu.make_async_copy(upward_hbm, upward_ref, sems.at[3])
            hidden_copy = pltpu.make_async_copy(hidden_hbm, hidden_ref, sems.at[4])
            upward_copy.start()
            hidden_copy.start()
    gain = small_of(small_own, small_got, which)(GAIN_B, 1)
    dy = dy_ref[...]
    fetched(pairs[0], down, sems.at[0])
    grad = jnp.zeros(hidden_ref.shape, f32)
    for j in range(down.shape[0] // tile):
        span = slice(j * tile, (j + 1) * tile)
        dactive = dense_nt(dy, down[span, :])
        if j == 0:
            upward_copy.wait()
        dup = (dactive * gelu_slope(upward_ref[:, span])).astype(bf16)
        put(dup, j * tile // half_ff, j * tile % half_ff)
        if j == 0:
            fetched(pairs[1], up, sems.at[1])
        grad = grad + dense_nt(dup, up[:, span])
    hidden_copy.wait()
    hidden = hidden_ref[...]
    inverse = rms_inverse(hidden)
    unit = hidden * inverse
    gain_grad_ref[...] = jnp.sum(grad * unit, axis=0, keepdims=True)
    scaled = grad * gain
    dhidden = dy.astype(f32) + inverse * (scaled - unit * jnp.mean(scaled * unit, axis=-1, keepdims=True))
    dhidden_ref[...] = dhidden
    low = dhidden.astype(bf16)
    for i in range(2):
        put(low[:, i * half : (i + 1) * half], i, half_ff)
        put(dy[:, i * half : (i + 1) * half], i, half_ff + half)
    fetched(pairs[2], mixer, sems.at[2])
    datt_ref[...] = dense_nt(low, mixer[...]).astype(bf16)


def feed_back(info, layer, dy, upward, hidden, smalls, weights, extras):
    count, width = dy.shape
    ff = upward.shape[1]
    shape = jax.ShapeDtypeStruct
    return one_step(
        functools.partial(feed_back_kernel, tile=width, extra=len(extras), layer=layer),
        in_specs=[SMEM_SPEC, VMEM_SPEC, HBM_SPEC, HBM_SPEC, VMEM_SPEC, VMEM_SPEC] + [HBM_SPEC] * (6 + len(extras)),
        out_specs=[VMEM_SPEC, VMEM_SPEC, FAR_SPEC, VMEM_SPEC, VMEM_SPEC, SMEM_SPEC],
        out_shape=[
            shape((count, ff // 2 + width), bf16),
            shape((count, ff // 2 + width), bf16),
            shape((count, width), f32),
            shape((count, width), bf16),
            shape((1, width), f32),
            TOKEN,
        ],
        scratch_shapes=[
            pltpu.VMEM((width, width), bf16),
            pltpu.VMEM((width, ff), bf16),
            pltpu.VMEM((ff, width), bf16),
            pltpu.VMEM((count, ff), f32),
            pltpu.VMEM((count, width), f32),
            pltpu.SemaphoreType.DMA((5,)),
        ],
        compiler_params=pltpu.CompilerParams(vmem_limit_bytes=SMALL_VMEM),
    )(info, dy, upward, hidden, *smalls, *weights, *extras)


def attend_back_kernel(
    info, q_ref, datt_ref, u_ref, lse_ref, k_hbm, v_hbm, small_own, small_got, *rest, bq, bk, extra, layer
):
    (
        dq_ref, keep_ref, send_ref, pre_grad_ref, post_grad_ref, token_ref,
        qp, dp, dk, dv, w, delta, k_ref, v_ref, sems,
    ) = rest[extra:]
    token_ref[0] = 0
    step = pl.program_id(0)
    copies = [pltpu.make_async_copy(x, y, sems.at[i]) for i, (x, y) in enumerate(((k_hbm, k_ref), (v_hbm, v_ref)))]

    @pl.when(step == 0)
    def _():
        for copy in copies:
            copy.start()

    length, which, q_start = info[LENGTH], info[WHICH + layer], info[STARTS + step]
    small = small_of(small_own, small_got, which)
    pre, post = small(PRE, HEADS), small(POST, HEADS)

    @pl.when(step == 0)
    def _():
        dk[...] = jnp.zeros_like(dk)
        dv[...] = jnp.zeros_like(dv)
        pre_grad_ref[...] = jnp.zeros_like(pre_grad_ref)
        post_grad_ref[...] = jnp.zeros_like(post_grad_ref)

    q32 = q_ref[...].astype(f32)
    datt = datt_ref[...].astype(f32)
    for h in range(HEADS):
        part = slice(h * bq, (h + 1) * bq)
        qp[part, :] = (q32 * pre[h : h + 1, :]).astype(bf16)
        scaled = datt * post[h : h + 1, :]
        dp[part, :] = scaled.astype(bf16)
        u = u_ref[part, :].astype(f32)
        delta[part, :] = jnp.broadcast_to(jnp.sum(scaled * u, axis=-1, keepdims=True), (bq, 128))
        post_grad_ref[h : h + 1, :] += jnp.sum(datt * u, axis=0, keepdims=True)
    w[...] = jnp.zeros_like(w)
    blocks = (jnp.minimum(q_start + bq, length) + bk - 1) // bk

    @pl.when(step == 0)
    def _():
        for copy in copies:
            copy.wait()

    def block(kb, c):
        span = pl.ds(pl.multiple_of(kb * bk, bk), bk)
        bias = bias_of(q_start, kb * bk, length, bq, bk)
        k_blk, v_blk = k_ref[span, :], v_ref[span, :]
        logits = dense_nt(qp[...], k_blk)
        logits = (logits.reshape(HEADS, bq, bk) + bias[None]).reshape(HEADS * bq, bk)
        grad = dense_nt(dp[...], v_blk)
        lse, spread = lse_ref[...], delta[...]
        attention, dlog = [], []
        for x, g in zip(lane_parts(logits), lane_parts(grad)):
            a = jnp.exp(x - lse)
            attention.append(a.astype(bf16))
            dlog.append((a * (g - spread)).astype(bf16))
        attention, dlog = jnp.concatenate(attention, axis=1), jnp.concatenate(dlog, axis=1)
        dv[span, :] += dense_tn(attention, dp[...])
        dk[span, :] += dense_tn(dlog, qp[...])
        w[...] += dense(dlog, k_blk)
        return c

    lax.fori_loop(0, blocks, block, 0)
    dq = jnp.zeros_like(q32)
    for h in range(HEADS):
        part = w[h * bq : (h + 1) * bq, :]
        dq = dq + part * pre[h : h + 1, :]
        pre_grad_ref[h : h + 1, :] += jnp.sum(part * q32, axis=0, keepdims=True)
    dq_ref[...] = dq.astype(bf16)

    for section, (kept, sent) in enumerate(((dk, dv), (dv, dk))):

        @pl.when((step == pl.num_programs(0) - 1) & (info[SECTION] == section))
        def _(kept=kept, sent=sent):
            keep_ref[...] = kept[...].astype(bf16)
            send_ref[...] = sent[...].astype(bf16)


def attend_back(info, layer, q, datt, u, lse, k, v, smalls, bk, extras):
    count, width = q.shape
    seq = k.shape[0]
    bq = count // 2
    full = lambda i, place: (0, 0)
    row = lambda i, place: (i, 0)
    shape = jax.ShapeDtypeStruct
    return pl.pallas_call(
        cost_estimate=SMALL_COST,
        kernel=functools.partial(attend_back_kernel, bq=bq, bk=bk, extra=len(extras), layer=layer),
        grid_spec=pltpu.PrefetchScalarGridSpec(
            num_scalar_prefetch=1,
            grid=(2,),
            in_specs=[
                pl.BlockSpec((bq, width), row),
                pl.BlockSpec((bq, width), row),
                pl.BlockSpec((HEADS * bq, width), row),
                pl.BlockSpec((HEADS * bq, 128), row),
                HBM_SPEC,
                HBM_SPEC,
                pl.BlockSpec((SMALL_ROWS, width), full),
                pl.BlockSpec((SMALL_ROWS, width), full),
            ]
            + [HBM_SPEC] * len(extras),
            out_specs=[
                pl.BlockSpec((bq, width), row),
                pl.BlockSpec((seq, width), full),
                pl.BlockSpec((seq, width), full),
                pl.BlockSpec((HEADS, width), full),
                pl.BlockSpec((HEADS, width), full),
                SMEM_SPEC,
            ],
            scratch_shapes=[
                pltpu.VMEM((HEADS * bq, width), bf16),
                pltpu.VMEM((HEADS * bq, width), bf16),
                pltpu.VMEM((seq, width), f32),
                pltpu.VMEM((seq, width), f32),
                pltpu.VMEM((HEADS * bq, width), f32),
                pltpu.VMEM((HEADS * bq, 128), f32),
                pltpu.VMEM((seq, width), bf16),
                pltpu.VMEM((seq, width), bf16),
                pltpu.SemaphoreType.DMA((2,)),
            ],
        ),
        out_shape=[
            shape((count, width), bf16),
            shape((seq, width), bf16),
            shape((seq, width), bf16),
            shape((HEADS, width), f32),
            shape((HEADS, width), f32),
            TOKEN,
        ],
        compiler_params=pltpu.CompilerParams(vmem_limit_bytes=BIG_VMEM),
    )(info, q, datt, u, lse, k, v, *smalls, *extras)


def swap_section(x):
    return lax.ppermute(x, "section", [(0, 1), (1, 0)])


def xor_permute(x, axis, by):
    return lax.ppermute(x, axis, [(i, i ^ by) for i in range(lax.axis_size(axis))])


def from_xor_order(x, index):
    places = range(x.shape[0])
    return jnp.concatenate([lax.dynamic_index_in_dim(x, index ^ i, 0) for i in places])


def token_kernel(*refs):
    refs[-1][0] = 0


def token_after(*arrays):
    arrays = [x if x.ndim == 1 else x[(0,) * (x.ndim - 2)][:16, :128] for x in arrays]
    return pl.pallas_call(
        token_kernel,
        cost_estimate=SMALL_COST,
        in_specs=[SMEM_SPEC if x.ndim == 1 else VMEM_SPEC for x in arrays],
        out_specs=SMEM_SPEC,
        out_shape=TOKEN,
    )(*arrays)[0]


def half_columns(ref, which, size):
    return ref[:, pl.ds(pl.multiple_of(which * size, size), size)]


def split_blocks(blocks, kept, sent, mine):
    for i in range(kept.shape[0]):
        kept[i] = blocks[2 * i + mine]
        sent[i] = blocks[2 * i + 1 - mine]


def split_blocks_first(blocks, kept, sent, mine):
    for i in range(kept.shape[0]):
        at = 4 * (i // 2) + i % 2
        kept[i] = blocks[at + 2 * mine]
        sent[i] = blocks[at + 2 * (1 - mine)]


def products_kernel(
    seat, active, active_other, two, two_other, att, att_other, right, right_other,
    down_kept, down_sent, up_kept, up_sent, token_ref, down_blocks, up_blocks,
):
    token_ref[0] = 0
    width = att.shape[1]
    half, half_ff = width // 2, active.shape[1] // 2
    both = lambda left, left_other, cols: dense_tn(left, right[:, cols]) + dense_tn(left_other, right_other[:, cols])
    rows = down_blocks.shape[1]
    each = width // rows
    for j in range(active.shape[1] // width):
        cols = slice(j * width, (j + 1) * width)
        grad = both(active[:, cols], active_other[:, cols], slice(half_ff + half, half_ff + width))
        down_blocks[j * each : (j + 1) * each] = grad.astype(bf16).reshape(each, rows, half)
    split_blocks(down_blocks, down_kept, down_sent, seat[CTX] % 2)
    rows = up_blocks.shape[1]
    tile = half_ff // 2
    for j in range(2):
        cols = slice(j * tile, (j + 1) * tile)
        up_blocks[:, :, cols] = both(two[...], two_other[...], cols).astype(bf16).reshape(-1, rows, tile)
    cols = slice(half_ff, half_ff + half)
    up_blocks[:, :, cols] = both(att[...], att_other[...], cols).astype(bf16).reshape(-1, rows, half)
    split_blocks_first(up_blocks, up_kept, up_sent, seat[CTX] // 2)


def products(seat, arrays, count, rows):
    ff, width = arrays[0].shape[1], arrays[4].shape[1]
    down, up = (ff // count, width // 2), (rows, (ff + width) // 2)
    shape = lambda x: jax.ShapeDtypeStruct((count // 2, *x), bf16)
    outs = one_step(
        products_kernel,
        in_specs=[SMEM_SPEC] + [FAR_SPEC] * 6 + [VMEM_SPEC] * 2,
        out_specs=[FAR_SPEC] * 4 + [SMEM_SPEC],
        out_shape=[shape(down)] * 2 + [shape(up)] * 2 + [TOKEN],
        scratch_shapes=[pltpu.VMEM((count, *down), bf16), pltpu.VMEM((count, *up), bf16)],
        compiler_params=pltpu.CompilerParams(vmem_limit_bytes=SMALL_VMEM),
    )(seat, *arrays)
    return FastSum(*outs[:2], (1, 2)), FastSum(*outs[2:4], (2, 1)), outs[4]


def second_kernel(seat, token_in, *refs, bits, passing, closing, behind):
    count = len(bits)
    refs = refs[behind + passing :]
    parts, refs = refs[2 * count : 2 * count + closing], refs[: 2 * count] + refs[2 * count + closing :]
    refs[4 * count][0] = token_in[0]
    if closing:
        refs[4 * count + 1][...] = functools.reduce(jnp.add, [x[...].astype(f32) for x in parts])
    for i, bit in enumerate(bits):
        kept, got = refs[2 * i], refs[2 * i + 1]
        kept_out, sent_out = refs[2 * count + 2 * i], refs[2 * count + 2 * i + 1]
        mine = (seat[1] // bit) % 2
        for j in range(kept_out.shape[0]):
            for out, at in ((kept_out, 2 * j + mine), (sent_out, 2 * j + 1 - mine)):
                out[j] = (kept[at].astype(f32) + got[at].astype(f32)).astype(bf16)


def last_kernel(seat, token_in, *refs, count, rows, dp_count, passing):
    refs = refs[passing:]
    total, outs, token_ref = refs[2 * count], refs[2 * count + 1 : 2 * count + dp_count], refs[2 * count + dp_count]
    token_ref[0] = token_in[0]
    at = 0
    for i in range(count):
        kept, got = refs[2 * i], refs[2 * i + 1]
        size = kept.shape[2]
        for j in range(kept.shape[1] // rows):
            part = slice(j * rows, (j + 1) * rows)
            for by in range(len(outs) + 1):
                z = seat[2] ^ by
                value = kept[z, part, :].astype(f32) + got[z, part, :].astype(f32)
                if by == 0:
                    total[:, at : at + size] = value
                else:
                    outs[by - 1][:, at : at + size] = value.astype(bf16)
            at += size


def halved_kernel(seat, token_in, *refs, count, rows, passing, closing):
    refs = refs[passing:]
    parts, refs = refs[2 * count : 2 * count + closing], refs[: 2 * count] + refs[2 * count + closing :]
    kept_out, sent_out, token_ref = refs[2 * count : 2 * count + 3]
    if closing:
        refs[2 * count + 3][...] = functools.reduce(jnp.add, [x[...].astype(f32) for x in parts])
    token_ref[0] = token_in[0]
    mine = seat[2] % 2
    at = 0
    for i in range(count):
        kept, got = refs[2 * i], refs[2 * i + 1]
        size = kept.shape[2]
        for j in range(kept.shape[1] // rows):
            part = slice(j * rows, (j + 1) * rows)
            for b in range(2):
                for out, z in ((kept_out, 2 * b + mine), (sent_out, 2 * b + 1 - mine)):
                    value = kept[z, part, :].astype(f32) + got[z, part, :].astype(f32)
                    out[b, :, at : at + size] = value.astype(bf16)
            at += size


def middle_kernel(seat, token_in, *refs, passing):
    kept, got, total, sent, token_ref = refs[passing : passing + 5]
    token_ref[0] = token_in[0]
    mine = seat[2] // 2
    total[...] = kept[mine].astype(f32) + got[mine].astype(f32)
    sent[...] = (kept[1 - mine].astype(f32) + got[1 - mine].astype(f32)).astype(bf16)


class Halved:
    def __init__(self, kept, sent):
        self.kept, self.got = kept, xor_permute(sent, "dp", 1)


def halved_step(seat, token, sums, rows, passing, closing, spec):
    closed = [jax.ShapeDtypeStruct(x.shape, f32) for x in closing[:1]]
    specs_in, specs_out, shapes, aliases = handed_on(passing, 2, 3 + len(closed))
    size = sum(x.kept.shape[1] // rows * x.kept.shape[2] for x in sums)
    shape = jax.ShapeDtypeStruct((2, rows, size), bf16)
    kept, sent, token, *rest = one_step(
        functools.partial(halved_kernel, count=len(sums), rows=rows, passing=len(passing), closing=len(closing)),
        in_specs=[SMEM_SPEC] * 2 + specs_in + [spec] * (2 * len(sums) + len(closing)),
        out_specs=[spec, VMEM_SPEC, SMEM_SPEC] + [FAR_SPEC] * len(closed) + specs_out,
        out_shape=[shape, shape, TOKEN] + closed + shapes,
        input_output_aliases=aliases,
        compiler_params=pltpu.CompilerParams(vmem_limit_bytes=SMALL_VMEM),
    )(seat, token, *passing, *[y for x in sums for y in (x.kept, x.got)], *closing)
    return Halved(kept, sent), token, tuple(rest[len(closed) :]), rest[0] if closed else None


def middle_step(seat, token, halved, passing, spec):
    specs_in, specs_out, shapes, aliases = handed_on(passing, 2, 3)
    shape = jax.ShapeDtypeStruct
    total, sent, token, *passing = one_step(
        functools.partial(middle_kernel, passing=len(passing)),
        in_specs=[SMEM_SPEC] * 2 + specs_in + [spec] * 2,
        out_specs=[FAR_SPEC, VMEM_SPEC, SMEM_SPEC] + specs_out,
        out_shape=[shape(halved.kept.shape[1:], f32), shape(halved.kept.shape[1:], bf16), TOKEN] + shapes,
        input_output_aliases=aliases,
        compiler_params=pltpu.CompilerParams(vmem_limit_bytes=SMALL_VMEM),
    )(seat, token, *passing, halved.kept, halved.got)
    halved.parts = (total, xor_permute(sent, "dp", 2))
    return token, tuple(passing)


class FastSum:
    def __init__(self, kept, sent, bits):
        self.kept, self.bits = kept, bits
        self.got = xor_permute(sent, "ctx", bits[0])

    def start(self):
        self.got = xor_permute(self.sent, "ctx", self.bits[1])


def handed_on(passing, before, after):
    specs = [ANY_SPEC] * len(passing)
    shapes = [jax.ShapeDtypeStruct(x.shape, x.dtype) for x in passing]
    return specs, specs, shapes, {before + i: after + i for i in range(len(passing))}


def hand_on_kernel(token_in, *refs, meanwhile, passing):
    refs[meanwhile + passing][0] = token_in[0]


def hand_on(token, meanwhile, passing):
    specs_in, specs_out, shapes, aliases = handed_on(passing, 1 + len(meanwhile), 1)
    outs = one_step(
        functools.partial(hand_on_kernel, meanwhile=len(meanwhile), passing=len(passing)),
        in_specs=[SMEM_SPEC] + [VMEM_SPEC] * len(meanwhile) + specs_in,
        out_specs=[SMEM_SPEC] + specs_out,
        out_shape=[TOKEN] + shapes,
        input_output_aliases=aliases,
    )(token, *meanwhile, *passing)
    return outs[0], outs[1:]


def second_step(seat, token, sums, passing, closing, behind, spec):
    closed = [jax.ShapeDtypeStruct(x.shape, f32) for x in closing[:1]]
    specs_in, specs_out, shapes, aliases = handed_on(passing, 2 + len(behind), 2 * len(sums) + 1 + len(closed))
    shape = lambda x: jax.ShapeDtypeStruct((x.shape[0] // 2,) + x.shape[1:], bf16)
    outs = one_step(
        functools.partial(second_kernel, bits=[x.bits[1] for x in sums], passing=len(passing), closing=len(closing), behind=len(behind)),
        in_specs=[SMEM_SPEC] * 2 + [ANY_SPEC] * len(behind) + specs_in + [spec] * (2 * len(sums) + len(closing)),
        out_specs=[VMEM_SPEC] * (2 * len(sums)) + [SMEM_SPEC] + [FAR_SPEC] * len(closed) + specs_out,
        out_shape=[shape(x.kept) for x in sums for _ in range(2)] + [TOKEN] + closed + shapes,
        input_output_aliases=aliases,
        compiler_params=pltpu.CompilerParams(vmem_limit_bytes=SMALL_VMEM),
    )(seat, token, *behind, *passing, *[y for x in sums for y in (x.kept, x.got)], *closing)
    for i, x in enumerate(sums):
        x.kept, x.sent = outs[2 * i], outs[2 * i + 1]
    outs = outs[2 * len(sums) :]
    return outs[0], outs[1 + len(closed) :], outs[1] if closed else None


def last_step(seat, token, sums, rows, passing):
    dp_count = sums[0].kept.shape[0]
    specs_in, specs_out, shapes, aliases = handed_on(passing, 2, dp_count + 1)
    size = sum(x.kept.shape[1] // rows * x.kept.shape[2] for x in sums)
    shape = jax.ShapeDtypeStruct((rows, size), bf16)
    outs = one_step(
        functools.partial(last_kernel, count=len(sums), rows=rows, dp_count=dp_count, passing=len(passing)),
        in_specs=[SMEM_SPEC] * 2 + specs_in + [VMEM_SPEC] * (2 * len(sums)),
        out_specs=[VMEM_SPEC] * dp_count + [SMEM_SPEC] + specs_out,
        out_shape=[jax.ShapeDtypeStruct((rows, size), f32)] + [shape] * (dp_count - 1) + [TOKEN] + shapes,
        input_output_aliases=aliases,
        compiler_params=pltpu.CompilerParams(vmem_limit_bytes=SMALL_VMEM),
    )(seat, token, *passing, *[y for x in sums for y in (x.kept, x.got)])
    gots = [xor_permute(x, "dp", by) for by, x in enumerate(outs[1:dp_count], 1)]
    return outs[0], gots, outs[dp_count], outs[dp_count + 1 :]


def final_parts_kernel(seat, *refs, counts):
    *refs, keep, send = refs
    sums, at = [], 0
    for count in counts:
        sums.append(functools.reduce(jnp.add, [x[...].astype(f32) for x in refs[at : at + count]]))
        at += count
    cut = sums[0].shape[1]
    for section in range(2):

        @pl.when(seat[0] == section)
        def _(section=section):
            for out, layer in ((keep, section), (send, 1 - section)):
                out[:, :cut] = sums[2 * layer]
                out[:, cut:] = sums[2 * layer + 1]


def final_parts(seat, groups):
    parts = [x for group in groups for x in group]
    rows = parts[0].shape[0]
    out = jax.ShapeDtypeStruct((rows, groups[0][0].shape[1] + groups[1][0].shape[1]), f32)
    return one_step(
        functools.partial(final_parts_kernel, counts=[len(x) for x in groups]),
        in_specs=[SMEM_SPEC] + [VMEM_SPEC] * len(parts),
        out_specs=[VMEM_SPEC] * 2,
        out_shape=[out, out],
        compiler_params=pltpu.CompilerParams(vmem_limit_bytes=SMALL_VMEM),
    )(seat, *parts)


def final_outs_kernel(seat, keep, got, joint, mixer, up, down):
    half, half_up, rows = mixer.shape[1] // 2, up.shape[1] // 2, mixer.shape[0]
    width = 2 * half
    for section in range(2):

        @pl.when(seat[0] == section)
        def _(section=section):
            for i, ref in enumerate((keep, got) if section == 0 else (got, keep)):
                times = down.shape[0] // rows
                for j in range(times):
                    down[j * rows : (j + 1) * rows, i * half : (i + 1) * half] = ref[:, j * half : (j + 1) * half]
                at = times * half
                up[:, i * half_up : (i + 1) * half_up] = ref[:, at : at + half_up]
                at += half_up
                mixer[:, i * half : (i + 1) * half] = ref[:, at : at + half]
                at += half
                joint[:, (1 + i) * width : (2 + i) * width] = ref[:, at : at + width]
                joint[:, i * half : (i + 1) * half] = ref[:, at + width : at + width + half]


def final_outs(seat, keep, got, width, ff):
    rows = keep.shape[0]
    shape = lambda *x: jax.ShapeDtypeStruct(x, f32)
    return one_step(
        final_outs_kernel,
        in_specs=[SMEM_SPEC] + [VMEM_SPEC] * 2,
        out_specs=[VMEM_SPEC] * 4,
        out_shape=[shape(rows, 3 * width), shape(rows, width), shape(rows, ff), shape(rows * (ff // width), width)],
        compiler_params=pltpu.CompilerParams(vmem_limit_bytes=SMALL_VMEM),
    )(seat, keep, got)


def mix_grads_kernel(small, _, pre, post):
    rows = lax.broadcasted_iota(jnp.int32, (HEADS, small.shape[1]), 0)
    cols = lax.broadcasted_iota(jnp.int32, (HEADS, small.shape[1]), 1)
    heads = jnp.where(cols // HEAD == rows, 1.0, 0.0).astype(f32)
    dot = lambda a, b: lax.dot_general(
        a, b, (((1,), (1,)), ((), ())), precision=lax.Precision.HIGHEST, preferred_element_type=f32
    )
    pre[:, 0, :] = 0.125 * dot(heads, small[2 : 2 + HEADS, :])
    post[:, 0, :] = dot(small[2 + HEADS : 2 + 2 * HEADS, :], heads)


def mix_grads(small, behind):
    out = jax.ShapeDtypeStruct((HEADS, 1, HEADS), f32)
    return one_step(
        mix_grads_kernel, in_specs=[VMEM_SPEC, ANY_SPEC], out_specs=[VMEM_SPEC] * 2, out_shape=[out, out]
    )(small, behind)


def total_of(part, gots):
    for got in gots:
        part = part + got.astype(f32)
    return part


def join_kernel(
    seat, token_in, keep_ref, got_ref, normed_ref, own, own_other, dq, dq_other, joint_own, joint_got,
    small_own, small_got, dn_kept, dn_sent, dnq_ref, a_kept, a_sent, b_kept, b_sent, gain_grad_ref, token_ref,
    kv_w, q_w, dkv, dn, a_blocks, b_blocks, sems, *, layer,
):
    token_ref[0] = token_in[0]
    width = dkv.shape[1]
    section, which = seat[SECTION], seat[WHICH + layer]
    for i, ref in enumerate((joint_own, joint_got)):

        @pl.when(which == i)
        def _(ref=ref):
            cols = pl.ds(pl.multiple_of((1 + section) * width, width), width)
            pltpu.make_async_copy(ref.at[0, :, cols], kv_w, sems.at[0]).start()
            pltpu.make_async_copy(ref.at[0, :, pl.ds(0, width)], q_w, sems.at[1]).start()

    dkv[...] = (keep_ref[...].astype(f32) + got_ref[...].astype(f32)).astype(bf16)
    rows, size_a, size_b = a_blocks.shape[1], a_blocks.shape[2], b_blocks.shape[2]
    grad = dense_tn(normed_ref[...], dkv[:, :size_a])
    a_blocks[...] = grad.astype(bf16).reshape(-1, rows, size_a)
    grad = dense_tn(normed_ref[...], dkv[:, size_a:])
    b_blocks[:, :, : width - size_a] = grad.astype(bf16).reshape(-1, rows, width - size_a)
    half = width // 2
    grad = dense_tn(own[...], half_columns(dq, section, half)) + dense_tn(
        own_other[...], half_columns(dq_other, section, half)
    )
    b_blocks[:, :, width - size_a :] = grad.astype(bf16).reshape(-1, rows, half)
    split_blocks(a_blocks, a_kept, a_sent, seat[1] % 2)
    split_blocks_first(b_blocks, b_kept, b_sent, seat[1] // 2)
    for i in range(2):
        pltpu.make_async_copy(joint_own.at[0, :, pl.ds(0, width)], (kv_w, q_w)[i], sems.at[i]).wait()
    back = dense_nt(dkv[...], kv_w[...])
    dn[...] = back.astype(bf16)
    back_q = dense_nt(dq[...], q_w[...])
    dnq_ref[...] = back_q
    gain_grad = jnp.sum(back * normed_ref[...].astype(f32), axis=0, keepdims=True)
    gain_grad = gain_grad + jnp.sum(back_q * own[...].astype(f32), axis=0, keepdims=True)
    gain_grad_ref[...] = gain_grad / small_of(small_own, small_got, which)(GAIN_A, 1)
    blk = own.shape[0] // 2
    last = dn.shape[0] // blk - 1
    for i in range(dn_kept.shape[0] // blk):
        for out, side in ((dn_kept, section), (dn_sent, 1 - section)):
            core = (i // 2) * 2 + side
            at = core if i % 2 == 0 else last - core
            out[i * blk : (i + 1) * blk, :] = dn[pl.ds(pl.multiple_of(at * blk, blk), blk), :]


def join(seat, layer, token, arrays, joints, smalls, count, rows):
    seq, width = arrays[0].shape
    own_count = arrays[3].shape[0]
    size_a = 2 * width // 3
    size_b = width - size_a + width // 2
    shape = jax.ShapeDtypeStruct
    a_shape, b_shape = (shape((count // 2, rows, size), bf16) for size in (size_a, size_b))
    half_rows = shape((seq // 2, width), bf16)
    return one_step(
        functools.partial(join_kernel, layer=layer),
        in_specs=[SMEM_SPEC] * 2
        + [VMEM_SPEC] * 2
        + [FAR_SPEC] * 3
        + [VMEM_SPEC] * 2
        + [HBM_SPEC] * 2
        + [VMEM_SPEC] * 2,
        out_specs=[VMEM_SPEC] * 8 + [SMEM_SPEC],
        out_shape=[half_rows, half_rows, shape((own_count, width), f32)]
        + [a_shape, a_shape, b_shape, b_shape, shape((1, width), f32), TOKEN],
        scratch_shapes=[
            pltpu.VMEM((width, width), bf16),
            pltpu.VMEM((width, width), bf16),
            pltpu.VMEM((seq, width), bf16),
            pltpu.VMEM((seq, width), bf16),
            pltpu.VMEM((count, rows, size_a), bf16),
            pltpu.VMEM((count, rows, size_b), bf16),
            pltpu.SemaphoreType.DMA((2,)),
        ],
        compiler_params=pltpu.CompilerParams(vmem_limit_bytes=SMALL_VMEM),
    )(seat, token, *arrays, *joints, *smalls)


class Summer:
    def __init__(self, blocks, backwards):
        self.dp_count, ctx_count = blocks[0].shape[:2]
        bits = [1 << i for i in range(ctx_count.bit_length() - 1)]
        self.left = bits[::-1]
        self.order = bits[::-1] if backwards else bits
        self.parts = [x.reshape((self.dp_count,) + (2,) * len(bits) + x.shape[2:]) for x in blocks]

    def send(self, token=0):
        bit, self.order = self.order[0], self.order[1:]
        self.axis = 1 + self.left.index(bit)
        self.left = [b for b in self.left if b != bit]
        self.mine = (lax.axis_index("ctx") // bit) % 2
        at = 1 - self.mine + token
        sent = [lax.dynamic_index_in_dim(x, at, self.axis, keepdims=False) for x in self.parts]
        sent = sent[0] if len(sent) == 1 else jnp.concatenate(sent, axis=-1)
        self.got = xor_permute(sent, "ctx", bit)
        return [sent]

    def add(self, token):
        at, parts = 0, []
        for x in self.parts:
            kept = lax.dynamic_index_in_dim(x, self.mine + token, self.axis, keepdims=False)
            got = self.got[..., at : at + x.shape[-1]]
            at += x.shape[-1]
            parts.append((kept.astype(f32) + got.astype(f32)).astype(bf16))
        self.parts = parts

    def rest(self, token):
        self.add(token)
        while self.order:
            self.send()
            self.add(0)


class LastSum:
    def __init__(self, summers, rows):
        pieces = []
        for x in [x for one in summers for x in one.parts]:
            pieces += [x[:, i : i + rows] for i in range(0, x.shape[1], rows)]
        self.part = jnp.concatenate(pieces, axis=-1)

    def send(self):
        dp = lax.axis_index("dp")
        sent = [
            lax.dynamic_index_in_dim(self.part, dp ^ by, 0, keepdims=False)
            for by in range(1, self.part.shape[0])
        ]
        self.got = [xor_permute(x, "dp", by) for by, x in enumerate(sent, 1)]
        return sent

    @property
    def total(self):
        return lax.dynamic_index_in_dim(self.part, lax.axis_index("dp"), 0, keepdims=False).astype(f32)


def all_sum(x, tokens):
    steps = [(axis, 1 << i) for axis in ("ctx", "dp") for i in range(lax.axis_size(axis).bit_length() - 1)]
    for i, (axis, bit) in enumerate(steps):
        got = xor_permute(x, axis, bit)
        x = x + tokens[min(i, len(tokens) - 1)].astype(f32) + got
    return x


def local(
    inputs, lengths, cotangent, first_gain, joint_weight, pre_mix, post_mix,
    mixer_weight, second_gain, up_weight, down_weight,
):
    s = lax.axis_index("section")
    ctx = lax.axis_index("ctx")
    n = lax.axis_size("ctx")
    dp_count = lax.axis_size("dp")
    chips = n // 2
    micro_count, row_count, local_len, width = inputs.shape
    ff = up_weight.shape[2]
    seq = local_len * n
    blk = local_len // 2
    m = ctx // chips
    xi = ctx % chips
    core = xi * 2 + s
    zero = jnp.zeros((), jnp.int32)
    inputs = inputs.reshape(micro_count, 2, blk, width)
    cotangent = cotangent.reshape(micro_count, 2, blk, width)
    pick = lambda arr, i: lax.dynamic_index_in_dim(arr, i, 0, keepdims=False)

    spread = lambda mix: jnp.dot(mix, jnp.repeat(jnp.eye(HEADS, dtype=f32), HEAD, axis=1), precision=lax.Precision.HIGHEST)
    lines = lambda x, size: jnp.pad(x, ((0, size - x.shape[0]), (0, 0)))
    gains = jnp.concatenate([first_gain, second_gain]).astype(f32)
    small_own = jnp.concatenate(
        [lines(gains, PRE), lines(0.125 * spread(pre_mix[0].T), POST - PRE), lines(spread(post_mix[0]), SMALL_ROWS - POST)]
    )
    smalls = (small_own, swap_section(small_own))
    joints, mixers, ups, downs = (
        (w, swap_section(w)) for w in (joint_weight, mixer_weight, up_weight, down_weight)
    )

    mine = pick(inputs, m)
    pieces = []
    for d in range(1, n):
        target = m ^ (1 if d >= chips else 0)
        pieces.append(xor_permute(pick(pick(inputs, target), s), "ctx", d))
    other_pieces = [swap_section(jnp.concatenate(pieces))]
    chip_of = [ctx ^ d for d in range(1, n)]
    blocks0 = [2 * ctx, 2 * ctx + 1] + [2 * c + s for c in chip_of] + [2 * c + 1 - s for c in chip_of]
    pieces0 = [mine.reshape(2 * blk, width)] + pieces + other_pieces

    length = pick(lengths.reshape(-1), m)
    low_start = core * blk
    high_start = (2 * n - 1 - core) * blk
    bk = min(256, seq)
    cores1 = [(xi ^ d) * 2 + side for side in (s, 1 - s) for d in range(chips)]
    blocks1 = [b for c in cores1 for b in (c, 2 * n - 1 - c)]
    info = [s, ctx, lax.axis_index("dp"), length, low_start, high_start, s != 0, s != 1, *blocks0, *blocks1]
    info = jnp.stack([jnp.asarray(x, jnp.int32) for x in info])

    def gather_row(x):
        got = [x] + [xor_permute(x, "ctx", d) for d in range(1, chips)]
        return got + [swap_section(y) for y in got]

    def forward(layer, pieces, meanwhile):
        attended, q, normed_own, x_own, token, normed_all, k, v, u, lse = attend(
            info, layer, pieces, 2 * blk, smalls, joints, bk
        )
        weights = [x for pair in (mixers, ups, downs) for x in pair]
        out, hidden, normed_two, upward, active, token = feed(
            info, layer, x_own, attended, smalls, weights, ff, meanwhile
        )
        rows = [(x, swap_section(x)) for x in (active, normed_two, attended, normed_own)]
        return out, (x_own, q, k, v, u, lse, hidden, upward, rows, normed_all)

    def half(x, which):
        return lax.dynamic_slice_in_dim(x, which * (x.shape[1] // 2), x.shape[1] // 2, 1)

    def product(left, right):
        return (dense_tn(left[0], right[0]) + dense_tn(left[1], right[1])).astype(bf16)

    def blocks_of(grad):
        return grad.reshape(dp_count, n, grad.shape[0] // (dp_count * n), grad.shape[1])

    shard = width // (dp_count * n)

    fast = n == 4 and dp_count == 4 and shard % 16 == 0
    count = dp_count * n

    class Slow:
        def first(rows, keep, other):
            active, two, att, _ = rows
            cut, end = ff // 2, (ff + width) // 2
            of = lambda *cols: (keep[:, slice(*cols)], other[:, slice(*cols)])
            down_sum = Summer([blocks_of(product(active, of(end, None)))], False)
            up_sum = Summer([blocks_of(product(two, of(0, cut))), blocks_of(product(att, of(cut, end)))], True)
            return down_sum, up_sum, token_after(*down_sum.send(), *up_sum.send()).reshape(1)

        def second(token, sums, passing=(), closing=(), behind=()):
            for one in sums:
                one.add(token[0])
            return token, passing, total_of(closing[0], closing[1:]) if closing else None

        def last(token, sums, passing=()):
            for one in sums:
                one.rest(token[0])
            one = LastSum(sums, shard)
            one.send()
            one.parts = (one.total, *one.got)
            return one, token, passing

        def halved(token, sums, passing=(), closing=()):
            return *Slow.last(token, sums, passing), total_of(closing[0], closing[1:]) if closing else None

        def middle(token, one, passing=()):
            return token, passing

    class Fast:
        def first(rows, keep, other):
            return products(info, (*rows[0], *rows[1], *rows[2], keep, other), count, shard)

        def second(token, sums, passing=(), closing=(), behind=()):
            return second_step(info, token, sums, passing, closing, behind, VMEM_SPEC if behind else FAR_SPEC)

        def last(token, sums, passing=()):
            part, gots, token, passing = last_step(info, token, sums, shard, passing)
            one = types.SimpleNamespace(parts=(part, *gots))
            return one, token, passing

        def halved(token, sums, passing=(), closing=()):
            return halved_step(info, token, sums, shard, passing, closing, VMEM_SPEC if closing else FAR_SPEC)

        def middle(token, one, passing=()):
            return middle_step(info, token, one, passing, FAR_SPEC if passing else VMEM_SPEC)

    steps = Fast if fast else Slow

    def backward(layer, dy, kept, earlier):
        x_own, q, k, v, u, lse, hidden, upward, rows, normed_all = kept
        rows_normed = rows[3]
        here = s == layer
        gain_a = jnp.where(here, smalls[0][GAIN_A], smalls[1][GAIN_A])
        earlier[0]()
        weights = [x for pair in (mixers, ups, downs) for x in pair]
        keep, send, dhidden, datt, gain_b_grad, token = feed_back(
            info, layer, dy, upward, hidden, smalls, weights, ()
        )
        token, (send,) = earlier[1](token, (send,))
        down_sum, up_sum, first_token = steps.first(rows, keep, swap_section(send))
        dq, dkv_keep, dkv_send, pre_rows, post_rows, token = attend_back(
            info, layer, q, datt, u, lse, k, v, smalls, bk, (token, first_token)
        )
        token, (dkv_send, dq) = earlier[2](token, (down_sum, up_sum), (dkv_send, dq))
        got, dq_other = swap_section(dkv_send), swap_section(dq)
        if fast:
            dn_kept, dn_sent, dnq, a_kept, a_sent, b_kept, b_sent, gain_a_grad, token = join(
                info, layer, token, (dkv_keep, got, normed_all, *rows_normed, dq, dq_other), joints, smalls, count, shard
            )
            kv_sum, q_sum = FastSum(a_kept, a_sent, (1, 2)), FastSum(b_kept, b_sent, (2, 1))
            dn_kept, dn_sent = (x.reshape(chips, 2, blk, width) for x in (dn_kept, dn_sent))
        else:
            joint_w = jnp.where(here, joints[0][0], joints[1][0])
            kv_w = lax.dynamic_slice_in_dim(joint_w, width * (1 + s), width, 1)
            dkv = (dkv_keep.astype(f32) + got.astype(f32)).astype(bf16)
            dn = dense_nt(dkv, kv_w)
            gain_a_grad = jnp.sum(dn * normed_all.astype(f32), axis=0)
            dn = dn.astype(bf16).reshape(2 * n, blk, width)
            dn = jnp.stack([dn[i if h == 0 else 2 * n - 1 - i] for i in range(n) for h in range(2)])
            dn = dn.reshape(chips, 2, 2, blk, width)
            dn_kept = lax.dynamic_index_in_dim(dn, s, 1, keepdims=False)
            dn_sent = lax.dynamic_index_in_dim(dn, 1 - s, 1, keepdims=False)
            dnq = dense_nt(dq, joint_w[:, :width])
            gain_a_grad = (gain_a_grad + jnp.sum(dnq * rows_normed[0].astype(f32), axis=0)) / gain_a
            kv_part = blocks_of(dense_tn(normed_all, dkv).astype(bf16))
            q_part = blocks_of(product(rows_normed, (half(dq, s), half(dq_other, s))))
            cut = 2 * width // 3
            kv_sum = Summer([kv_part[..., :cut]], False)
            q_sum = Summer([kv_part[..., cut:], q_part], True)
            kv_sum.send()
            q_sum.send()
        token, (dn_sent,) = earlier[3](token, (dn_sent,), (down_sum, up_sum))
        low = (dn_kept.astype(f32) + swap_section(dn_sent).astype(f32)).astype(bf16)
        gots = [xor_permute(pick(low, xi ^ d), "ctx", d) for d in range(1, chips)]
        sums = (down_sum, up_sum, kv_sum, q_sum)
        token = earlier[4](token, low, sums)
        scattered = pick(low, xi + token[0]).astype(f32)
        for x in gots:
            scattered = scattered + x.astype(f32)
        scaled = (scattered.reshape(2 * blk, width) + dnq) * gain_a
        values = x_own.astype(f32)
        inverse = rms_inverse(values)
        unit = values * inverse
        dfront = inverse * (scaled - unit * jnp.mean(scaled * unit, axis=-1, keepdims=True))
        small = jnp.concatenate([gain_a_grad.reshape(1, -1), gain_b_grad.reshape(1, -1), pre_rows, post_rows])
        return dhidden + dfront, sums, small, token

    low_chip = ctx < chips
    there = [(i, chips + i) for i in range(chips)] + [(n - 1 - i, i) for i in range(chips)]
    here = [(n - 1 - i, chips + i) for i in range(chips)] + [(i, i) for i in range(chips)]
    first = jnp.where(low_chip, s, 1 - s)
    halves = lax.dynamic_index_in_dim(cotangent, first, 1, keepdims=False)
    ones, twos = jnp.where(low_chip, halves[1], halves[0]), jnp.where(low_chip, halves[0], halves[1])
    one, two = lax.ppermute(ones, "ctx", there), lax.ppermute(twos, "ctx", here)
    dy1 = jnp.concatenate([jnp.where(m == 0, two, one), jnp.where(m == 0, one, two)])
    x1, kept0 = forward(0, pieces0, (one, two))
    y, kept1 = forward(1, gather_row(x1), ())

    def send_home(x):
        x = x.reshape(2, blk, width)
        one = lax.ppermute(jnp.where(m == 0, x[1], x[0]), "ctx", [(b, a) for a, b in there])
        two = lax.ppermute(jnp.where(m == 0, x[0], x[1]), "ctx", [(b, a) for a, b in here])
        return one, two

    def at_home(one, two):
        return jnp.where(low_chip, jnp.stack([two, one]), jnp.stack([one, two]))

    def start(sums):
        for one in sums:
            one.start() if fast else one.send()

    def no_step():
        return None

    state = {}

    def after_attention(token, sums, passing):
        token, passing, _ = steps.second(token, sums, passing)
        start(sums)
        return token, passing

    def after_join(token, passing, sums):
        state["big"], token, passing, _ = steps.halved(token, sums, passing)
        return token, passing

    def after_low(token, low, sums):
        token, _, _ = steps.second(token, sums[2:], behind=(low,))
        start(sums[2:])
        return token

    first_steps = (no_step, lambda token, passing: (token, passing), after_attention, after_join, after_low)
    dx1, (_, _, kv1, q1), small1, _ = backward(1, dy1, kept1, first_steps)
    dy0 = dx1.astype(bf16)
    y_sent = send_home(y)

    def after_feed(token, passing):
        state["joint1"], token, passing, _ = steps.halved(token, [kv1, q1], (*passing, *y_sent))
        token, (passing, *state["y"]) = steps.middle(token, state["big"], passing)
        return token, (passing,)

    def after_attention(token, sums, passing):
        token, passing, state["big1"] = steps.second(token, sums, passing, state["big"].parts)
        start(sums)
        token, passing = steps.middle(token, state["joint1"], passing)
        return token, passing

    def after_join(token, passing, sums):
        state["big0"], token, passing, state["joint1"] = steps.halved(token, sums, passing, state["joint1"].parts)
        state["token"] = token
        return token, passing

    def after_low(token, low, sums):
        token, _, _ = steps.second(token, sums[2:], behind=(low,))
        start(sums[2:])
        return steps.middle(token, state["big0"])[0]

    dx0, (down0, up0, kv0, q0), small0, token = backward(
        0, dy0, kept0, (no_step, after_feed, after_attention, after_join, after_low)
    )
    early = token
    dx0 = dx0.astype(bf16)
    dx_home = at_home(*send_home(dx0))
    y_home = at_home(*state["y"])

    small_got = swap_section(jnp.where(s == 0, small1, small0))
    small = jnp.where(s == 0, small0, small1) + small_got
    joint0, last_token, _ = steps.last(token, [kv0, q0], (dx0,))
    small = all_sum(small, (state["token"][0], early[0], token[0], last_token[0]))

    got = swap_section(jnp.where(s == 0, y_home, dx_home))
    held = jnp.where(s == 0, dx_home, y_home)
    is_first = jnp.where(low_chip, s, 1 - s) == 0
    ends = jnp.stack([jnp.where(is_first, held, got), jnp.where(is_first, got, held)], axis=1)
    ends = ends.reshape(1, micro_count, row_count, local_len, width)

    at = (lax.axis_index("dp") * n + ctx) * shard
    gain_a_out, gain_b_out = (lax.dynamic_slice_in_dim(small[i], at, shard, 0) for i in range(2))
    half_d, half_ff, times = width // 2, ff // 2, ff // width
    if fast:
        groups = (state["big0"].parts, joint0.parts, (state["big1"],), (state["joint1"],))
        keep, send = final_parts(info, groups)
        behind = keep
        joint_out, mixer_out, up_out, down_out = final_outs(info, keep, swap_section(send), width, ff)
    else:
        behind = small
        big0, joint0 = (total_of(x.parts[0], x.parts[1:]) for x in (state["big0"], joint0))
        pairs = ((big0, state["big1"]), (joint0, state["joint1"]))
        outs = []
        for at_zero, at_one in pairs:
            other = swap_section(jnp.where(s == 0, at_one, at_zero))
            own = jnp.where(s == 0, at_zero, at_one)
            outs.append((jnp.where(s == 0, own, other), jnp.where(s == 0, other, own)))
        (big_a, big_b), (joint_a, joint_b) = outs
        side = lambda *cuts: jnp.concatenate([x[:, at : at + size] for x, at, size in cuts], axis=1)
        down_out = jnp.concatenate(
            [side((big_a, i * half_d, half_d), (big_b, i * half_d, half_d)) for i in range(times)]
        )
        at = times * half_d
        up_out = side((big_a, at, half_ff), (big_b, at, half_ff))
        mixer_out = side((big_a, at + half_ff, half_d), (big_b, at + half_ff, half_d))
        joint_out = side((joint_a, width, half_d), (joint_b, width, half_d), (joint_a, 0, width), (joint_b, 0, width))
    pre_out, post_out = (x.transpose(1, 0, 2) for x in mix_grads(small, behind))
    return (
        ends,
        gain_a_out[None],
        joint_out[None],
        pre_out,
        post_out,
        mixer_out[None],
        gain_b_out[None],
        up_out[None],
        down_out[None],
    )


def solution(mesh):
    in_specs = (
        P(None, "dp", "ctx", None),
        P(None, "dp"),
        P(None, "dp", "ctx", None),
        P("section", None),
        P("section", None, None),
        P("section", None, None),
        P("section", None, None),
        P("section", None, None),
        P("section", None),
        P("section", None, None),
        P("section", None, None),
    )
    out_specs = (
        P("section", None, "dp", "ctx", None),
        P("section", ("dp", "ctx")),
        P("section", ("dp", "ctx"), None),
        P("section", None, None),
        P("section", None, None),
        P("section", ("dp", "ctx"), None),
        P("section", ("dp", "ctx")),
        P("section", ("dp", "ctx"), None),
        P("section", ("dp", "ctx"), None),
    )
    return jax.shard_map(local, mesh=mesh, in_specs=in_specs, out_specs=out_specs, check_vma=False)
```

```python
import functools
import math
import types

import jax
import jax.numpy as jnp
from jax import lax
from jax.experimental import pallas as pl
from jax.experimental.pallas import tpu as pltpu
from jax.sharding import PartitionSpec as P

HEADS = 12
HEAD = 64
eps = 1e-06
MASKED = -1e30
f32 = jnp.float32
bf16 = jnp.bfloat16
MIB = 1024 * 1024
SMALL_VMEM = 36 * MIB
BIG_VMEM = 60 * MIB


def dense(left_side, right_side):
    return jnp.dot(left_side, right_side, preferred_element_type=f32)


def dense_tn(left_side, right_side):
    return lax.dot_general(
        left_side, right_side, (((0,), (0,)), ((), ())), preferred_element_type=f32
    )


def dense_nt(left_side, right_side):
    return lax.dot_general(
        left_side, right_side, (((1,), (1,)), ((), ())), preferred_element_type=f32
    )


GAIN_A, GAIN_B, PRE, POST = 0, 1, 8, 24
SECTION, CTX, DP, LENGTH, STARTS, WHICH, BLOCKS = 0, 1, 2, 3, 4, 6, 8
SMALL_ROWS = 40


def small_of(own, got, which):
    return lambda at, size: jnp.where(which == 0, own[at : at + size, :], got[at : at + size, :])


def rms_inverse(values):
    return lax.rsqrt(jnp.mean(values * values, axis=-1, keepdims=True) + eps)


def lane_parts(x):
    return [x[:, i : i + 128] for i in range(0, x.shape[1], 128)]


def bias_of(q_start, k_start, length, bq, bk):
    rows = q_start + lax.broadcasted_iota(jnp.int32, (bq, bk), 0)
    cols = k_start + lax.broadcasted_iota(jnp.int32, (bq, bk), 1)
    return jnp.where((cols <= rows) & (cols < length), 0.0, MASKED).astype(f32)


def attend_kernel(info, small_own, small_got, joint_own, joint_got, *rest, bk, count_in, layer):
    (
        att_ref, q_ref, own_ref, x_ref, token_ref, normed_hbm, k_hbm, v_hbm, u_hbm, lse_hbm,
        joint, raw, normed, k, v, u, lse, qp, logit, total, top, norm, sems,
    ) = rest[count_in:]
    token_ref[0] = 0
    length, which = info[LENGTH], info[WHICH + layer]
    fetch((joint_own, joint_got), which, joint, sems.at[0])
    seq, width = normed.shape
    count = att_ref.shape[0]
    bq = count // 2
    small = small_of(small_own, small_got, which)
    gain, pre, post = small(GAIN_A, 1), small(PRE, HEADS), small(POST, HEADS)
    at = BLOCKS + layer * (seq // bq)
    for piece in rest[:count_in]:
        for j in range(piece.shape[0] // bq):
            x = piece[j * bq : (j + 1) * bq, :]
            span = pl.ds(pl.multiple_of(info[at] * bq, bq), bq)
            raw[span, :] = x
            x = x.astype(f32)
            normed[span, :] = (x * rms_inverse(x) * gain).astype(bf16)
            at += 1
    for i in range(2):
        span = pl.ds(pl.multiple_of(info[STARTS + i], bq), bq)
        own_ref[i * bq : (i + 1) * bq, :] = normed[span, :]
        x_ref[i * bq : (i + 1) * bq, :] = raw[span, :]
    fetched((joint_own, joint_got), joint, sems.at[0])
    cut = width // 3
    for i in range(3):
        cols = slice(width + i * cut, width + (i + 1) * cut)
        k[:, i * cut : (i + 1) * cut] = dense(normed[...], joint[:, cols]).astype(bf16)
    for i in range(3):
        cols = slice(2 * width + i * cut, 2 * width + (i + 1) * cut)
        v[:, i * cut : (i + 1) * cut] = dense(normed[...], joint[:, cols]).astype(bf16)
    q_ref[...] = dense(own_ref[...], joint[:, :width]).astype(bf16)
    outs = [
        pltpu.make_async_copy(a, b, sems.at[1 + i])
        for i, (a, b) in enumerate(((normed, normed_hbm), (k, k_hbm), (v, v_hbm)))
    ]
    for out in outs:
        out.start()

    def rows_step(step, carry):
        q_start = info[STARTS + step]
        mine = pl.ds(pl.multiple_of(step * bq, bq), bq)
        q32 = q_ref[mine, :].astype(f32)
        for h in range(HEADS):
            qp[h * bq : (h + 1) * bq, :] = (q32 * pre[h : h + 1, :]).astype(bf16)
        blocks = (jnp.minimum(q_start + bq, length) + bk - 1) // bk
        top[...] = jnp.full_like(top, MASKED)
        total[...] = jnp.zeros_like(total)
        norm[...] = jnp.zeros_like(norm)

        def score(kb, c):
            bias = bias_of(q_start, kb * bk, length, bq, bk)
            tile = dense_nt(qp[...], k[pl.ds(pl.multiple_of(kb * bk, bk), bk), :])
            tile = (tile.reshape(HEADS, bq, bk) + bias[None]).reshape(HEADS * bq, bk)
            logit[kb] = tile
            top[...] = functools.reduce(jnp.maximum, lane_parts(tile), top[...])
            return c

        lax.fori_loop(0, blocks, score, 0)
        highest = jnp.max(top[...], axis=-1, keepdims=True)
        top[...] = jnp.broadcast_to(highest, top.shape)

        def apply(kb, c):
            high = top[...]
            parts = [jnp.exp(x - high) for x in lane_parts(logit[kb])]
            norm[...] = functools.reduce(jnp.add, parts, norm[...])
            e = jnp.concatenate([x.astype(bf16) for x in parts], axis=1)
            total[...] += dense(e, v[pl.ds(pl.multiple_of(kb * bk, bk), bk), :])
            return c

        lax.fori_loop(0, blocks, apply, 0)
        sums = jnp.sum(norm[...], axis=-1, keepdims=True)
        scale = 1.0 / sums
        rows = pl.ds(pl.multiple_of(step * HEADS * bq, HEADS * bq), HEADS * bq)
        lse[rows, :] = jnp.broadcast_to(highest + jnp.log(sums), top.shape)
        att = jnp.zeros((bq, width), f32)
        for g in range(HEADS):
            part = total[g * bq : (g + 1) * bq, :] * scale[g * bq : (g + 1) * bq]
            u[pl.ds(pl.multiple_of(step * HEADS * bq + g * bq, bq), bq), :] = part.astype(bf16)
            att = att + part * post[g : g + 1, :]
        att_ref[mine, :] = att.astype(bf16)
        return carry

    lax.fori_loop(0, 2, rows_step, 0)
    outs += [pltpu.make_async_copy(u, u_hbm, sems.at[4]), pltpu.make_async_copy(lse, lse_hbm, sems.at[5])]
    for out in outs[3:]:
        out.start()
    for out in outs:
        out.wait()


VMEM_SPEC = pl.BlockSpec(memory_space=pltpu.VMEM)
FAR_SPEC = pl.BlockSpec(memory_space=pltpu.VMEM)
ANY_SPEC = pl.BlockSpec(memory_space=pl.ANY)
HBM_SPEC = pl.BlockSpec(memory_space=pltpu.HBM)
SMEM_SPEC = pl.BlockSpec(memory_space=pltpu.SMEM)
TOKEN = jax.ShapeDtypeStruct((1,), jnp.int32)

LARGE = 64 * 1024
SMALL_COST = pl.CostEstimate(flops=0, bytes_accessed=0, transcendentals=0)


def in_hbm(spec, x):
    return (spec is FAR_SPEC or spec is HBM_SPEC) and math.prod(x.shape) >= LARGE


def from_hbm(spec, x):
    return pltpu.with_memory_space_constraint(x, pltpu.HBM) if in_hbm(spec, x) else x


def result_in_hbm(spec, x):
    return pltpu.HBM(x.shape, x.dtype) if in_hbm(spec, x) else x


def one_step(kernel, *, in_specs, out_specs, out_shape, **rest):
    def whole(spec, x):
        if spec is not VMEM_SPEC and spec is not FAR_SPEC:
            return spec
        zeros = (0,) * len(x.shape)
        return pl.BlockSpec(x.shape, lambda i: zeros, pipeline_mode=pl.Buffered(1))

    def run(*args):
        return pl.pallas_call(
            kernel,
            cost_estimate=SMALL_COST,
            grid=(1,),
            in_specs=[whole(*x) for x in zip(in_specs, args, strict=True)],
            out_specs=[whole(*x) for x in zip(out_specs, out_shape, strict=True)],
            out_shape=[result_in_hbm(*x) for x in zip(out_specs, out_shape)],
            **rest,
        )(*[from_hbm(*x) for x in zip(in_specs, args)])

    return run


def attend(info, layer, pieces, count, smalls, joints, bk):
    width = pieces[0].shape[1]
    seq = sum(x.shape[0] for x in pieces)
    bq = count // 2
    shape = jax.ShapeDtypeStruct
    return one_step(
        functools.partial(attend_kernel, bk=bk, count_in=len(pieces), layer=layer),
        in_specs=[SMEM_SPEC] + [VMEM_SPEC] * 2 + [HBM_SPEC] * 2 + [VMEM_SPEC] * len(pieces),
        out_specs=[VMEM_SPEC, FAR_SPEC, FAR_SPEC, VMEM_SPEC, SMEM_SPEC] + [HBM_SPEC] * 5,
        out_shape=[shape((count, width), bf16)] * 4
        + [TOKEN]
        + [shape((seq, width), bf16)] * 3
        + [shape((HEADS * count, width), bf16), shape((HEADS * count, 128), f32)],
        scratch_shapes=[
            pltpu.VMEM((width, 3 * width), bf16),
            pltpu.VMEM((seq, width), bf16),
            pltpu.VMEM((seq, width), bf16),
            pltpu.VMEM((seq, width), bf16),
            pltpu.VMEM((seq, width), bf16),
            pltpu.VMEM((HEADS * count, width), bf16),
            pltpu.VMEM((HEADS * count, 128), f32),
            pltpu.VMEM((HEADS * bq, width), bf16),
            pltpu.VMEM((seq // bk, HEADS * bq, bk), f32),
            pltpu.VMEM((HEADS * bq, width), f32),
            pltpu.VMEM((HEADS * bq, 128), f32),
            pltpu.VMEM((HEADS * bq, 128), f32),
            pltpu.SemaphoreType.DMA((6,)),
        ],
        compiler_params=pltpu.CompilerParams(vmem_limit_bytes=BIG_VMEM),
    )(info, *smalls, *joints, *pieces)


def feed_kernel(
    info, x_ref, att_ref, small_own, small_got,
    mixer_own, mixer_got, up_own, up_got, down_own, down_got, *rest, tile, extra, layer,
):
    (
        out_ref, hidden_ref, two_ref, upward_hbm, active_hbm, token_ref,
        mixer, up, down, upward, active, sems,
    ) = rest[extra:]
    token_ref[0] = 0
    which = info[WHICH + layer]
    pairs = ((mixer_own, mixer_got), (up_own, up_got), (down_own, down_got))
    fetch(pairs[0], which, mixer, sems.at[0])
    tiles = down.shape[0] // tile
    for j in range(tiles):
        fetch(pairs[1], which, up, sems.at[1 + j], column_part(j, tile))
        fetch(pairs[2], which, down, sems.at[1 + tiles + j], row_part(j, tile))
    gain = small_of(small_own, small_got, which)(GAIN_B, 1)
    fetched(pairs[0], mixer, sems.at[0])
    hidden = x_ref[...].astype(f32) + dense(att_ref[...], mixer[...])
    hidden_ref[...] = hidden
    two = (hidden * rms_inverse(hidden) * gain).astype(bf16)
    two_ref[...] = two
    result, outs = hidden, []
    for j in range(tiles):
        span = slice(j * tile, (j + 1) * tile)
        fetched(pairs[1], up, sems.at[1 + j], column_part(j, tile))
        u = dense(two, up[:, span])
        upward[:, span] = u
        act = (0.5 * u * (1.0 + jnp.tanh(0.7978845608 * (u + 0.044715 * (u * u * u))))).astype(bf16)
        active[:, span] = act
        part = column_part(j, tile)
        for i, (x, y) in enumerate(((upward, upward_hbm), (active, active_hbm))):
            outs.append(pltpu.make_async_copy(x.at[part], y.at[part], sems.at[1 + (2 + i) * tiles + j]))
            outs[-1].start()
        fetched(pairs[2], down, sems.at[1 + tiles + j], row_part(j, tile))
        result = result + dense(act, down[span, :])
    out_ref[...] = result.astype(bf16)
    for out in outs:
        out.wait()


def feed(info, layer, x, attended, smalls, weights, ff, extras):
    count, width = x.shape
    shape = jax.ShapeDtypeStruct
    return one_step(
        functools.partial(feed_kernel, tile=width, extra=len(extras), layer=layer),
        in_specs=[SMEM_SPEC] + [VMEM_SPEC] * 4 + [HBM_SPEC] * (6 + len(extras)),
        out_specs=[VMEM_SPEC, FAR_SPEC, FAR_SPEC] + [HBM_SPEC] * 2 + [SMEM_SPEC],
        out_shape=[
            shape((count, width), bf16),
            shape((count, width), f32),
            shape((count, width), bf16),
            shape((count, ff), f32),
            shape((count, ff), bf16),
            TOKEN,
        ],
        scratch_shapes=[
            pltpu.VMEM((width, width), bf16),
            pltpu.VMEM((width, ff), bf16),
            pltpu.VMEM((ff, width), bf16),
            pltpu.VMEM((count, ff), f32),
            pltpu.VMEM((count, ff), bf16),
            pltpu.SemaphoreType.DMA((1 + 4 * (ff // width),)),
        ],
        compiler_params=pltpu.CompilerParams(vmem_limit_bytes=SMALL_VMEM),
    )(info, x, attended, *smalls, *weights, *extras)


def fetch(pair, which, buffer, semaphore, at=()):
    for i, ref in enumerate(pair):

        @pl.when(which == i)
        def _(ref=ref):
            pltpu.make_async_copy(ref.at[(0, *at)], buffer.at[at] if at else buffer, semaphore).start()


def fetched(pair, buffer, semaphore, at=()):
    pltpu.make_async_copy(pair[0].at[(0, *at)], buffer.at[at] if at else buffer, semaphore).wait()


def row_part(i, size):
    return pl.ds(i * size, size), slice(None)


def column_part(i, size):
    return slice(None), pl.ds(i * size, size)


def gelu_slope(u):
    inner = 0.7978845608 * (u + 0.044715 * (u * u * u))
    t = jnp.tanh(inner)
    return 0.5 * (1.0 + t) + 0.5 * u * (1.0 - t * t) * (0.7978845608 + 0.1070322243 * (u * u))


def feed_back_kernel(
    info, dy_ref, upward_hbm, hidden_hbm, small_own, small_got,
    mixer_own, mixer_got, up_own, up_got, down_own, down_got, *rest, tile, extra, layer,
):
    (
        keep_ref, send_ref, dhidden_ref, datt_ref, gain_grad_ref, token_ref,
        mixer, up, down, upward_ref, hidden_ref, sems,
    ) = rest[extra:]
    token_ref[0] = 0
    which = info[WHICH + layer]
    width = dy_ref.shape[1]
    half_ff, half = down.shape[0] // 2, width // 2

    def put(value, number, at):
        for ref, equal in ((keep_ref, True), (send_ref, False)):

            @pl.when((info[SECTION] == number) == equal)
            def _(ref=ref):
                ref[:, at : at + value.shape[1]] = value

    pairs = ((down_own, down_got), (up_own, up_got), (mixer_own, mixer_got))
    tiles = down.shape[0] // tile
    for j in range(tiles):
        fetch(pairs[0], which, down, sems.at[j], row_part(j, tile))
        if j == 0:
            upward_copy = pltpu.make_async_copy(upward_hbm, upward_ref, sems.at[2 * tiles])
            upward_copy.start()
        fetch(pairs[1], which, up, sems.at[tiles + j], column_part(j, tile))
    hidden_copy = pltpu.make_async_copy(hidden_hbm, hidden_ref, sems.at[2 * tiles + 1])
    hidden_copy.start()
    fetch(pairs[2], which, mixer, sems.at[2 * tiles + 2])
    gain = small_of(small_own, small_got, which)(GAIN_B, 1)
    dy = dy_ref[...]
    grad = jnp.zeros(hidden_ref.shape, f32)
    for j in range(tiles):
        span = slice(j * tile, (j + 1) * tile)
        fetched(pairs[0], down, sems.at[j], row_part(j, tile))
        dactive = dense_nt(dy, down[span, :])
        if j == 0:
            upward_copy.wait()
        dup = (dactive * gelu_slope(upward_ref[:, span])).astype(bf16)
        put(dup, j * tile // half_ff, j * tile % half_ff)
        fetched(pairs[1], up, sems.at[tiles + j], column_part(j, tile))
        grad = grad + dense_nt(dup, up[:, span])
    hidden_copy.wait()
    hidden = hidden_ref[...]
    inverse = rms_inverse(hidden)
    unit = hidden * inverse
    gain_grad_ref[...] = jnp.sum(grad * unit, axis=0, keepdims=True)
    scaled = grad * gain
    dhidden = dy.astype(f32) + inverse * (scaled - unit * jnp.mean(scaled * unit, axis=-1, keepdims=True))
    dhidden_ref[...] = dhidden
    low = dhidden.astype(bf16)
    for i in range(2):
        put(low[:, i * half : (i + 1) * half], i, half_ff)
        put(dy[:, i * half : (i + 1) * half], i, half_ff + half)
    fetched(pairs[2], mixer, sems.at[2 * tiles + 2])
    datt_ref[...] = dense_nt(low, mixer[...]).astype(bf16)


def feed_back(info, layer, dy, upward, hidden, smalls, weights, extras):
    count, width = dy.shape
    ff = upward.shape[1]
    shape = jax.ShapeDtypeStruct
    return one_step(
        functools.partial(feed_back_kernel, tile=width, extra=len(extras), layer=layer),
        in_specs=[SMEM_SPEC, VMEM_SPEC, HBM_SPEC, HBM_SPEC, VMEM_SPEC, VMEM_SPEC] + [HBM_SPEC] * (6 + len(extras)),
        out_specs=[VMEM_SPEC, VMEM_SPEC, FAR_SPEC, VMEM_SPEC, VMEM_SPEC, SMEM_SPEC],
        out_shape=[
            shape((count, ff // 2 + width), bf16),
            shape((count, ff // 2 + width), bf16),
            shape((count, width), f32),
            shape((count, width), bf16),
            shape((1, width), f32),
            TOKEN,
        ],
        scratch_shapes=[
            pltpu.VMEM((width, width), bf16),
            pltpu.VMEM((width, ff), bf16),
            pltpu.VMEM((ff, width), bf16),
            pltpu.VMEM((count, ff), f32),
            pltpu.VMEM((count, width), f32),
            pltpu.SemaphoreType.DMA((2 * (ff // width) + 3,)),
        ],
        compiler_params=pltpu.CompilerParams(vmem_limit_bytes=SMALL_VMEM),
    )(info, dy, upward, hidden, *smalls, *weights, *extras)


def attend_back_kernel(
    info, q_ref, datt_ref, u_ref, lse_ref, k_hbm, v_hbm, small_own, small_got, *rest, bq, bk, extra, layer
):
    (
        dq_ref, keep_ref, send_ref, pre_grad_ref, post_grad_ref, token_ref,
        qp, dp, dk, dv, w, delta, k_ref, v_ref, sems,
    ) = rest[extra:]
    token_ref[0] = 0
    step = pl.program_id(0)
    copies = [pltpu.make_async_copy(x, y, sems.at[i]) for i, (x, y) in enumerate(((k_hbm, k_ref), (v_hbm, v_ref)))]

    @pl.when(step == 0)
    def _():
        for copy in copies:
            copy.start()

    length, which, q_start = info[LENGTH], info[WHICH + layer], info[STARTS + step]
    small = small_of(small_own, small_got, which)
    pre, post = small(PRE, HEADS), small(POST, HEADS)

    @pl.when(step == 0)
    def _():
        dk[...] = jnp.zeros_like(dk)
        dv[...] = jnp.zeros_like(dv)
        pre_grad_ref[...] = jnp.zeros_like(pre_grad_ref)
        post_grad_ref[...] = jnp.zeros_like(post_grad_ref)

    q32 = q_ref[...].astype(f32)
    datt = datt_ref[...].astype(f32)
    for h in range(HEADS):
        part = slice(h * bq, (h + 1) * bq)
        qp[part, :] = (q32 * pre[h : h + 1, :]).astype(bf16)
        scaled = datt * post[h : h + 1, :]
        dp[part, :] = scaled.astype(bf16)
        u = u_ref[part, :].astype(f32)
        delta[part, :] = jnp.broadcast_to(jnp.sum(scaled * u, axis=-1, keepdims=True), (bq, 128))
        post_grad_ref[h : h + 1, :] += jnp.sum(datt * u, axis=0, keepdims=True)
    w[...] = jnp.zeros_like(w)
    blocks = (jnp.minimum(q_start + bq, length) + bk - 1) // bk

    @pl.when(step == 0)
    def _():
        for copy in copies:
            copy.wait()

    def block(kb, c):
        span = pl.ds(pl.multiple_of(kb * bk, bk), bk)
        bias = bias_of(q_start, kb * bk, length, bq, bk)
        k_blk, v_blk = k_ref[span, :], v_ref[span, :]
        logits = dense_nt(qp[...], k_blk)
        logits = (logits.reshape(HEADS, bq, bk) + bias[None]).reshape(HEADS * bq, bk)
        grad = dense_nt(dp[...], v_blk)
        lse, spread = lse_ref[...], delta[...]
        attention, dlog = [], []
        for x, g in zip(lane_parts(logits), lane_parts(grad)):
            a = jnp.exp(x - lse)
            attention.append(a.astype(bf16))
            dlog.append((a * (g - spread)).astype(bf16))
        attention, dlog = jnp.concatenate(attention, axis=1), jnp.concatenate(dlog, axis=1)
        dv[span, :] += dense_tn(attention, dp[...])
        dk[span, :] += dense_tn(dlog, qp[...])
        w[...] += dense(dlog, k_blk)
        return c

    lax.fori_loop(0, blocks, block, 0)
    dq = jnp.zeros_like(q32)
    for h in range(HEADS):
        part = w[h * bq : (h + 1) * bq, :]
        dq = dq + part * pre[h : h + 1, :]
        pre_grad_ref[h : h + 1, :] += jnp.sum(part * q32, axis=0, keepdims=True)
    dq_ref[...] = dq.astype(bf16)

    for section, (kept, sent) in enumerate(((dk, dv), (dv, dk))):

        @pl.when((step == pl.num_programs(0) - 1) & (info[SECTION] == section))
        def _(kept=kept, sent=sent):
            keep_ref[...] = kept[...].astype(bf16)
            send_ref[...] = sent[...].astype(bf16)


def attend_back(info, layer, q, datt, u, lse, k, v, smalls, bk, extras):
    count, width = q.shape
    seq = k.shape[0]
    bq = count // 2
    full = lambda i, place: (0, 0)
    row = lambda i, place: (i, 0)
    shape = jax.ShapeDtypeStruct
    return pl.pallas_call(
        cost_estimate=SMALL_COST,
        kernel=functools.partial(attend_back_kernel, bq=bq, bk=bk, extra=len(extras), layer=layer),
        grid_spec=pltpu.PrefetchScalarGridSpec(
            num_scalar_prefetch=1,
            grid=(2,),
            in_specs=[
                pl.BlockSpec((bq, width), row),
                pl.BlockSpec((bq, width), row),
                pl.BlockSpec((HEADS * bq, width), row),
                pl.BlockSpec((HEADS * bq, 128), row),
                HBM_SPEC,
                HBM_SPEC,
                pl.BlockSpec((SMALL_ROWS, width), full),
                pl.BlockSpec((SMALL_ROWS, width), full),
            ]
            + [HBM_SPEC] * len(extras),
            out_specs=[
                pl.BlockSpec((bq, width), row),
                pl.BlockSpec((seq, width), full),
                pl.BlockSpec((seq, width), full),
                pl.BlockSpec((HEADS, width), full),
                pl.BlockSpec((HEADS, width), full),
                SMEM_SPEC,
            ],
            scratch_shapes=[
                pltpu.VMEM((HEADS * bq, width), bf16),
                pltpu.VMEM((HEADS * bq, width), bf16),
                pltpu.VMEM((seq, width), f32),
                pltpu.VMEM((seq, width), f32),
                pltpu.VMEM((HEADS * bq, width), f32),
                pltpu.VMEM((HEADS * bq, 128), f32),
                pltpu.VMEM((seq, width), bf16),
                pltpu.VMEM((seq, width), bf16),
                pltpu.SemaphoreType.DMA((2,)),
            ],
        ),
        out_shape=[
            shape((count, width), bf16),
            shape((seq, width), bf16),
            shape((seq, width), bf16),
            shape((HEADS, width), f32),
            shape((HEADS, width), f32),
            TOKEN,
        ],
        compiler_params=pltpu.CompilerParams(vmem_limit_bytes=BIG_VMEM),
    )(info, q, datt, u, lse, k, v, *smalls, *extras)


def swap_section(x):
    return lax.ppermute(x, "section", [(0, 1), (1, 0)])


def xor_permute(x, axis, by):
    return lax.ppermute(x, axis, [(i, i ^ by) for i in range(lax.axis_size(axis))])


def from_xor_order(x, index):
    places = range(x.shape[0])
    return jnp.concatenate([lax.dynamic_index_in_dim(x, index ^ i, 0) for i in places])


def token_kernel(*refs):
    refs[-1][0] = 0


def token_after(*arrays):
    arrays = [x if x.ndim == 1 else x[(0,) * (x.ndim - 2)][:16, :128] for x in arrays]
    return pl.pallas_call(
        token_kernel,
        cost_estimate=SMALL_COST,
        in_specs=[SMEM_SPEC if x.ndim == 1 else VMEM_SPEC for x in arrays],
        out_specs=SMEM_SPEC,
        out_shape=TOKEN,
    )(*arrays)[0]


def half_columns(ref, which, size):
    return ref[:, pl.ds(pl.multiple_of(which * size, size), size)]


def split_blocks(blocks, kept, sent, mine):
    for i in range(kept.shape[0]):
        kept[i] = blocks[2 * i + mine]
        sent[i] = blocks[2 * i + 1 - mine]


def split_blocks_first(blocks, kept, sent, mine):
    for i in range(kept.shape[0]):
        at = 4 * (i // 2) + i % 2
        kept[i] = blocks[at + 2 * mine]
        sent[i] = blocks[at + 2 * (1 - mine)]


def products_kernel(
    seat, active, active_other, two, two_other, att, att_other, right, right_other,
    down_kept, down_sent, up_kept, up_sent, token_ref, down_blocks, up_blocks,
):
    token_ref[0] = 0
    width = att.shape[1]
    half, half_ff = width // 2, active.shape[1] // 2
    both = lambda left, left_other, cols: dense_tn(left, right[:, cols]) + dense_tn(left_other, right_other[:, cols])
    rows = down_blocks.shape[1]
    each = width // rows
    for j in range(active.shape[1] // width):
        cols = slice(j * width, (j + 1) * width)
        grad = both(active[:, cols], active_other[:, cols], slice(half_ff + half, half_ff + width))
        down_blocks[j * each : (j + 1) * each] = grad.astype(bf16).reshape(each, rows, half)
    split_blocks(down_blocks, down_kept, down_sent, seat[CTX] % 2)
    rows = up_blocks.shape[1]
    tile = half_ff // 2
    for j in range(2):
        cols = slice(j * tile, (j + 1) * tile)
        up_blocks[:, :, cols] = both(two[...], two_other[...], cols).astype(bf16).reshape(-1, rows, tile)
    cols = slice(half_ff, half_ff + half)
    up_blocks[:, :, cols] = both(att[...], att_other[...], cols).astype(bf16).reshape(-1, rows, half)
    split_blocks_first(up_blocks, up_kept, up_sent, seat[CTX] // 2)


def products(seat, arrays, count, rows):
    ff, width = arrays[0].shape[1], arrays[4].shape[1]
    down, up = (ff // count, width // 2), (rows, (ff + width) // 2)
    shape = lambda x: jax.ShapeDtypeStruct((count // 2, *x), bf16)
    outs = one_step(
        products_kernel,
        in_specs=[SMEM_SPEC] + [FAR_SPEC] * 6 + [VMEM_SPEC] * 2,
        out_specs=[FAR_SPEC] * 4 + [SMEM_SPEC],
        out_shape=[shape(down)] * 2 + [shape(up)] * 2 + [TOKEN],
        scratch_shapes=[pltpu.VMEM((count, *down), bf16), pltpu.VMEM((count, *up), bf16)],
        compiler_params=pltpu.CompilerParams(vmem_limit_bytes=SMALL_VMEM),
    )(seat, *arrays)
    return FastSum(*outs[:2], (1, 2)), FastSum(*outs[2:4], (2, 1)), outs[4]


def second_kernel(seat, token_in, *refs, bits, passing, closing, behind):
    count = len(bits)
    refs = refs[behind + passing :]
    parts, refs = refs[2 * count : 2 * count + closing], refs[: 2 * count] + refs[2 * count + closing :]
    refs[4 * count][0] = token_in[0]
    if closing:
        refs[4 * count + 1][...] = functools.reduce(jnp.add, [x[...].astype(f32) for x in parts])
    for i, bit in enumerate(bits):
        kept, got = refs[2 * i], refs[2 * i + 1]
        kept_out, sent_out = refs[2 * count + 2 * i], refs[2 * count + 2 * i + 1]
        mine = (seat[1] // bit) % 2
        for j in range(kept_out.shape[0]):
            for out, at in ((kept_out, 2 * j + mine), (sent_out, 2 * j + 1 - mine)):
                out[j] = (kept[at].astype(f32) + got[at].astype(f32)).astype(bf16)


def last_kernel(seat, token_in, *refs, count, rows, dp_count, passing):
    refs = refs[passing:]
    total, outs, token_ref = refs[2 * count], refs[2 * count + 1 : 2 * count + dp_count], refs[2 * count + dp_count]
    token_ref[0] = token_in[0]
    at = 0
    for i in range(count):
        kept, got = refs[2 * i], refs[2 * i + 1]
        size = kept.shape[2]
        for j in range(kept.shape[1] // rows):
            part = slice(j * rows, (j + 1) * rows)
            for by in range(len(outs) + 1):
                z = seat[2] ^ by
                value = kept[z, part, :].astype(f32) + got[z, part, :].astype(f32)
                if by == 0:
                    total[:, at : at + size] = value
                else:
                    outs[by - 1][:, at : at + size] = value.astype(bf16)
            at += size


def halved_kernel(seat, token_in, *refs, count, rows, passing, closing):
    refs = refs[passing:]
    parts, refs = refs[2 * count : 2 * count + closing], refs[: 2 * count] + refs[2 * count + closing :]
    kept_out, sent_out, token_ref = refs[2 * count : 2 * count + 3]
    if closing:
        refs[2 * count + 3][...] = functools.reduce(jnp.add, [x[...].astype(f32) for x in parts])
    token_ref[0] = token_in[0]
    mine = seat[2] % 2
    at = 0
    for i in range(count):
        kept, got = refs[2 * i], refs[2 * i + 1]
        size = kept.shape[2]
        for j in range(kept.shape[1] // rows):
            part = slice(j * rows, (j + 1) * rows)
            for b in range(2):
                for out, z in ((kept_out, 2 * b + mine), (sent_out, 2 * b + 1 - mine)):
                    value = kept[z, part, :].astype(f32) + got[z, part, :].astype(f32)
                    out[b, :, at : at + size] = value.astype(bf16)
            at += size


def middle_kernel(seat, token_in, *refs, passing):
    kept, got, total, sent, token_ref = refs[passing : passing + 5]
    token_ref[0] = token_in[0]
    mine = seat[2] // 2
    total[...] = kept[mine].astype(f32) + got[mine].astype(f32)
    sent[...] = (kept[1 - mine].astype(f32) + got[1 - mine].astype(f32)).astype(bf16)


class Halved:
    def __init__(self, kept, sent):
        self.kept, self.got = kept, xor_permute(sent, "dp", 1)


def halved_step(seat, token, sums, rows, passing, closing, spec):
    closed = [jax.ShapeDtypeStruct(x.shape, f32) for x in closing[:1]]
    specs_in, specs_out, shapes, aliases = handed_on(passing, 2, 3 + len(closed))
    size = sum(x.kept.shape[1] // rows * x.kept.shape[2] for x in sums)
    shape = jax.ShapeDtypeStruct((2, rows, size), bf16)
    kept, sent, token, *rest = one_step(
        functools.partial(halved_kernel, count=len(sums), rows=rows, passing=len(passing), closing=len(closing)),
        in_specs=[SMEM_SPEC] * 2 + specs_in + [spec] * (2 * len(sums) + len(closing)),
        out_specs=[spec, VMEM_SPEC, SMEM_SPEC] + [FAR_SPEC] * len(closed) + specs_out,
        out_shape=[shape, shape, TOKEN] + closed + shapes,
        input_output_aliases=aliases,
        compiler_params=pltpu.CompilerParams(vmem_limit_bytes=SMALL_VMEM),
    )(seat, token, *passing, *[y for x in sums for y in (x.kept, x.got)], *closing)
    return Halved(kept, sent), token, tuple(rest[len(closed) :]), rest[0] if closed else None


def middle_step(seat, token, halved, passing, spec):
    specs_in, specs_out, shapes, aliases = handed_on(passing, 2, 3)
    shape = jax.ShapeDtypeStruct
    total, sent, token, *passing = one_step(
        functools.partial(middle_kernel, passing=len(passing)),
        in_specs=[SMEM_SPEC] * 2 + specs_in + [spec] * 2,
        out_specs=[FAR_SPEC, VMEM_SPEC, SMEM_SPEC] + specs_out,
        out_shape=[shape(halved.kept.shape[1:], f32), shape(halved.kept.shape[1:], bf16), TOKEN] + shapes,
        input_output_aliases=aliases,
        compiler_params=pltpu.CompilerParams(vmem_limit_bytes=SMALL_VMEM),
    )(seat, token, *passing, halved.kept, halved.got)
    halved.parts = (total, xor_permute(sent, "dp", 2))
    return token, tuple(passing)


class FastSum:
    def __init__(self, kept, sent, bits):
        self.kept, self.bits = kept, bits
        self.got = xor_permute(sent, "ctx", bits[0])

    def start(self):
        self.got = xor_permute(self.sent, "ctx", self.bits[1])


def handed_on(passing, before, after):
    specs = [ANY_SPEC] * len(passing)
    shapes = [jax.ShapeDtypeStruct(x.shape, x.dtype) for x in passing]
    return specs, specs, shapes, {before + i: after + i for i in range(len(passing))}


def hand_on_kernel(token_in, *refs, meanwhile, passing):
    refs[meanwhile + passing][0] = token_in[0]


def hand_on(token, meanwhile, passing):
    specs_in, specs_out, shapes, aliases = handed_on(passing, 1 + len(meanwhile), 1)
    outs = one_step(
        functools.partial(hand_on_kernel, meanwhile=len(meanwhile), passing=len(passing)),
        in_specs=[SMEM_SPEC] + [VMEM_SPEC] * len(meanwhile) + specs_in,
        out_specs=[SMEM_SPEC] + specs_out,
        out_shape=[TOKEN] + shapes,
        input_output_aliases=aliases,
    )(token, *meanwhile, *passing)
    return outs[0], outs[1:]


def second_step(seat, token, sums, passing, closing, behind, spec):
    closed = [jax.ShapeDtypeStruct(x.shape, f32) for x in closing[:1]]
    specs_in, specs_out, shapes, aliases = handed_on(passing, 2 + len(behind), 2 * len(sums) + 1 + len(closed))
    shape = lambda x: jax.ShapeDtypeStruct((x.shape[0] // 2,) + x.shape[1:], bf16)
    outs = one_step(
        functools.partial(second_kernel, bits=[x.bits[1] for x in sums], passing=len(passing), closing=len(closing), behind=len(behind)),
        in_specs=[SMEM_SPEC] * 2 + [ANY_SPEC] * len(behind) + specs_in + [spec] * (2 * len(sums) + len(closing)),
        out_specs=[VMEM_SPEC] * (2 * len(sums)) + [SMEM_SPEC] + [FAR_SPEC] * len(closed) + specs_out,
        out_shape=[shape(x.kept) for x in sums for _ in range(2)] + [TOKEN] + closed + shapes,
        input_output_aliases=aliases,
        compiler_params=pltpu.CompilerParams(vmem_limit_bytes=SMALL_VMEM),
    )(seat, token, *behind, *passing, *[y for x in sums for y in (x.kept, x.got)], *closing)
    for i, x in enumerate(sums):
        x.kept, x.sent = outs[2 * i], outs[2 * i + 1]
    outs = outs[2 * len(sums) :]
    return outs[0], outs[1 + len(closed) :], outs[1] if closed else None


def last_step(seat, token, sums, rows, passing):
    dp_count = sums[0].kept.shape[0]
    specs_in, specs_out, shapes, aliases = handed_on(passing, 2, dp_count + 1)
    size = sum(x.kept.shape[1] // rows * x.kept.shape[2] for x in sums)
    shape = jax.ShapeDtypeStruct((rows, size), bf16)
    outs = one_step(
        functools.partial(last_kernel, count=len(sums), rows=rows, dp_count=dp_count, passing=len(passing)),
        in_specs=[SMEM_SPEC] * 2 + specs_in + [VMEM_SPEC] * (2 * len(sums)),
        out_specs=[VMEM_SPEC] * dp_count + [SMEM_SPEC] + specs_out,
        out_shape=[jax.ShapeDtypeStruct((rows, size), f32)] + [shape] * (dp_count - 1) + [TOKEN] + shapes,
        input_output_aliases=aliases,
        compiler_params=pltpu.CompilerParams(vmem_limit_bytes=SMALL_VMEM),
    )(seat, token, *passing, *[y for x in sums for y in (x.kept, x.got)])
    gots = [xor_permute(x, "dp", by) for by, x in enumerate(outs[1:dp_count], 1)]
    return outs[0], gots, outs[dp_count], outs[dp_count + 1 :]


def final_parts_kernel(seat, *refs, counts):
    *refs, keep, send = refs
    sums, at = [], 0
    for count in counts:
        sums.append(functools.reduce(jnp.add, [x[...].astype(f32) for x in refs[at : at + count]]))
        at += count
    cut = sums[0].shape[1]
    for section in range(2):

        @pl.when(seat[0] == section)
        def _(section=section):
            for out, layer in ((keep, section), (send, 1 - section)):
                out[:, :cut] = sums[2 * layer]
                out[:, cut:] = sums[2 * layer + 1]


def final_parts(seat, groups):
    parts = [x for group in groups for x in group]
    rows = parts[0].shape[0]
    out = jax.ShapeDtypeStruct((rows, groups[0][0].shape[1] + groups[1][0].shape[1]), f32)
    return one_step(
        functools.partial(final_parts_kernel, counts=[len(x) for x in groups]),
        in_specs=[SMEM_SPEC] + [VMEM_SPEC] * len(parts),
        out_specs=[VMEM_SPEC] * 2,
        out_shape=[out, out],
        compiler_params=pltpu.CompilerParams(vmem_limit_bytes=SMALL_VMEM),
    )(seat, *parts)


def final_outs_kernel(seat, keep, got, joint, mixer, up, down):
    half, half_up, rows = mixer.shape[1] // 2, up.shape[1] // 2, mixer.shape[0]
    width = 2 * half
    for section in range(2):

        @pl.when(seat[0] == section)
        def _(section=section):
            for i, ref in enumerate((keep, got) if section == 0 else (got, keep)):
                times = down.shape[0] // rows
                for j in range(times):
                    down[j * rows : (j + 1) * rows, i * half : (i + 1) * half] = ref[:, j * half : (j + 1) * half]
                at = times * half
                up[:, i * half_up : (i + 1) * half_up] = ref[:, at : at + half_up]
                at += half_up
                mixer[:, i * half : (i + 1) * half] = ref[:, at : at + half]
                at += half
                joint[:, (1 + i) * width : (2 + i) * width] = ref[:, at : at + width]
                joint[:, i * half : (i + 1) * half] = ref[:, at + width : at + width + half]


def final_outs(seat, keep, got, width, ff):
    rows = keep.shape[0]
    shape = lambda *x: jax.ShapeDtypeStruct(x, f32)
    return one_step(
        final_outs_kernel,
        in_specs=[SMEM_SPEC] + [VMEM_SPEC] * 2,
        out_specs=[VMEM_SPEC] * 4,
        out_shape=[shape(rows, 3 * width), shape(rows, width), shape(rows, ff), shape(rows * (ff // width), width)],
        compiler_params=pltpu.CompilerParams(vmem_limit_bytes=SMALL_VMEM),
    )(seat, keep, got)


def mix_grads_kernel(small, _, pre, post):
    rows = lax.broadcasted_iota(jnp.int32, (HEADS, small.shape[1]), 0)
    cols = lax.broadcasted_iota(jnp.int32, (HEADS, small.shape[1]), 1)
    heads = jnp.where(cols // HEAD == rows, 1.0, 0.0).astype(f32)
    dot = lambda a, b: lax.dot_general(
        a, b, (((1,), (1,)), ((), ())), precision=lax.Precision.HIGHEST, preferred_element_type=f32
    )
    pre[:, 0, :] = 0.125 * dot(heads, small[2 : 2 + HEADS, :])
    post[:, 0, :] = dot(small[2 + HEADS : 2 + 2 * HEADS, :], heads)


def mix_grads(small, behind):
    out = jax.ShapeDtypeStruct((HEADS, 1, HEADS), f32)
    return one_step(
        mix_grads_kernel, in_specs=[VMEM_SPEC, ANY_SPEC], out_specs=[VMEM_SPEC] * 2, out_shape=[out, out]
    )(small, behind)


def total_of(part, gots):
    for got in gots:
        part = part + got.astype(f32)
    return part


def join_kernel(
    seat, token_in, keep_ref, got_ref, normed_ref, own, own_other, dq, dq_other, joint_own, joint_got,
    small_own, small_got, dn_kept, dn_sent, dnq_ref, a_kept, a_sent, b_kept, b_sent, gain_grad_ref, token_ref,
    kv_w, q_w, dkv, dn, a_blocks, b_blocks, sems, *, layer,
):
    token_ref[0] = token_in[0]
    width = dkv.shape[1]
    section, which = seat[SECTION], seat[WHICH + layer]
    for i, ref in enumerate((joint_own, joint_got)):

        @pl.when(which == i)
        def _(ref=ref):
            cols = pl.ds(pl.multiple_of((1 + section) * width, width), width)
            pltpu.make_async_copy(ref.at[0, :, cols], kv_w, sems.at[0]).start()
            pltpu.make_async_copy(ref.at[0, :, pl.ds(0, width)], q_w, sems.at[1]).start()

    dkv[...] = (keep_ref[...].astype(f32) + got_ref[...].astype(f32)).astype(bf16)
    rows, size_a, size_b = a_blocks.shape[1], a_blocks.shape[2], b_blocks.shape[2]
    grad = dense_tn(normed_ref[...], dkv[:, :size_a])
    a_blocks[...] = grad.astype(bf16).reshape(-1, rows, size_a)
    grad = dense_tn(normed_ref[...], dkv[:, size_a:])
    b_blocks[:, :, : width - size_a] = grad.astype(bf16).reshape(-1, rows, width - size_a)
    half = width // 2
    grad = dense_tn(own[...], half_columns(dq, section, half)) + dense_tn(
        own_other[...], half_columns(dq_other, section, half)
    )
    b_blocks[:, :, width - size_a :] = grad.astype(bf16).reshape(-1, rows, half)
    split_blocks(a_blocks, a_kept, a_sent, seat[1] % 2)
    split_blocks_first(b_blocks, b_kept, b_sent, seat[1] // 2)
    for i in range(2):
        pltpu.make_async_copy(joint_own.at[0, :, pl.ds(0, width)], (kv_w, q_w)[i], sems.at[i]).wait()
    back = dense_nt(dkv[...], kv_w[...])
    dn[...] = back.astype(bf16)
    back_q = dense_nt(dq[...], q_w[...])
    dnq_ref[...] = back_q
    gain_grad = jnp.sum(back * normed_ref[...].astype(f32), axis=0, keepdims=True)
    gain_grad = gain_grad + jnp.sum(back_q * own[...].astype(f32), axis=0, keepdims=True)
    gain_grad_ref[...] = gain_grad / small_of(small_own, small_got, which)(GAIN_A, 1)
    blk = own.shape[0] // 2
    last = dn.shape[0] // blk - 1
    for i in range(dn_kept.shape[0] // blk):
        for out, side in ((dn_kept, section), (dn_sent, 1 - section)):
            core = (i // 2) * 2 + side
            at = core if i % 2 == 0 else last - core
            out[i * blk : (i + 1) * blk, :] = dn[pl.ds(pl.multiple_of(at * blk, blk), blk), :]


def join(seat, layer, token, arrays, joints, smalls, count, rows):
    seq, width = arrays[0].shape
    own_count = arrays[3].shape[0]
    size_a = 2 * width // 3
    size_b = width - size_a + width // 2
    shape = jax.ShapeDtypeStruct
    a_shape, b_shape = (shape((count // 2, rows, size), bf16) for size in (size_a, size_b))
    half_rows = shape((seq // 2, width), bf16)
    return one_step(
        functools.partial(join_kernel, layer=layer),
        in_specs=[SMEM_SPEC] * 2
        + [VMEM_SPEC] * 2
        + [FAR_SPEC] * 3
        + [VMEM_SPEC] * 2
        + [HBM_SPEC] * 2
        + [VMEM_SPEC] * 2,
        out_specs=[VMEM_SPEC] * 8 + [SMEM_SPEC],
        out_shape=[half_rows, half_rows, shape((own_count, width), f32)]
        + [a_shape, a_shape, b_shape, b_shape, shape((1, width), f32), TOKEN],
        scratch_shapes=[
            pltpu.VMEM((width, width), bf16),
            pltpu.VMEM((width, width), bf16),
            pltpu.VMEM((seq, width), bf16),
            pltpu.VMEM((seq, width), bf16),
            pltpu.VMEM((count, rows, size_a), bf16),
            pltpu.VMEM((count, rows, size_b), bf16),
            pltpu.SemaphoreType.DMA((2,)),
        ],
        compiler_params=pltpu.CompilerParams(vmem_limit_bytes=SMALL_VMEM),
    )(seat, token, *arrays, *joints, *smalls)


class Summer:
    def __init__(self, blocks, backwards):
        self.dp_count, ctx_count = blocks[0].shape[:2]
        bits = [1 << i for i in range(ctx_count.bit_length() - 1)]
        self.left = bits[::-1]
        self.order = bits[::-1] if backwards else bits
        self.parts = [x.reshape((self.dp_count,) + (2,) * len(bits) + x.shape[2:]) for x in blocks]

    def send(self, token=0):
        bit, self.order = self.order[0], self.order[1:]
        self.axis = 1 + self.left.index(bit)
        self.left = [b for b in self.left if b != bit]
        self.mine = (lax.axis_index("ctx") // bit) % 2
        at = 1 - self.mine + token
        sent = [lax.dynamic_index_in_dim(x, at, self.axis, keepdims=False) for x in self.parts]
        sent = sent[0] if len(sent) == 1 else jnp.concatenate(sent, axis=-1)
        self.got = xor_permute(sent, "ctx", bit)
        return [sent]

    def add(self, token):
        at, parts = 0, []
        for x in self.parts:
            kept = lax.dynamic_index_in_dim(x, self.mine + token, self.axis, keepdims=False)
            got = self.got[..., at : at + x.shape[-1]]
            at += x.shape[-1]
            parts.append((kept.astype(f32) + got.astype(f32)).astype(bf16))
        self.parts = parts

    def rest(self, token):
        self.add(token)
        while self.order:
            self.send()
            self.add(0)


class LastSum:
    def __init__(self, summers, rows):
        pieces = []
        for x in [x for one in summers for x in one.parts]:
            pieces += [x[:, i : i + rows] for i in range(0, x.shape[1], rows)]
        self.part = jnp.concatenate(pieces, axis=-1)

    def send(self):
        dp = lax.axis_index("dp")
        sent = [
            lax.dynamic_index_in_dim(self.part, dp ^ by, 0, keepdims=False)
            for by in range(1, self.part.shape[0])
        ]
        self.got = [xor_permute(x, "dp", by) for by, x in enumerate(sent, 1)]
        return sent

    @property
    def total(self):
        return lax.dynamic_index_in_dim(self.part, lax.axis_index("dp"), 0, keepdims=False).astype(f32)


def all_sum(x, tokens):
    steps = [(axis, 1 << i) for axis in ("ctx", "dp") for i in range(lax.axis_size(axis).bit_length() - 1)]
    for i, (axis, bit) in enumerate(steps):
        got = xor_permute(x, axis, bit)
        x = x + tokens[min(i, len(tokens) - 1)].astype(f32) + got
    return x


def local(
    inputs, lengths, cotangent, first_gain, joint_weight, pre_mix, post_mix,
    mixer_weight, second_gain, up_weight, down_weight,
):
    s = lax.axis_index("section")
    ctx = lax.axis_index("ctx")
    n = lax.axis_size("ctx")
    dp_count = lax.axis_size("dp")
    chips = n // 2
    micro_count, row_count, local_len, width = inputs.shape
    ff = up_weight.shape[2]
    seq = local_len * n
    blk = local_len // 2
    m = ctx // chips
    xi = ctx % chips
    core = xi * 2 + s
    zero = jnp.zeros((), jnp.int32)
    inputs = inputs.reshape(micro_count, 2, blk, width)
    cotangent = cotangent.reshape(micro_count, 2, blk, width)
    pick = lambda arr, i: lax.dynamic_index_in_dim(arr, i, 0, keepdims=False)

    spread = lambda mix: jnp.dot(mix, jnp.repeat(jnp.eye(HEADS, dtype=f32), HEAD, axis=1), precision=lax.Precision.HIGHEST)
    lines = lambda x, size: jnp.pad(x, ((0, size - x.shape[0]), (0, 0)))
    gains = jnp.concatenate([first_gain, second_gain]).astype(f32)
    small_own = jnp.concatenate(
        [lines(gains, PRE), lines(0.125 * spread(pre_mix[0].T), POST - PRE), lines(spread(post_mix[0]), SMALL_ROWS - POST)]
    )
    smalls = (small_own, swap_section(small_own))
    joints, mixers, ups, downs = (
        (w, swap_section(w)) for w in (joint_weight, mixer_weight, up_weight, down_weight)
    )

    mine = pick(inputs, m)
    pieces = []
    for d in range(1, n):
        target = m ^ (1 if d >= chips else 0)
        pieces.append(xor_permute(pick(pick(inputs, target), s), "ctx", d))
    other_pieces = [swap_section(jnp.concatenate(pieces))]
    chip_of = [ctx ^ d for d in range(1, n)]
    blocks0 = [2 * ctx, 2 * ctx + 1] + [2 * c + s for c in chip_of] + [2 * c + 1 - s for c in chip_of]
    pieces0 = [mine.reshape(2 * blk, width)] + pieces + other_pieces

    length = pick(lengths.reshape(-1), m)
    low_start = core * blk
    high_start = (2 * n - 1 - core) * blk
    bk = min(256, seq)
    cores1 = [(xi ^ d) * 2 + side for side in (s, 1 - s) for d in range(chips)]
    blocks1 = [b for c in cores1 for b in (c, 2 * n - 1 - c)]
    info = [s, ctx, lax.axis_index("dp"), length, low_start, high_start, s != 0, s != 1, *blocks0, *blocks1]
    info = jnp.stack([jnp.asarray(x, jnp.int32) for x in info])

    def gather_row(x):
        got = [x] + [xor_permute(x, "ctx", d) for d in range(1, chips)]
        return got + [swap_section(y) for y in got]

    def forward(layer, pieces, meanwhile):
        attended, q, normed_own, x_own, token, normed_all, k, v, u, lse = attend(
            info, layer, pieces, 2 * blk, smalls, joints, bk
        )
        weights = [x for pair in (mixers, ups, downs) for x in pair]
        out, hidden, normed_two, upward, active, token = feed(
            info, layer, x_own, attended, smalls, weights, ff, meanwhile
        )
        rows = [(x, swap_section(x)) for x in (active, normed_two, attended, normed_own)]
        return out, (x_own, q, k, v, u, lse, hidden, upward, rows, normed_all)

    def half(x, which):
        return lax.dynamic_slice_in_dim(x, which * (x.shape[1] // 2), x.shape[1] // 2, 1)

    def product(left, right):
        return (dense_tn(left[0], right[0]) + dense_tn(left[1], right[1])).astype(bf16)

    def blocks_of(grad):
        return grad.reshape(dp_count, n, grad.shape[0] // (dp_count * n), grad.shape[1])

    shard = width // (dp_count * n)

    fast = n == 4 and dp_count == 4 and shard % 16 == 0
    count = dp_count * n

    class Slow:
        def first(rows, keep, other):
            active, two, att, _ = rows
            cut, end = ff // 2, (ff + width) // 2
            of = lambda *cols: (keep[:, slice(*cols)], other[:, slice(*cols)])
            down_sum = Summer([blocks_of(product(active, of(end, None)))], False)
            up_sum = Summer([blocks_of(product(two, of(0, cut))), blocks_of(product(att, of(cut, end)))], True)
            return down_sum, up_sum, token_after(*down_sum.send(), *up_sum.send()).reshape(1)

        def second(token, sums, passing=(), closing=(), behind=()):
            for one in sums:
                one.add(token[0])
            return token, passing, total_of(closing[0], closing[1:]) if closing else None

        def last(token, sums, passing=()):
            for one in sums:
                one.rest(token[0])
            one = LastSum(sums, shard)
            one.send()
            one.parts = (one.total, *one.got)
            return one, token, passing

        def halved(token, sums, passing=(), closing=()):
            return *Slow.last(token, sums, passing), total_of(closing[0], closing[1:]) if closing else None

        def middle(token, one, passing=()):
            return token, passing

    class Fast:
        def first(rows, keep, other):
            return products(info, (*rows[0], *rows[1], *rows[2], keep, other), count, shard)

        def second(token, sums, passing=(), closing=(), behind=()):
            return second_step(info, token, sums, passing, closing, behind, VMEM_SPEC if behind else FAR_SPEC)

        def last(token, sums, passing=()):
            part, gots, token, passing = last_step(info, token, sums, shard, passing)
            one = types.SimpleNamespace(parts=(part, *gots))
            return one, token, passing

        def halved(token, sums, passing=(), closing=()):
            return halved_step(info, token, sums, shard, passing, closing, VMEM_SPEC if closing else FAR_SPEC)

        def middle(token, one, passing=()):
            return middle_step(info, token, one, passing, FAR_SPEC if passing else VMEM_SPEC)

    steps = Fast if fast else Slow

    def backward(layer, dy, kept, earlier):
        x_own, q, k, v, u, lse, hidden, upward, rows, normed_all = kept
        rows_normed = rows[3]
        here = s == layer
        gain_a = jnp.where(here, smalls[0][GAIN_A], smalls[1][GAIN_A])
        earlier[0]()
        weights = [x for pair in (mixers, ups, downs) for x in pair]
        keep, send, dhidden, datt, gain_b_grad, token = feed_back(
            info, layer, dy, upward, hidden, smalls, weights, ()
        )
        token, (send,) = earlier[1](token, (send,))
        down_sum, up_sum, first_token = steps.first(rows, keep, swap_section(send))
        dq, dkv_keep, dkv_send, pre_rows, post_rows, token = attend_back(
            info, layer, q, datt, u, lse, k, v, smalls, bk, (token, first_token)
        )
        token, (dkv_send, dq) = earlier[2](token, (down_sum, up_sum), (dkv_send, dq))
        got, dq_other = swap_section(dkv_send), swap_section(dq)
        if fast:
            dn_kept, dn_sent, dnq, a_kept, a_sent, b_kept, b_sent, gain_a_grad, token = join(
                info, layer, token, (dkv_keep, got, normed_all, *rows_normed, dq, dq_other), joints, smalls, count, shard
            )
            kv_sum, q_sum = FastSum(a_kept, a_sent, (1, 2)), FastSum(b_kept, b_sent, (2, 1))
            dn_kept, dn_sent = (x.reshape(chips, 2, blk, width) for x in (dn_kept, dn_sent))
        else:
            joint_w = jnp.where(here, joints[0][0], joints[1][0])
            kv_w = lax.dynamic_slice_in_dim(joint_w, width * (1 + s), width, 1)
            dkv = (dkv_keep.astype(f32) + got.astype(f32)).astype(bf16)
            dn = dense_nt(dkv, kv_w)
            gain_a_grad = jnp.sum(dn * normed_all.astype(f32), axis=0)
            dn = dn.astype(bf16).reshape(2 * n, blk, width)
            dn = jnp.stack([dn[i if h == 0 else 2 * n - 1 - i] for i in range(n) for h in range(2)])
            dn = dn.reshape(chips, 2, 2, blk, width)
            dn_kept = lax.dynamic_index_in_dim(dn, s, 1, keepdims=False)
            dn_sent = lax.dynamic_index_in_dim(dn, 1 - s, 1, keepdims=False)
            dnq = dense_nt(dq, joint_w[:, :width])
            gain_a_grad = (gain_a_grad + jnp.sum(dnq * rows_normed[0].astype(f32), axis=0)) / gain_a
            kv_part = blocks_of(dense_tn(normed_all, dkv).astype(bf16))
            q_part = blocks_of(product(rows_normed, (half(dq, s), half(dq_other, s))))
            cut = 2 * width // 3
            kv_sum = Summer([kv_part[..., :cut]], False)
            q_sum = Summer([kv_part[..., cut:], q_part], True)
            kv_sum.send()
            q_sum.send()
        token, (dn_sent,) = earlier[3](token, (dn_sent,), (down_sum, up_sum))
        low = (dn_kept.astype(f32) + swap_section(dn_sent).astype(f32)).astype(bf16)
        gots = [xor_permute(pick(low, xi ^ d), "ctx", d) for d in range(1, chips)]
        sums = (down_sum, up_sum, kv_sum, q_sum)
        token = earlier[4](token, low, sums)
        scattered = pick(low, xi + token[0]).astype(f32)
        for x in gots:
            scattered = scattered + x.astype(f32)
        scaled = (scattered.reshape(2 * blk, width) + dnq) * gain_a
        values = x_own.astype(f32)
        inverse = rms_inverse(values)
        unit = values * inverse
        dfront = inverse * (scaled - unit * jnp.mean(scaled * unit, axis=-1, keepdims=True))
        small = jnp.concatenate([gain_a_grad.reshape(1, -1), gain_b_grad.reshape(1, -1), pre_rows, post_rows])
        return dhidden + dfront, sums, small, token

    low_chip = ctx < chips
    there = [(i, chips + i) for i in range(chips)] + [(n - 1 - i, i) for i in range(chips)]
    here = [(n - 1 - i, chips + i) for i in range(chips)] + [(i, i) for i in range(chips)]
    first = jnp.where(low_chip, s, 1 - s)
    halves = lax.dynamic_index_in_dim(cotangent, first, 1, keepdims=False)
    ones, twos = jnp.where(low_chip, halves[1], halves[0]), jnp.where(low_chip, halves[0], halves[1])
    one, two = lax.ppermute(ones, "ctx", there), lax.ppermute(twos, "ctx", here)
    dy1 = jnp.concatenate([jnp.where(m == 0, two, one), jnp.where(m == 0, one, two)])
    x1, kept0 = forward(0, pieces0, (one, two))
    y, kept1 = forward(1, gather_row(x1), ())

    def send_home(x):
        x = x.reshape(2, blk, width)
        one = lax.ppermute(jnp.where(m == 0, x[1], x[0]), "ctx", [(b, a) for a, b in there])
        two = lax.ppermute(jnp.where(m == 0, x[0], x[1]), "ctx", [(b, a) for a, b in here])
        return one, two

    def at_home(one, two):
        return jnp.where(low_chip, jnp.stack([two, one]), jnp.stack([one, two]))

    def start(sums):
        for one in sums:
            one.start() if fast else one.send()

    def no_step():
        return None

    state = {}

    def after_attention(token, sums, passing):
        token, passing, _ = steps.second(token, sums, passing)
        start(sums)
        return token, passing

    def after_join(token, passing, sums):
        state["big"], token, passing, _ = steps.halved(token, sums, passing)
        return token, passing

    def after_low(token, low, sums):
        token, _, _ = steps.second(token, sums[2:], behind=(low,))
        start(sums[2:])
        return token

    first_steps = (no_step, lambda token, passing: (token, passing), after_attention, after_join, after_low)
    dx1, (_, _, kv1, q1), small1, _ = backward(1, dy1, kept1, first_steps)
    dy0 = dx1.astype(bf16)
    y_sent = send_home(y)

    def after_feed(token, passing):
        state["joint1"], token, passing, _ = steps.halved(token, [kv1, q1], (*passing, *y_sent))
        token, (passing, *state["y"]) = steps.middle(token, state["big"], passing)
        return token, (passing,)

    def after_attention(token, sums, passing):
        token, passing, state["big1"] = steps.second(token, sums, passing, state["big"].parts)
        start(sums)
        token, passing = steps.middle(token, state["joint1"], passing)
        return token, passing

    def after_join(token, passing, sums):
        state["big0"], token, passing, state["joint1"] = steps.halved(token, sums, passing, state["joint1"].parts)
        state["token"] = token
        return token, passing

    def after_low(token, low, sums):
        token, _, _ = steps.second(token, sums[2:], behind=(low,))
        start(sums[2:])
        return steps.middle(token, state["big0"])[0]

    dx0, (down0, up0, kv0, q0), small0, token = backward(
        0, dy0, kept0, (no_step, after_feed, after_attention, after_join, after_low)
    )
    early = token
    dx0 = dx0.astype(bf16)
    dx_home = at_home(*send_home(dx0))
    y_home = at_home(*state["y"])

    small_got = swap_section(jnp.where(s == 0, small1, small0))
    small = jnp.where(s == 0, small0, small1) + small_got
    joint0, last_token, _ = steps.last(token, [kv0, q0], (dx0,))
    small = all_sum(small, (state["token"][0], early[0], token[0], last_token[0]))

    got = swap_section(jnp.where(s == 0, y_home, dx_home))
    held = jnp.where(s == 0, dx_home, y_home)
    is_first = jnp.where(low_chip, s, 1 - s) == 0
    ends = jnp.stack([jnp.where(is_first, held, got), jnp.where(is_first, got, held)], axis=1)
    ends = ends.reshape(1, micro_count, row_count, local_len, width)

    at = (lax.axis_index("dp") * n + ctx) * shard
    gain_a_out, gain_b_out = (lax.dynamic_slice_in_dim(small[i], at, shard, 0) for i in range(2))
    half_d, half_ff, times = width // 2, ff // 2, ff // width
    if fast:
        groups = (state["big0"].parts, joint0.parts, (state["big1"],), (state["joint1"],))
        keep, send = final_parts(info, groups)
        behind = keep
        joint_out, mixer_out, up_out, down_out = final_outs(info, keep, swap_section(send), width, ff)
    else:
        behind = small
        big0, joint0 = (total_of(x.parts[0], x.parts[1:]) for x in (state["big0"], joint0))
        pairs = ((big0, state["big1"]), (joint0, state["joint1"]))
        outs = []
        for at_zero, at_one in pairs:
            other = swap_section(jnp.where(s == 0, at_one, at_zero))
            own = jnp.where(s == 0, at_zero, at_one)
            outs.append((jnp.where(s == 0, own, other), jnp.where(s == 0, other, own)))
        (big_a, big_b), (joint_a, joint_b) = outs
        side = lambda *cuts: jnp.concatenate([x[:, at : at + size] for x, at, size in cuts], axis=1)
        down_out = jnp.concatenate(
            [side((big_a, i * half_d, half_d), (big_b, i * half_d, half_d)) for i in range(times)]
        )
        at = times * half_d
        up_out = side((big_a, at, half_ff), (big_b, at, half_ff))
        mixer_out = side((big_a, at + half_ff, half_d), (big_b, at + half_ff, half_d))
        joint_out = side((joint_a, width, half_d), (joint_b, width, half_d), (joint_a, 0, width), (joint_b, 0, width))
    pre_out, post_out = (x.transpose(1, 0, 2) for x in mix_grads(small, behind))
    return (
        ends,
        gain_a_out[None],
        joint_out[None],
        pre_out,
        post_out,
        mixer_out[None],
        gain_b_out[None],
        up_out[None],
        down_out[None],
    )


def solution(mesh):
    in_specs = (
        P(None, "dp", "ctx", None),
        P(None, "dp"),
        P(None, "dp", "ctx", None),
        P("section", None),
        P("section", None, None),
        P("section", None, None),
        P("section", None, None),
        P("section", None, None),
        P("section", None),
        P("section", None, None),
        P("section", None, None),
    )
    out_specs = (
        P("section", None, "dp", "ctx", None),
        P("section", ("dp", "ctx")),
        P("section", ("dp", "ctx"), None),
        P("section", None, None),
        P("section", None, None),
        P("section", ("dp", "ctx"), None),
        P("section", ("dp", "ctx")),
        P("section", ("dp", "ctx"), None),
        P("section", ("dp", "ctx"), None),
    )
    return jax.shard_map(local, mesh=mesh, in_specs=in_specs, out_specs=out_specs, check_vma=False)
```

```python
import functools
import math
import types

import jax
import jax.numpy as jnp
from jax import lax
from jax.experimental import pallas as pl
from jax.experimental.pallas import tpu as pltpu
from jax.sharding import PartitionSpec as P

HEADS = 12
HEAD = 64
eps = 1e-06
MASKED = -1e30
f32 = jnp.float32
bf16 = jnp.bfloat16
MIB = 1024 * 1024
SMALL_VMEM = 36 * MIB
BIG_VMEM = 60 * MIB


def dense(left_side, right_side):
    return jnp.dot(left_side, right_side, preferred_element_type=f32)


def dense_tn(left_side, right_side):
    return lax.dot_general(
        left_side, right_side, (((0,), (0,)), ((), ())), preferred_element_type=f32
    )


def dense_nt(left_side, right_side):
    return lax.dot_general(
        left_side, right_side, (((1,), (1,)), ((), ())), preferred_element_type=f32
    )


GAIN_A, GAIN_B, PRE, POST = 0, 1, 8, 24
SECTION, CTX, DP, LENGTH, STARTS, WHICH, BLOCKS = 0, 1, 2, 3, 4, 6, 8
SMALL_ROWS = 40


def small_of(own, got, which):
    return lambda at, size: jnp.where(which == 0, own[at : at + size, :], got[at : at + size, :])


def rms_inverse(values):
    return lax.rsqrt(jnp.mean(values * values, axis=-1, keepdims=True) + eps)


def lane_parts(x):
    return [x[:, i : i + 128] for i in range(0, x.shape[1], 128)]


def bias_of(q_start, k_start, length, bq, bk):
    rows = q_start + lax.broadcasted_iota(jnp.int32, (bq, bk), 0)
    cols = k_start + lax.broadcasted_iota(jnp.int32, (bq, bk), 1)
    return jnp.where((cols <= rows) & (cols < length), 0.0, MASKED).astype(f32)


def attend_kernel(info, small_own, small_got, joint_own, joint_got, *rest, bk, count_in, layer):
    (
        att_ref, q_ref, own_ref, x_ref, token_ref, normed_hbm, k_hbm, v_hbm, u_hbm, lse_hbm,
        joint, raw, normed, k, v, u, lse, qp, logit, total, top, norm, sems,
    ) = rest[count_in:]
    token_ref[0] = 0
    length, which = info[LENGTH], info[WHICH + layer]
    fetch((joint_own, joint_got), which, joint, sems.at[0])
    seq, width = normed.shape
    count = att_ref.shape[0]
    bq = count // 2
    small = small_of(small_own, small_got, which)
    gain, pre, post = small(GAIN_A, 1), small(PRE, HEADS), small(POST, HEADS)
    at = BLOCKS + layer * (seq // bq)
    for piece in rest[:count_in]:
        for j in range(piece.shape[0] // bq):
            x = piece[j * bq : (j + 1) * bq, :]
            span = pl.ds(pl.multiple_of(info[at] * bq, bq), bq)
            raw[span, :] = x
            x = x.astype(f32)
            normed[span, :] = (x * rms_inverse(x) * gain).astype(bf16)
            at += 1
    for i in range(2):
        span = pl.ds(pl.multiple_of(info[STARTS + i], bq), bq)
        own_ref[i * bq : (i + 1) * bq, :] = normed[span, :]
        x_ref[i * bq : (i + 1) * bq, :] = raw[span, :]
    fetched((joint_own, joint_got), joint, sems.at[0])
    cut = width // 3
    for i in range(3):
        cols = slice(width + i * cut, width + (i + 1) * cut)
        k[:, i * cut : (i + 1) * cut] = dense(normed[...], joint[:, cols]).astype(bf16)
    for i in range(3):
        cols = slice(2 * width + i * cut, 2 * width + (i + 1) * cut)
        v[:, i * cut : (i + 1) * cut] = dense(normed[...], joint[:, cols]).astype(bf16)
    q_ref[...] = dense(own_ref[...], joint[:, :width]).astype(bf16)
    outs = [
        pltpu.make_async_copy(a, b, sems.at[1 + i])
        for i, (a, b) in enumerate(((normed, normed_hbm), (k, k_hbm), (v, v_hbm)))
    ]
    for out in outs:
        out.start()

    def rows_step(step, carry):
        q_start = info[STARTS + step]
        mine = pl.ds(pl.multiple_of(step * bq, bq), bq)
        q32 = q_ref[mine, :].astype(f32)
        for h in range(HEADS):
            qp[h * bq : (h + 1) * bq, :] = (q32 * pre[h : h + 1, :]).astype(bf16)
        blocks = (jnp.minimum(q_start + bq, length) + bk - 1) // bk
        top[...] = jnp.full_like(top, MASKED)
        total[...] = jnp.zeros_like(total)
        norm[...] = jnp.zeros_like(norm)

        def score(kb, c):
            bias = bias_of(q_start, kb * bk, length, bq, bk)
            tile = dense_nt(qp[...], k[pl.ds(pl.multiple_of(kb * bk, bk), bk), :])
            tile = (tile.reshape(HEADS, bq, bk) + bias[None]).reshape(HEADS * bq, bk)
            logit[kb] = tile
            top[...] = functools.reduce(jnp.maximum, lane_parts(tile), top[...])
            return c

        lax.fori_loop(0, blocks, score, 0)
        highest = jnp.max(top[...], axis=-1, keepdims=True)
        top[...] = jnp.broadcast_to(highest, top.shape)

        def apply(kb, c):
            high = top[...]
            parts = [jnp.exp(x - high) for x in lane_parts(logit[kb])]
            norm[...] = functools.reduce(jnp.add, parts, norm[...])
            e = jnp.concatenate([x.astype(bf16) for x in parts], axis=1)
            total[...] += dense(e, v[pl.ds(pl.multiple_of(kb * bk, bk), bk), :])
            return c

        lax.fori_loop(0, blocks, apply, 0)
        sums = jnp.sum(norm[...], axis=-1, keepdims=True)
        scale = 1.0 / sums
        rows = pl.ds(pl.multiple_of(step * HEADS * bq, HEADS * bq), HEADS * bq)
        lse[rows, :] = jnp.broadcast_to(highest + jnp.log(sums), top.shape)
        att = jnp.zeros((bq, width), f32)
        for g in range(HEADS):
            part = total[g * bq : (g + 1) * bq, :] * scale[g * bq : (g + 1) * bq]
            u[pl.ds(pl.multiple_of(step * HEADS * bq + g * bq, bq), bq), :] = part.astype(bf16)
            att = att + part * post[g : g + 1, :]
        att_ref[mine, :] = att.astype(bf16)
        return carry

    lax.fori_loop(0, 2, rows_step, 0)
    outs += [pltpu.make_async_copy(u, u_hbm, sems.at[4]), pltpu.make_async_copy(lse, lse_hbm, sems.at[5])]
    for out in outs[3:]:
        out.start()
    for out in outs:
        out.wait()


VMEM_SPEC = pl.BlockSpec(memory_space=pltpu.VMEM)
FAR_SPEC = pl.BlockSpec(memory_space=pltpu.VMEM)
ANY_SPEC = pl.BlockSpec(memory_space=pl.ANY)
HBM_SPEC = pl.BlockSpec(memory_space=pltpu.HBM)
SMEM_SPEC = pl.BlockSpec(memory_space=pltpu.SMEM)
TOKEN = jax.ShapeDtypeStruct((1,), jnp.int32)

LARGE = 64 * 1024
SMALL_COST = pl.CostEstimate(flops=0, bytes_accessed=0, transcendentals=0)


def in_hbm(spec, x):
    return (spec is FAR_SPEC or spec is HBM_SPEC) and math.prod(x.shape) >= LARGE


def from_hbm(spec, x):
    return pltpu.with_memory_space_constraint(x, pltpu.HBM) if in_hbm(spec, x) else x


def result_in_hbm(spec, x):
    return pltpu.HBM(x.shape, x.dtype) if in_hbm(spec, x) else x


def one_step(kernel, *, in_specs, out_specs, out_shape, **rest):
    def whole(spec, x):
        if spec is not VMEM_SPEC and spec is not FAR_SPEC:
            return spec
        zeros = (0,) * len(x.shape)
        return pl.BlockSpec(x.shape, lambda i: zeros, pipeline_mode=pl.Buffered(1))

    def run(*args):
        return pl.pallas_call(
            kernel,
            cost_estimate=SMALL_COST,
            grid=(1,),
            in_specs=[whole(*x) for x in zip(in_specs, args, strict=True)],
            out_specs=[whole(*x) for x in zip(out_specs, out_shape, strict=True)],
            out_shape=[result_in_hbm(*x) for x in zip(out_specs, out_shape)],
            **rest,
        )(*[from_hbm(*x) for x in zip(in_specs, args)])

    return run


def attend(info, layer, pieces, count, smalls, joints, bk):
    width = pieces[0].shape[1]
    seq = sum(x.shape[0] for x in pieces)
    bq = count // 2
    shape = jax.ShapeDtypeStruct
    return one_step(
        functools.partial(attend_kernel, bk=bk, count_in=len(pieces), layer=layer),
        in_specs=[SMEM_SPEC] + [VMEM_SPEC] * 2 + [HBM_SPEC] * 2 + [VMEM_SPEC] * len(pieces),
        out_specs=[VMEM_SPEC, FAR_SPEC, FAR_SPEC, VMEM_SPEC, SMEM_SPEC] + [HBM_SPEC] * 5,
        out_shape=[shape((count, width), bf16)] * 4
        + [TOKEN]
        + [shape((seq, width), bf16)] * 3
        + [shape((HEADS * count, width), bf16), shape((HEADS * count, 128), f32)],
        scratch_shapes=[
            pltpu.VMEM((width, 3 * width), bf16),
            pltpu.VMEM((seq, width), bf16),
            pltpu.VMEM((seq, width), bf16),
            pltpu.VMEM((seq, width), bf16),
            pltpu.VMEM((seq, width), bf16),
            pltpu.VMEM((HEADS * count, width), bf16),
            pltpu.VMEM((HEADS * count, 128), f32),
            pltpu.VMEM((HEADS * bq, width), bf16),
            pltpu.VMEM((seq // bk, HEADS * bq, bk), f32),
            pltpu.VMEM((HEADS * bq, width), f32),
            pltpu.VMEM((HEADS * bq, 128), f32),
            pltpu.VMEM((HEADS * bq, 128), f32),
            pltpu.SemaphoreType.DMA((6,)),
        ],
        compiler_params=pltpu.CompilerParams(vmem_limit_bytes=BIG_VMEM),
    )(info, *smalls, *joints, *pieces)


def feed_kernel(
    info, x_ref, att_ref, small_own, small_got,
    mixer_own, mixer_got, up_own, up_got, down_own, down_got, *rest, tile, extra, layer,
):
    (
        out_ref, hidden_ref, two_ref, upward_hbm, active_hbm, token_ref,
        mixer, up, down, upward, active, sems,
    ) = rest[extra:]
    token_ref[0] = 0
    which = info[WHICH + layer]
    pairs = ((mixer_own, mixer_got), (up_own, up_got), (down_own, down_got))
    fetch(pairs[0], which, mixer, sems.at[0])
    tiles = down.shape[0] // tile
    for j in range(tiles):
        fetch(pairs[1], which, up, sems.at[1 + j], column_part(j, tile))
        fetch(pairs[2], which, down, sems.at[1 + tiles + j], row_part(j, tile))
    gain = small_of(small_own, small_got, which)(GAIN_B, 1)
    fetched(pairs[0], mixer, sems.at[0])
    hidden = x_ref[...].astype(f32) + dense(att_ref[...], mixer[...])
    hidden_ref[...] = hidden
    two = (hidden * rms_inverse(hidden) * gain).astype(bf16)
    two_ref[...] = two
    result, outs = hidden, []
    for j in range(tiles):
        span = slice(j * tile, (j + 1) * tile)
        fetched(pairs[1], up, sems.at[1 + j], column_part(j, tile))
        u = dense(two, up[:, span])
        upward[:, span] = u
        act = (0.5 * u * (1.0 + jnp.tanh(0.7978845608 * (u + 0.044715 * (u * u * u))))).astype(bf16)
        active[:, span] = act
        part = column_part(j, tile)
        for i, (x, y) in enumerate(((upward, upward_hbm), (active, active_hbm))):
            outs.append(pltpu.make_async_copy(x.at[part], y.at[part], sems.at[1 + (2 + i) * tiles + j]))
            outs[-1].start()
        fetched(pairs[2], down, sems.at[1 + tiles + j], row_part(j, tile))
        result = result + dense(act, down[span, :])
    out_ref[...] = result.astype(bf16)
    for out in outs:
        out.wait()


def feed(info, layer, x, attended, smalls, weights, ff, extras):
    count, width = x.shape
    shape = jax.ShapeDtypeStruct
    return one_step(
        functools.partial(feed_kernel, tile=width, extra=len(extras), layer=layer),
        in_specs=[SMEM_SPEC] + [VMEM_SPEC] * 4 + [HBM_SPEC] * (6 + len(extras)),
        out_specs=[VMEM_SPEC, FAR_SPEC, FAR_SPEC] + [HBM_SPEC] * 2 + [SMEM_SPEC],
        out_shape=[
            shape((count, width), bf16),
            shape((count, width), f32),
            shape((count, width), bf16),
            shape((count, ff), f32),
            shape((count, ff), bf16),
            TOKEN,
        ],
        scratch_shapes=[
            pltpu.VMEM((width, width), bf16),
            pltpu.VMEM((width, ff), bf16),
            pltpu.VMEM((ff, width), bf16),
            pltpu.VMEM((count, ff), f32),
            pltpu.VMEM((count, ff), bf16),
            pltpu.SemaphoreType.DMA((1 + 4 * (ff // width),)),
        ],
        compiler_params=pltpu.CompilerParams(vmem_limit_bytes=SMALL_VMEM),
    )(info, x, attended, *smalls, *weights, *extras)


def fetch(pair, which, buffer, semaphore, at=()):
    for i, ref in enumerate(pair):

        @pl.when(which == i)
        def _(ref=ref):
            pltpu.make_async_copy(ref.at[(0, *at)], buffer.at[at] if at else buffer, semaphore).start()


def fetched(pair, buffer, semaphore, at=()):
    pltpu.make_async_copy(pair[0].at[(0, *at)], buffer.at[at] if at else buffer, semaphore).wait()


def row_part(i, size):
    return pl.ds(i * size, size), slice(None)


def column_part(i, size):
    return slice(None), pl.ds(i * size, size)


def gelu_slope(u):
    inner = 0.7978845608 * (u + 0.044715 * (u * u * u))
    t = jnp.tanh(inner)
    return 0.5 * (1.0 + t) + 0.5 * u * (1.0 - t * t) * (0.7978845608 + 0.1070322243 * (u * u))


def feed_back_kernel(
    info, dy_ref, upward_hbm, hidden_hbm, small_own, small_got,
    mixer_own, mixer_got, up_own, up_got, down_own, down_got, *rest, tile, extra, layer,
):
    (
        keep_ref, send_ref, dhidden_ref, datt_ref, gain_grad_ref, token_ref,
        mixer, up, down, upward_ref, hidden_ref, sems,
    ) = rest[extra:]
    token_ref[0] = 0
    which = info[WHICH + layer]
    width = dy_ref.shape[1]
    half_ff, half = down.shape[0] // 2, width // 2

    def put(value, number, at):
        for ref, equal in ((keep_ref, True), (send_ref, False)):

            @pl.when((info[SECTION] == number) == equal)
            def _(ref=ref):
                ref[:, at : at + value.shape[1]] = value

    pairs = ((down_own, down_got), (up_own, up_got), (mixer_own, mixer_got))
    tiles = down.shape[0] // tile
    for j in range(tiles):
        fetch(pairs[0], which, down, sems.at[j], row_part(j, tile))
        if j == 0:
            upward_copy = pltpu.make_async_copy(upward_hbm, upward_ref, sems.at[2 * tiles])
            upward_copy.start()
        fetch(pairs[1], which, up, sems.at[tiles + j], column_part(j, tile))
    hidden_copy = pltpu.make_async_copy(hidden_hbm, hidden_ref, sems.at[2 * tiles + 1])
    hidden_copy.start()
    fetch(pairs[2], which, mixer, sems.at[2 * tiles + 2])
    gain = small_of(small_own, small_got, which)(GAIN_B, 1)
    dy = dy_ref[...]
    grad = jnp.zeros(hidden_ref.shape, f32)
    for j in range(tiles):
        span = slice(j * tile, (j + 1) * tile)
        fetched(pairs[0], down, sems.at[j], row_part(j, tile))
        dactive = dense_nt(dy, down[span, :])
        if j == 0:
            upward_copy.wait()
        dup = (dactive * gelu_slope(upward_ref[:, span])).astype(bf16)
        put(dup, j * tile // half_ff, j * tile % half_ff)
        fetched(pairs[1], up, sems.at[tiles + j], column_part(j, tile))
        grad = grad + dense_nt(dup, up[:, span])
    hidden_copy.wait()
    hidden = hidden_ref[...]
    inverse = rms_inverse(hidden)
    unit = hidden * inverse
    gain_grad_ref[...] = jnp.sum(grad * unit, axis=0, keepdims=True)
    scaled = grad * gain
    dhidden = dy.astype(f32) + inverse * (scaled - unit * jnp.mean(scaled * unit, axis=-1, keepdims=True))
    dhidden_ref[...] = dhidden
    low = dhidden.astype(bf16)
    for i in range(2):
        put(low[:, i * half : (i + 1) * half], i, half_ff)
        put(dy[:, i * half : (i + 1) * half], i, half_ff + half)
    fetched(pairs[2], mixer, sems.at[2 * tiles + 2])
    datt_ref[...] = dense_nt(low, mixer[...]).astype(bf16)


def feed_back(info, layer, dy, upward, hidden, smalls, weights, extras):
    count, width = dy.shape
    ff = upward.shape[1]
    shape = jax.ShapeDtypeStruct
    return one_step(
        functools.partial(feed_back_kernel, tile=width, extra=len(extras), layer=layer),
        in_specs=[SMEM_SPEC, VMEM_SPEC, HBM_SPEC, HBM_SPEC, VMEM_SPEC, VMEM_SPEC] + [HBM_SPEC] * (6 + len(extras)),
        out_specs=[VMEM_SPEC, VMEM_SPEC, FAR_SPEC, VMEM_SPEC, VMEM_SPEC, SMEM_SPEC],
        out_shape=[
            shape((count, ff // 2 + width), bf16),
            shape((count, ff // 2 + width), bf16),
            shape((count, width), f32),
            shape((count, width), bf16),
            shape((1, width), f32),
            TOKEN,
        ],
        scratch_shapes=[
            pltpu.VMEM((width, width), bf16),
            pltpu.VMEM((width, ff), bf16),
            pltpu.VMEM((ff, width), bf16),
            pltpu.VMEM((count, ff), f32),
            pltpu.VMEM((count, width), f32),
            pltpu.SemaphoreType.DMA((2 * (ff // width) + 3,)),
        ],
        compiler_params=pltpu.CompilerParams(vmem_limit_bytes=SMALL_VMEM),
    )(info, dy, upward, hidden, *smalls, *weights, *extras)


def attend_back_kernel(
    info, q_ref, datt_ref, u_ref, lse_ref, k_hbm, v_hbm, small_own, small_got, *rest, bq, bk, extra, layer
):
    (
        dq_ref, keep_ref, send_ref, pre_grad_ref, post_grad_ref, token_ref,
        qp, dp, dk, dv, w, delta, k_ref, v_ref, sems,
    ) = rest[extra:]
    token_ref[0] = 0
    step = pl.program_id(0)
    copies = [pltpu.make_async_copy(x, y, sems.at[i]) for i, (x, y) in enumerate(((k_hbm, k_ref), (v_hbm, v_ref)))]

    @pl.when(step == 0)
    def _():
        for copy in copies:
            copy.start()

    length, which, q_start = info[LENGTH], info[WHICH + layer], info[STARTS + step]
    small = small_of(small_own, small_got, which)
    pre, post = small(PRE, HEADS), small(POST, HEADS)

    @pl.when(step == 0)
    def _():
        dk[...] = jnp.zeros_like(dk)
        dv[...] = jnp.zeros_like(dv)
        pre_grad_ref[...] = jnp.zeros_like(pre_grad_ref)
        post_grad_ref[...] = jnp.zeros_like(post_grad_ref)

    q32 = q_ref[...].astype(f32)
    datt = datt_ref[...].astype(f32)
    for h in range(HEADS):
        part = slice(h * bq, (h + 1) * bq)
        qp[part, :] = (q32 * pre[h : h + 1, :]).astype(bf16)
        scaled = datt * post[h : h + 1, :]
        dp[part, :] = scaled.astype(bf16)
        u = u_ref[part, :].astype(f32)
        delta[part, :] = jnp.broadcast_to(jnp.sum(scaled * u, axis=-1, keepdims=True), (bq, 128))
        post_grad_ref[h : h + 1, :] += jnp.sum(datt * u, axis=0, keepdims=True)
    w[...] = jnp.zeros_like(w)
    blocks = (jnp.minimum(q_start + bq, length) + bk - 1) // bk

    @pl.when(step == 0)
    def _():
        for copy in copies:
            copy.wait()

    def block(kb, c):
        span = pl.ds(pl.multiple_of(kb * bk, bk), bk)
        bias = bias_of(q_start, kb * bk, length, bq, bk)
        k_blk, v_blk = k_ref[span, :], v_ref[span, :]
        logits = dense_nt(qp[...], k_blk)
        logits = (logits.reshape(HEADS, bq, bk) + bias[None]).reshape(HEADS * bq, bk)
        grad = dense_nt(dp[...], v_blk)
        lse, spread = lse_ref[...], delta[...]
        attention, dlog = [], []
        for x, g in zip(lane_parts(logits), lane_parts(grad)):
            a = jnp.exp(x - lse)
            attention.append(a.astype(bf16))
            dlog.append((a * (g - spread)).astype(bf16))
        attention, dlog = jnp.concatenate(attention, axis=1), jnp.concatenate(dlog, axis=1)
        dv[span, :] += dense_tn(attention, dp[...])
        dk[span, :] += dense_tn(dlog, qp[...])
        w[...] += dense(dlog, k_blk)
        return c

    lax.fori_loop(0, blocks, block, 0)
    dq = jnp.zeros_like(q32)
    for h in range(HEADS):
        part = w[h * bq : (h + 1) * bq, :]
        dq = dq + part * pre[h : h + 1, :]
        pre_grad_ref[h : h + 1, :] += jnp.sum(part * q32, axis=0, keepdims=True)
    dq_ref[...] = dq.astype(bf16)

    for section, (kept, sent) in enumerate(((dk, dv), (dv, dk))):

        @pl.when((step == pl.num_programs(0) - 1) & (info[SECTION] == section))
        def _(kept=kept, sent=sent):
            keep_ref[...] = kept[...].astype(bf16)
            send_ref[...] = sent[...].astype(bf16)


def attend_back(info, layer, q, datt, u, lse, k, v, smalls, bk, extras):
    count, width = q.shape
    seq = k.shape[0]
    bq = count // 2
    full = lambda i, place: (0, 0)
    row = lambda i, place: (i, 0)
    shape = jax.ShapeDtypeStruct
    return pl.pallas_call(
        cost_estimate=SMALL_COST,
        kernel=functools.partial(attend_back_kernel, bq=bq, bk=bk, extra=len(extras), layer=layer),
        grid_spec=pltpu.PrefetchScalarGridSpec(
            num_scalar_prefetch=1,
            grid=(2,),
            in_specs=[
                pl.BlockSpec((bq, width), row),
                pl.BlockSpec((bq, width), row),
                pl.BlockSpec((HEADS * bq, width), row),
                pl.BlockSpec((HEADS * bq, 128), row),
                HBM_SPEC,
                HBM_SPEC,
                pl.BlockSpec((SMALL_ROWS, width), full),
                pl.BlockSpec((SMALL_ROWS, width), full),
            ]
            + [HBM_SPEC] * len(extras),
            out_specs=[
                pl.BlockSpec((bq, width), row),
                pl.BlockSpec((seq, width), full),
                pl.BlockSpec((seq, width), full),
                pl.BlockSpec((HEADS, width), full),
                pl.BlockSpec((HEADS, width), full),
                SMEM_SPEC,
            ],
            scratch_shapes=[
                pltpu.VMEM((HEADS * bq, width), bf16),
                pltpu.VMEM((HEADS * bq, width), bf16),
                pltpu.VMEM((seq, width), f32),
                pltpu.VMEM((seq, width), f32),
                pltpu.VMEM((HEADS * bq, width), f32),
                pltpu.VMEM((HEADS * bq, 128), f32),
                pltpu.VMEM((seq, width), bf16),
                pltpu.VMEM((seq, width), bf16),
                pltpu.SemaphoreType.DMA((2,)),
            ],
        ),
        out_shape=[
            shape((count, width), bf16),
            shape((seq, width), bf16),
            shape((seq, width), bf16),
            shape((HEADS, width), f32),
            shape((HEADS, width), f32),
            TOKEN,
        ],
        compiler_params=pltpu.CompilerParams(vmem_limit_bytes=BIG_VMEM),
    )(info, q, datt, u, lse, k, v, *smalls, *extras)


def swap_section(x):
    return lax.ppermute(x, "section", [(0, 1), (1, 0)])


def xor_permute(x, axis, by):
    return lax.ppermute(x, axis, [(i, i ^ by) for i in range(lax.axis_size(axis))])


def from_xor_order(x, index):
    places = range(x.shape[0])
    return jnp.concatenate([lax.dynamic_index_in_dim(x, index ^ i, 0) for i in places])


def token_kernel(*refs):
    refs[-1][0] = 0


def token_after(*arrays):
    arrays = [x if x.ndim == 1 else x[(0,) * (x.ndim - 2)][:16, :128] for x in arrays]
    return pl.pallas_call(
        token_kernel,
        cost_estimate=SMALL_COST,
        in_specs=[SMEM_SPEC if x.ndim == 1 else VMEM_SPEC for x in arrays],
        out_specs=SMEM_SPEC,
        out_shape=TOKEN,
    )(*arrays)[0]


def half_columns(ref, which, size):
    return ref[:, pl.ds(pl.multiple_of(which * size, size), size)]


def split_blocks(blocks, kept, sent, mine):
    for i in range(kept.shape[0]):
        kept[i] = blocks[2 * i + mine]
        sent[i] = blocks[2 * i + 1 - mine]


def split_blocks_first(blocks, kept, sent, mine):
    for i in range(kept.shape[0]):
        at = 4 * (i // 2) + i % 2
        kept[i] = blocks[at + 2 * mine]
        sent[i] = blocks[at + 2 * (1 - mine)]


def products_kernel(
    seat, active_hbm, active_other_hbm, two, two_other, att, att_other, right, right_other,
    down_kept, down_sent, up_kept, up_sent, token_ref, active, active_other, down_blocks, up_blocks, sems,
):
    token_ref[0] = 0
    copies = [
        pltpu.make_async_copy(x, y, sems.at[i])
        for i, (x, y) in enumerate(((active_hbm, active), (active_other_hbm, active_other)))
    ]
    for copy in copies:
        copy.start()
    width = att.shape[1]
    half, half_ff = width // 2, active.shape[1] // 2
    both = lambda left, left_other, cols: dense_tn(left, right[:, cols]) + dense_tn(left_other, right_other[:, cols])
    rows = up_blocks.shape[1]
    tile = half_ff // 2
    for j in range(2):
        cols = slice(j * tile, (j + 1) * tile)
        up_blocks[:, :, cols] = both(two[...], two_other[...], cols).astype(bf16).reshape(-1, rows, tile)
    cols = slice(half_ff, half_ff + half)
    up_blocks[:, :, cols] = both(att[...], att_other[...], cols).astype(bf16).reshape(-1, rows, half)
    split_blocks_first(up_blocks, up_kept, up_sent, seat[CTX] // 2)
    for copy in copies:
        copy.wait()
    rows = down_blocks.shape[1]
    each = width // rows
    for j in range(active.shape[1] // width):
        cols = slice(j * width, (j + 1) * width)
        grad = both(active[:, cols], active_other[:, cols], slice(half_ff + half, half_ff + width))
        down_blocks[j * each : (j + 1) * each] = grad.astype(bf16).reshape(each, rows, half)
    split_blocks(down_blocks, down_kept, down_sent, seat[CTX] % 2)


def products(seat, arrays, count, rows):
    ff, width = arrays[0].shape[1], arrays[4].shape[1]
    down, up = (ff // count, width // 2), (rows, (ff + width) // 2)
    shape = lambda x: jax.ShapeDtypeStruct((count // 2, *x), bf16)
    outs = one_step(
        products_kernel,
        in_specs=[SMEM_SPEC] + [HBM_SPEC] * 2 + [FAR_SPEC] * 4 + [VMEM_SPEC] * 2,
        out_specs=[FAR_SPEC] * 4 + [SMEM_SPEC],
        out_shape=[shape(down)] * 2 + [shape(up)] * 2 + [TOKEN],
        scratch_shapes=[
            pltpu.VMEM(arrays[0].shape, bf16),
            pltpu.VMEM(arrays[1].shape, bf16),
            pltpu.VMEM((count, *down), bf16),
            pltpu.VMEM((count, *up), bf16),
            pltpu.SemaphoreType.DMA((2,)),
        ],
        compiler_params=pltpu.CompilerParams(vmem_limit_bytes=SMALL_VMEM),
    )(seat, *arrays)
    return FastSum(*outs[:2], (1, 2)), FastSum(*outs[2:4], (2, 1)), outs[4]


def second_kernel(seat, token_in, *refs, bits, passing, closing, behind):
    count = len(bits)
    refs = refs[behind + passing :]
    parts, refs = refs[2 * count : 2 * count + closing], refs[: 2 * count] + refs[2 * count + closing :]
    refs[4 * count][0] = token_in[0]
    if closing:
        refs[4 * count + 1][...] = functools.reduce(jnp.add, [x[...].astype(f32) for x in parts])
    for i, bit in enumerate(bits):
        kept, got = refs[2 * i], refs[2 * i + 1]
        kept_out, sent_out = refs[2 * count + 2 * i], refs[2 * count + 2 * i + 1]
        mine = (seat[1] // bit) % 2
        for j in range(kept_out.shape[0]):
            for out, at in ((kept_out, 2 * j + mine), (sent_out, 2 * j + 1 - mine)):
                out[j] = (kept[at].astype(f32) + got[at].astype(f32)).astype(bf16)


def last_kernel(seat, token_in, *refs, count, rows, dp_count, passing):
    refs = refs[passing:]
    total, outs, token_ref = refs[2 * count], refs[2 * count + 1 : 2 * count + dp_count], refs[2 * count + dp_count]
    token_ref[0] = token_in[0]
    at = 0
    for i in range(count):
        kept, got = refs[2 * i], refs[2 * i + 1]
        size = kept.shape[2]
        for j in range(kept.shape[1] // rows):
            part = slice(j * rows, (j + 1) * rows)
            for by in range(len(outs) + 1):
                z = seat[2] ^ by
                value = kept[z, part, :].astype(f32) + got[z, part, :].astype(f32)
                if by == 0:
                    total[:, at : at + size] = value
                else:
                    outs[by - 1][:, at : at + size] = value.astype(bf16)
            at += size


def halved_kernel(seat, token_in, *refs, count, rows, passing, closing):
    refs = refs[passing:]
    parts, refs = refs[2 * count : 2 * count + closing], refs[: 2 * count] + refs[2 * count + closing :]
    kept_out, sent_out, token_ref = refs[2 * count : 2 * count + 3]
    if closing:
        refs[2 * count + 3][...] = functools.reduce(jnp.add, [x[...].astype(f32) for x in parts])
    token_ref[0] = token_in[0]
    mine = seat[2] % 2
    at = 0
    for i in range(count):
        kept, got = refs[2 * i], refs[2 * i + 1]
        size = kept.shape[2]
        for j in range(kept.shape[1] // rows):
            part = slice(j * rows, (j + 1) * rows)
            for b in range(2):
                for out, z in ((kept_out, 2 * b + mine), (sent_out, 2 * b + 1 - mine)):
                    value = kept[z, part, :].astype(f32) + got[z, part, :].astype(f32)
                    out[b, :, at : at + size] = value.astype(bf16)
            at += size


def middle_kernel(seat, token_in, *refs, passing):
    kept, got, total, sent, token_ref = refs[passing : passing + 5]
    token_ref[0] = token_in[0]
    mine = seat[2] // 2
    total[...] = kept[mine].astype(f32) + got[mine].astype(f32)
    sent[...] = (kept[1 - mine].astype(f32) + got[1 - mine].astype(f32)).astype(bf16)


class Halved:
    def __init__(self, kept, sent):
        self.kept, self.got = kept, xor_permute(sent, "dp", 1)


def halved_step(seat, token, sums, rows, passing, closing, spec):
    closed = [jax.ShapeDtypeStruct(x.shape, f32) for x in closing[:1]]
    specs_in, specs_out, shapes, aliases = handed_on(passing, 2, 3 + len(closed))
    size = sum(x.kept.shape[1] // rows * x.kept.shape[2] for x in sums)
    shape = jax.ShapeDtypeStruct((2, rows, size), bf16)
    kept, sent, token, *rest = one_step(
        functools.partial(halved_kernel, count=len(sums), rows=rows, passing=len(passing), closing=len(closing)),
        in_specs=[SMEM_SPEC] * 2 + specs_in + [spec] * (2 * len(sums) + len(closing)),
        out_specs=[spec, VMEM_SPEC, SMEM_SPEC] + [FAR_SPEC] * len(closed) + specs_out,
        out_shape=[shape, shape, TOKEN] + closed + shapes,
        input_output_aliases=aliases,
        compiler_params=pltpu.CompilerParams(vmem_limit_bytes=SMALL_VMEM),
    )(seat, token, *passing, *[y for x in sums for y in (x.kept, x.got)], *closing)
    return Halved(kept, sent), token, tuple(rest[len(closed) :]), rest[0] if closed else None


def middle_step(seat, token, halved, passing, spec):
    specs_in, specs_out, shapes, aliases = handed_on(passing, 2, 3)
    shape = jax.ShapeDtypeStruct
    total, sent, token, *passing = one_step(
        functools.partial(middle_kernel, passing=len(passing)),
        in_specs=[SMEM_SPEC] * 2 + specs_in + [spec] * 2,
        out_specs=[FAR_SPEC, VMEM_SPEC, SMEM_SPEC] + specs_out,
        out_shape=[shape(halved.kept.shape[1:], f32), shape(halved.kept.shape[1:], bf16), TOKEN] + shapes,
        input_output_aliases=aliases,
        compiler_params=pltpu.CompilerParams(vmem_limit_bytes=SMALL_VMEM),
    )(seat, token, *passing, halved.kept, halved.got)
    halved.parts = (total, xor_permute(sent, "dp", 2))
    return token, tuple(passing)


class FastSum:
    def __init__(self, kept, sent, bits):
        self.kept, self.bits = kept, bits
        self.got = xor_permute(sent, "ctx", bits[0])

    def start(self):
        self.got = xor_permute(self.sent, "ctx", self.bits[1])


def handed_on(passing, before, after):
    specs = [ANY_SPEC] * len(passing)
    shapes = [jax.ShapeDtypeStruct(x.shape, x.dtype) for x in passing]
    return specs, specs, shapes, {before + i: after + i for i in range(len(passing))}


def hand_on_kernel(token_in, *refs, meanwhile, passing):
    refs[meanwhile + passing][0] = token_in[0]


def hand_on(token, meanwhile, passing):
    specs_in, specs_out, shapes, aliases = handed_on(passing, 1 + len(meanwhile), 1)
    outs = one_step(
        functools.partial(hand_on_kernel, meanwhile=len(meanwhile), passing=len(passing)),
        in_specs=[SMEM_SPEC] + [VMEM_SPEC] * len(meanwhile) + specs_in,
        out_specs=[SMEM_SPEC] + specs_out,
        out_shape=[TOKEN] + shapes,
        input_output_aliases=aliases,
    )(token, *meanwhile, *passing)
    return outs[0], outs[1:]


def second_step(seat, token, sums, passing, closing, behind, spec):
    closed = [jax.ShapeDtypeStruct(x.shape, f32) for x in closing[:1]]
    specs_in, specs_out, shapes, aliases = handed_on(passing, 2 + len(behind), 2 * len(sums) + 1 + len(closed))
    shape = lambda x: jax.ShapeDtypeStruct((x.shape[0] // 2,) + x.shape[1:], bf16)
    outs = one_step(
        functools.partial(second_kernel, bits=[x.bits[1] for x in sums], passing=len(passing), closing=len(closing), behind=len(behind)),
        in_specs=[SMEM_SPEC] * 2 + [ANY_SPEC] * len(behind) + specs_in + [spec] * (2 * len(sums) + len(closing)),
        out_specs=[VMEM_SPEC] * (2 * len(sums)) + [SMEM_SPEC] + [FAR_SPEC] * len(closed) + specs_out,
        out_shape=[shape(x.kept) for x in sums for _ in range(2)] + [TOKEN] + closed + shapes,
        input_output_aliases=aliases,
        compiler_params=pltpu.CompilerParams(vmem_limit_bytes=SMALL_VMEM),
    )(seat, token, *behind, *passing, *[y for x in sums for y in (x.kept, x.got)], *closing)
    for i, x in enumerate(sums):
        x.kept, x.sent = outs[2 * i], outs[2 * i + 1]
    outs = outs[2 * len(sums) :]
    return outs[0], outs[1 + len(closed) :], outs[1] if closed else None


def last_step(seat, token, sums, rows, passing):
    dp_count = sums[0].kept.shape[0]
    specs_in, specs_out, shapes, aliases = handed_on(passing, 2, dp_count + 1)
    size = sum(x.kept.shape[1] // rows * x.kept.shape[2] for x in sums)
    shape = jax.ShapeDtypeStruct((rows, size), bf16)
    outs = one_step(
        functools.partial(last_kernel, count=len(sums), rows=rows, dp_count=dp_count, passing=len(passing)),
        in_specs=[SMEM_SPEC] * 2 + specs_in + [VMEM_SPEC] * (2 * len(sums)),
        out_specs=[VMEM_SPEC] * dp_count + [SMEM_SPEC] + specs_out,
        out_shape=[jax.ShapeDtypeStruct((rows, size), f32)] + [shape] * (dp_count - 1) + [TOKEN] + shapes,
        input_output_aliases=aliases,
        compiler_params=pltpu.CompilerParams(vmem_limit_bytes=SMALL_VMEM),
    )(seat, token, *passing, *[y for x in sums for y in (x.kept, x.got)])
    gots = [xor_permute(x, "dp", by) for by, x in enumerate(outs[1:dp_count], 1)]
    return outs[0], gots, outs[dp_count], outs[dp_count + 1 :]


def final_parts_kernel(seat, *refs, counts):
    *refs, keep, send = refs
    sums, at = [], 0
    for count in counts:
        sums.append(functools.reduce(jnp.add, [x[...].astype(f32) for x in refs[at : at + count]]))
        at += count
    cut = sums[0].shape[1]
    for section in range(2):

        @pl.when(seat[0] == section)
        def _(section=section):
            for out, layer in ((keep, section), (send, 1 - section)):
                out[:, :cut] = sums[2 * layer]
                out[:, cut:] = sums[2 * layer + 1]


def final_parts(seat, groups):
    parts = [x for group in groups for x in group]
    rows = parts[0].shape[0]
    out = jax.ShapeDtypeStruct((rows, groups[0][0].shape[1] + groups[1][0].shape[1]), f32)
    return one_step(
        functools.partial(final_parts_kernel, counts=[len(x) for x in groups]),
        in_specs=[SMEM_SPEC] + [VMEM_SPEC] * len(parts),
        out_specs=[VMEM_SPEC] * 2,
        out_shape=[out, out],
        compiler_params=pltpu.CompilerParams(vmem_limit_bytes=SMALL_VMEM),
    )(seat, *parts)


def final_outs_kernel(seat, keep, got, joint, mixer, up, down):
    half, half_up, rows = mixer.shape[1] // 2, up.shape[1] // 2, mixer.shape[0]
    width = 2 * half
    for section in range(2):

        @pl.when(seat[0] == section)
        def _(section=section):
            for i, ref in enumerate((keep, got) if section == 0 else (got, keep)):
                times = down.shape[0] // rows
                for j in range(times):
                    down[j * rows : (j + 1) * rows, i * half : (i + 1) * half] = ref[:, j * half : (j + 1) * half]
                at = times * half
                up[:, i * half_up : (i + 1) * half_up] = ref[:, at : at + half_up]
                at += half_up
                mixer[:, i * half : (i + 1) * half] = ref[:, at : at + half]
                at += half
                joint[:, (1 + i) * width : (2 + i) * width] = ref[:, at : at + width]
                joint[:, i * half : (i + 1) * half] = ref[:, at + width : at + width + half]


def final_outs(seat, keep, got, width, ff):
    rows = keep.shape[0]
    shape = lambda *x: jax.ShapeDtypeStruct(x, f32)
    return one_step(
        final_outs_kernel,
        in_specs=[SMEM_SPEC] + [VMEM_SPEC] * 2,
        out_specs=[VMEM_SPEC] * 4,
        out_shape=[shape(rows, 3 * width), shape(rows, width), shape(rows, ff), shape(rows * (ff // width), width)],
        compiler_params=pltpu.CompilerParams(vmem_limit_bytes=SMALL_VMEM),
    )(seat, keep, got)


def mix_grads_kernel(small, _, pre, post):
    rows = lax.broadcasted_iota(jnp.int32, (HEADS, small.shape[1]), 0)
    cols = lax.broadcasted_iota(jnp.int32, (HEADS, small.shape[1]), 1)
    heads = jnp.where(cols // HEAD == rows, 1.0, 0.0).astype(f32)
    dot = lambda a, b: lax.dot_general(
        a, b, (((1,), (1,)), ((), ())), precision=lax.Precision.HIGHEST, preferred_element_type=f32
    )
    pre[:, 0, :] = 0.125 * dot(heads, small[2 : 2 + HEADS, :])
    post[:, 0, :] = dot(small[2 + HEADS : 2 + 2 * HEADS, :], heads)


def mix_grads(small, behind):
    out = jax.ShapeDtypeStruct((HEADS, 1, HEADS), f32)
    return one_step(
        mix_grads_kernel, in_specs=[VMEM_SPEC, ANY_SPEC], out_specs=[VMEM_SPEC] * 2, out_shape=[out, out]
    )(small, behind)


def total_of(part, gots):
    for got in gots:
        part = part + got.astype(f32)
    return part


def join_kernel(
    seat, token_in, keep_ref, got_ref, normed_ref, own, own_other, dq, dq_other, joint_own, joint_got,
    small_own, small_got, dn_kept, dn_sent, dnq_ref, a_kept, a_sent, b_kept, b_sent, gain_grad_ref, token_ref,
    kv_w, q_w, dkv, dn, a_blocks, b_blocks, sems, *, layer,
):
    token_ref[0] = token_in[0]
    width = dkv.shape[1]
    section, which = seat[SECTION], seat[WHICH + layer]
    for i, ref in enumerate((joint_own, joint_got)):

        @pl.when(which == i)
        def _(ref=ref):
            cols = pl.ds(pl.multiple_of((1 + section) * width, width), width)
            pltpu.make_async_copy(ref.at[0, :, cols], kv_w, sems.at[0]).start()
            pltpu.make_async_copy(ref.at[0, :, pl.ds(0, width)], q_w, sems.at[1]).start()

    dkv[...] = (keep_ref[...].astype(f32) + got_ref[...].astype(f32)).astype(bf16)
    rows, size_a, size_b = a_blocks.shape[1], a_blocks.shape[2], b_blocks.shape[2]
    grad = dense_tn(normed_ref[...], dkv[:, :size_a])
    a_blocks[...] = grad.astype(bf16).reshape(-1, rows, size_a)
    grad = dense_tn(normed_ref[...], dkv[:, size_a:])
    b_blocks[:, :, : width - size_a] = grad.astype(bf16).reshape(-1, rows, width - size_a)
    half = width // 2
    grad = dense_tn(own[...], half_columns(dq, section, half)) + dense_tn(
        own_other[...], half_columns(dq_other, section, half)
    )
    b_blocks[:, :, width - size_a :] = grad.astype(bf16).reshape(-1, rows, half)
    split_blocks(a_blocks, a_kept, a_sent, seat[1] % 2)
    split_blocks_first(b_blocks, b_kept, b_sent, seat[1] // 2)
    for i in range(2):
        pltpu.make_async_copy(joint_own.at[0, :, pl.ds(0, width)], (kv_w, q_w)[i], sems.at[i]).wait()
    back = dense_nt(dkv[...], kv_w[...])
    dn[...] = back.astype(bf16)
    back_q = dense_nt(dq[...], q_w[...])
    dnq_ref[...] = back_q
    gain_grad = jnp.sum(back * normed_ref[...].astype(f32), axis=0, keepdims=True)
    gain_grad = gain_grad + jnp.sum(back_q * own[...].astype(f32), axis=0, keepdims=True)
    gain_grad_ref[...] = gain_grad / small_of(small_own, small_got, which)(GAIN_A, 1)
    blk = own.shape[0] // 2
    last = dn.shape[0] // blk - 1
    for i in range(dn_kept.shape[0] // blk):
        for out, side in ((dn_kept, section), (dn_sent, 1 - section)):
            core = (i // 2) * 2 + side
            at = core if i % 2 == 0 else last - core
            out[i * blk : (i + 1) * blk, :] = dn[pl.ds(pl.multiple_of(at * blk, blk), blk), :]


def join(seat, layer, token, arrays, joints, smalls, count, rows):
    seq, width = arrays[0].shape
    own_count = arrays[3].shape[0]
    size_a = 2 * width // 3
    size_b = width - size_a + width // 2
    shape = jax.ShapeDtypeStruct
    a_shape, b_shape = (shape((count // 2, rows, size), bf16) for size in (size_a, size_b))
    half_rows = shape((seq // 2, width), bf16)
    return one_step(
        functools.partial(join_kernel, layer=layer),
        in_specs=[SMEM_SPEC] * 2
        + [VMEM_SPEC] * 2
        + [FAR_SPEC] * 3
        + [VMEM_SPEC] * 2
        + [HBM_SPEC] * 2
        + [VMEM_SPEC] * 2,
        out_specs=[VMEM_SPEC] * 8 + [SMEM_SPEC],
        out_shape=[half_rows, half_rows, shape((own_count, width), f32)]
        + [a_shape, a_shape, b_shape, b_shape, shape((1, width), f32), TOKEN],
        scratch_shapes=[
            pltpu.VMEM((width, width), bf16),
            pltpu.VMEM((width, width), bf16),
            pltpu.VMEM((seq, width), bf16),
            pltpu.VMEM((seq, width), bf16),
            pltpu.VMEM((count, rows, size_a), bf16),
            pltpu.VMEM((count, rows, size_b), bf16),
            pltpu.SemaphoreType.DMA((2,)),
        ],
        compiler_params=pltpu.CompilerParams(vmem_limit_bytes=SMALL_VMEM),
    )(seat, token, *arrays, *joints, *smalls)


class Summer:
    def __init__(self, blocks, backwards):
        self.dp_count, ctx_count = blocks[0].shape[:2]
        bits = [1 << i for i in range(ctx_count.bit_length() - 1)]
        self.left = bits[::-1]
        self.order = bits[::-1] if backwards else bits
        self.parts = [x.reshape((self.dp_count,) + (2,) * len(bits) + x.shape[2:]) for x in blocks]

    def send(self, token=0):
        bit, self.order = self.order[0], self.order[1:]
        self.axis = 1 + self.left.index(bit)
        self.left = [b for b in self.left if b != bit]
        self.mine = (lax.axis_index("ctx") // bit) % 2
        at = 1 - self.mine + token
        sent = [lax.dynamic_index_in_dim(x, at, self.axis, keepdims=False) for x in self.parts]
        sent = sent[0] if len(sent) == 1 else jnp.concatenate(sent, axis=-1)
        self.got = xor_permute(sent, "ctx", bit)
        return [sent]

    def add(self, token):
        at, parts = 0, []
        for x in self.parts:
            kept = lax.dynamic_index_in_dim(x, self.mine + token, self.axis, keepdims=False)
            got = self.got[..., at : at + x.shape[-1]]
            at += x.shape[-1]
            parts.append((kept.astype(f32) + got.astype(f32)).astype(bf16))
        self.parts = parts

    def rest(self, token):
        self.add(token)
        while self.order:
            self.send()
            self.add(0)


class LastSum:
    def __init__(self, summers, rows):
        pieces = []
        for x in [x for one in summers for x in one.parts]:
            pieces += [x[:, i : i + rows] for i in range(0, x.shape[1], rows)]
        self.part = jnp.concatenate(pieces, axis=-1)

    def send(self):
        dp = lax.axis_index("dp")
        sent = [
            lax.dynamic_index_in_dim(self.part, dp ^ by, 0, keepdims=False)
            for by in range(1, self.part.shape[0])
        ]
        self.got = [xor_permute(x, "dp", by) for by, x in enumerate(sent, 1)]
        return sent

    @property
    def total(self):
        return lax.dynamic_index_in_dim(self.part, lax.axis_index("dp"), 0, keepdims=False).astype(f32)


def all_sum(x, tokens):
    steps = [(axis, 1 << i) for axis in ("ctx", "dp") for i in range(lax.axis_size(axis).bit_length() - 1)]
    for i, (axis, bit) in enumerate(steps):
        got = xor_permute(x, axis, bit)
        x = x + tokens[min(i, len(tokens) - 1)].astype(f32) + got
    return x


def local(
    inputs, lengths, cotangent, first_gain, joint_weight, pre_mix, post_mix,
    mixer_weight, second_gain, up_weight, down_weight,
):
    s = lax.axis_index("section")
    ctx = lax.axis_index("ctx")
    n = lax.axis_size("ctx")
    dp_count = lax.axis_size("dp")
    chips = n // 2
    micro_count, row_count, local_len, width = inputs.shape
    ff = up_weight.shape[2]
    seq = local_len * n
    blk = local_len // 2
    m = ctx // chips
    xi = ctx % chips
    core = xi * 2 + s
    zero = jnp.zeros((), jnp.int32)
    inputs = inputs.reshape(micro_count, 2, blk, width)
    cotangent = cotangent.reshape(micro_count, 2, blk, width)
    pick = lambda arr, i: lax.dynamic_index_in_dim(arr, i, 0, keepdims=False)

    spread = lambda mix: jnp.dot(mix, jnp.repeat(jnp.eye(HEADS, dtype=f32), HEAD, axis=1), precision=lax.Precision.HIGHEST)
    lines = lambda x, size: jnp.pad(x, ((0, size - x.shape[0]), (0, 0)))
    gains = jnp.concatenate([first_gain, second_gain]).astype(f32)
    small_own = jnp.concatenate(
        [lines(gains, PRE), lines(0.125 * spread(pre_mix[0].T), POST - PRE), lines(spread(post_mix[0]), SMALL_ROWS - POST)]
    )
    smalls = (small_own, swap_section(small_own))
    joints, mixers, ups, downs = (
        (w, swap_section(w)) for w in (joint_weight, mixer_weight, up_weight, down_weight)
    )

    mine = pick(inputs, m)
    pieces = []
    for d in range(1, n):
        target = m ^ (1 if d >= chips else 0)
        pieces.append(xor_permute(pick(pick(inputs, target), s), "ctx", d))
    other_pieces = [swap_section(jnp.concatenate(pieces))]
    chip_of = [ctx ^ d for d in range(1, n)]
    blocks0 = [2 * ctx, 2 * ctx + 1] + [2 * c + s for c in chip_of] + [2 * c + 1 - s for c in chip_of]
    pieces0 = [mine.reshape(2 * blk, width)] + pieces + other_pieces

    length = pick(lengths.reshape(-1), m)
    low_start = core * blk
    high_start = (2 * n - 1 - core) * blk
    bk = min(256, seq)
    cores1 = [(xi ^ d) * 2 + side for side in (s, 1 - s) for d in range(chips)]
    blocks1 = [b for c in cores1 for b in (c, 2 * n - 1 - c)]
    info = [s, ctx, lax.axis_index("dp"), length, low_start, high_start, s != 0, s != 1, *blocks0, *blocks1]
    info = jnp.stack([jnp.asarray(x, jnp.int32) for x in info])

    def gather_row(x):
        got = [x] + [xor_permute(x, "ctx", d) for d in range(1, chips)]
        return got + [swap_section(y) for y in got]

    def forward(layer, pieces, meanwhile):
        attended, q, normed_own, x_own, token, normed_all, k, v, u, lse = attend(
            info, layer, pieces, 2 * blk, smalls, joints, bk
        )
        weights = [x for pair in (mixers, ups, downs) for x in pair]
        out, hidden, normed_two, upward, active, token = feed(
            info, layer, x_own, attended, smalls, weights, ff, meanwhile
        )
        rows = [(x, swap_section(x)) for x in (active, normed_two, attended, normed_own)]
        return out, (x_own, q, k, v, u, lse, hidden, upward, rows, normed_all)

    def half(x, which):
        return lax.dynamic_slice_in_dim(x, which * (x.shape[1] // 2), x.shape[1] // 2, 1)

    def product(left, right):
        return (dense_tn(left[0], right[0]) + dense_tn(left[1], right[1])).astype(bf16)

    def blocks_of(grad):
        return grad.reshape(dp_count, n, grad.shape[0] // (dp_count * n), grad.shape[1])

    shard = width // (dp_count * n)

    fast = n == 4 and dp_count == 4 and shard % 16 == 0
    count = dp_count * n

    class Slow:
        def first(rows, keep, other):
            active, two, att, _ = rows
            cut, end = ff // 2, (ff + width) // 2
            of = lambda *cols: (keep[:, slice(*cols)], other[:, slice(*cols)])
            down_sum = Summer([blocks_of(product(active, of(end, None)))], False)
            up_sum = Summer([blocks_of(product(two, of(0, cut))), blocks_of(product(att, of(cut, end)))], True)
            return down_sum, up_sum, token_after(*down_sum.send(), *up_sum.send()).reshape(1)

        def second(token, sums, passing=(), closing=(), behind=()):
            for one in sums:
                one.add(token[0])
            return token, passing, total_of(closing[0], closing[1:]) if closing else None

        def last(token, sums, passing=()):
            for one in sums:
                one.rest(token[0])
            one = LastSum(sums, shard)
            one.send()
            one.parts = (one.total, *one.got)
            return one, token, passing

        def halved(token, sums, passing=(), closing=()):
            return *Slow.last(token, sums, passing), total_of(closing[0], closing[1:]) if closing else None

        def middle(token, one, passing=()):
            return token, passing

    class Fast:
        def first(rows, keep, other):
            return products(info, (*rows[0], *rows[1], *rows[2], keep, other), count, shard)

        def second(token, sums, passing=(), closing=(), behind=()):
            return second_step(info, token, sums, passing, closing, behind, VMEM_SPEC if behind else FAR_SPEC)

        def last(token, sums, passing=()):
            part, gots, token, passing = last_step(info, token, sums, shard, passing)
            one = types.SimpleNamespace(parts=(part, *gots))
            return one, token, passing

        def halved(token, sums, passing=(), closing=()):
            return halved_step(info, token, sums, shard, passing, closing, VMEM_SPEC if closing else FAR_SPEC)

        def middle(token, one, passing=()):
            return middle_step(info, token, one, passing, FAR_SPEC if passing else VMEM_SPEC)

    steps = Fast if fast else Slow

    def backward(layer, dy, kept, earlier):
        x_own, q, k, v, u, lse, hidden, upward, rows, normed_all = kept
        rows_normed = rows[3]
        here = s == layer
        gain_a = jnp.where(here, smalls[0][GAIN_A], smalls[1][GAIN_A])
        earlier[0]()
        weights = [x for pair in (mixers, ups, downs) for x in pair]
        keep, send, dhidden, datt, gain_b_grad, token = feed_back(
            info, layer, dy, upward, hidden, smalls, weights, ()
        )
        token, (send,) = earlier[1](token, (send,))
        down_sum, up_sum, first_token = steps.first(rows, keep, swap_section(send))
        dq, dkv_keep, dkv_send, pre_rows, post_rows, token = attend_back(
            info, layer, q, datt, u, lse, k, v, smalls, bk, (token, first_token)
        )
        token, (dkv_send, dq) = earlier[2](token, (down_sum, up_sum), (dkv_send, dq))
        got, dq_other = swap_section(dkv_send), swap_section(dq)
        if fast:
            dn_kept, dn_sent, dnq, a_kept, a_sent, b_kept, b_sent, gain_a_grad, token = join(
                info, layer, token, (dkv_keep, got, normed_all, *rows_normed, dq, dq_other), joints, smalls, count, shard
            )
            kv_sum, q_sum = FastSum(a_kept, a_sent, (1, 2)), FastSum(b_kept, b_sent, (2, 1))
            dn_kept, dn_sent = (x.reshape(chips, 2, blk, width) for x in (dn_kept, dn_sent))
        else:
            joint_w = jnp.where(here, joints[0][0], joints[1][0])
            kv_w = lax.dynamic_slice_in_dim(joint_w, width * (1 + s), width, 1)
            dkv = (dkv_keep.astype(f32) + got.astype(f32)).astype(bf16)
            dn = dense_nt(dkv, kv_w)
            gain_a_grad = jnp.sum(dn * normed_all.astype(f32), axis=0)
            dn = dn.astype(bf16).reshape(2 * n, blk, width)
            dn = jnp.stack([dn[i if h == 0 else 2 * n - 1 - i] for i in range(n) for h in range(2)])
            dn = dn.reshape(chips, 2, 2, blk, width)
            dn_kept = lax.dynamic_index_in_dim(dn, s, 1, keepdims=False)
            dn_sent = lax.dynamic_index_in_dim(dn, 1 - s, 1, keepdims=False)
            dnq = dense_nt(dq, joint_w[:, :width])
            gain_a_grad = (gain_a_grad + jnp.sum(dnq * rows_normed[0].astype(f32), axis=0)) / gain_a
            kv_part = blocks_of(dense_tn(normed_all, dkv).astype(bf16))
            q_part = blocks_of(product(rows_normed, (half(dq, s), half(dq_other, s))))
            cut = 2 * width // 3
            kv_sum = Summer([kv_part[..., :cut]], False)
            q_sum = Summer([kv_part[..., cut:], q_part], True)
            kv_sum.send()
            q_sum.send()
        token, (dn_sent,) = earlier[3](token, (dn_sent,), (down_sum, up_sum))
        low = (dn_kept.astype(f32) + swap_section(dn_sent).astype(f32)).astype(bf16)
        gots = [xor_permute(pick(low, xi ^ d), "ctx", d) for d in range(1, chips)]
        sums = (down_sum, up_sum, kv_sum, q_sum)
        token = earlier[4](token, low, sums)
        scattered = pick(low, xi + token[0]).astype(f32)
        for x in gots:
            scattered = scattered + x.astype(f32)
        scaled = (scattered.reshape(2 * blk, width) + dnq) * gain_a
        values = x_own.astype(f32)
        inverse = rms_inverse(values)
        unit = values * inverse
        dfront = inverse * (scaled - unit * jnp.mean(scaled * unit, axis=-1, keepdims=True))
        small = jnp.concatenate([gain_a_grad.reshape(1, -1), gain_b_grad.reshape(1, -1), pre_rows, post_rows])
        return dhidden + dfront, sums, small, token

    low_chip = ctx < chips
    there = [(i, chips + i) for i in range(chips)] + [(n - 1 - i, i) for i in range(chips)]
    here = [(n - 1 - i, chips + i) for i in range(chips)] + [(i, i) for i in range(chips)]
    first = jnp.where(low_chip, s, 1 - s)
    halves = lax.dynamic_index_in_dim(cotangent, first, 1, keepdims=False)
    ones, twos = jnp.where(low_chip, halves[1], halves[0]), jnp.where(low_chip, halves[0], halves[1])
    one, two = lax.ppermute(ones, "ctx", there), lax.ppermute(twos, "ctx", here)
    dy1 = jnp.concatenate([jnp.where(m == 0, two, one), jnp.where(m == 0, one, two)])
    x1, kept0 = forward(0, pieces0, (one, two))
    y, kept1 = forward(1, gather_row(x1), ())

    def send_home(x):
        x = x.reshape(2, blk, width)
        one = lax.ppermute(jnp.where(m == 0, x[1], x[0]), "ctx", [(b, a) for a, b in there])
        two = lax.ppermute(jnp.where(m == 0, x[0], x[1]), "ctx", [(b, a) for a, b in here])
        return one, two

    def at_home(one, two):
        return jnp.where(low_chip, jnp.stack([two, one]), jnp.stack([one, two]))

    def start(sums):
        for one in sums:
            one.start() if fast else one.send()

    def no_step():
        return None

    state = {}

    def after_attention(token, sums, passing):
        token, passing, _ = steps.second(token, sums, passing)
        start(sums)
        return token, passing

    def after_join(token, passing, sums):
        state["big"], token, passing, _ = steps.halved(token, sums, passing)
        return token, passing

    def after_low(token, low, sums):
        token, _, _ = steps.second(token, sums[2:], behind=(low,))
        start(sums[2:])
        return token

    first_steps = (no_step, lambda token, passing: (token, passing), after_attention, after_join, after_low)
    dx1, (_, _, kv1, q1), small1, _ = backward(1, dy1, kept1, first_steps)
    dy0 = dx1.astype(bf16)
    y_sent = send_home(y)

    def after_feed(token, passing):
        state["joint1"], token, passing, _ = steps.halved(token, [kv1, q1], (*passing, *y_sent))
        token, (passing, *state["y"]) = steps.middle(token, state["big"], passing)
        return token, (passing,)

    def after_attention(token, sums, passing):
        token, passing, state["big1"] = steps.second(token, sums, passing, state["big"].parts)
        start(sums)
        token, passing = steps.middle(token, state["joint1"], passing)
        return token, passing

    def after_join(token, passing, sums):
        state["big0"], token, passing, state["joint1"] = steps.halved(token, sums, passing, state["joint1"].parts)
        state["token"] = token
        return token, passing

    def after_low(token, low, sums):
        token, _, _ = steps.second(token, sums[2:], behind=(low,))
        start(sums[2:])
        return steps.middle(token, state["big0"])[0]

    dx0, (down0, up0, kv0, q0), small0, token = backward(
        0, dy0, kept0, (no_step, after_feed, after_attention, after_join, after_low)
    )
    early = token
    dx0 = dx0.astype(bf16)
    dx_home = at_home(*send_home(dx0))
    y_home = at_home(*state["y"])

    small_got = swap_section(jnp.where(s == 0, small1, small0))
    small = jnp.where(s == 0, small0, small1) + small_got
    joint0, last_token, _ = steps.last(token, [kv0, q0], (dx0,))
    small = all_sum(small, (state["token"][0], early[0], token[0], last_token[0]))

    got = swap_section(jnp.where(s == 0, y_home, dx_home))
    held = jnp.where(s == 0, dx_home, y_home)
    is_first = jnp.where(low_chip, s, 1 - s) == 0
    ends = jnp.stack([jnp.where(is_first, held, got), jnp.where(is_first, got, held)], axis=1)
    ends = ends.reshape(1, micro_count, row_count, local_len, width)

    at = (lax.axis_index("dp") * n + ctx) * shard
    gain_a_out, gain_b_out = (lax.dynamic_slice_in_dim(small[i], at, shard, 0) for i in range(2))
    half_d, half_ff, times = width // 2, ff // 2, ff // width
    if fast:
        groups = (state["big0"].parts, joint0.parts, (state["big1"],), (state["joint1"],))
        keep, send = final_parts(info, groups)
        behind = keep
        joint_out, mixer_out, up_out, down_out = final_outs(info, keep, swap_section(send), width, ff)
    else:
        behind = small
        big0, joint0 = (total_of(x.parts[0], x.parts[1:]) for x in (state["big0"], joint0))
        pairs = ((big0, state["big1"]), (joint0, state["joint1"]))
        outs = []
        for at_zero, at_one in pairs:
            other = swap_section(jnp.where(s == 0, at_one, at_zero))
            own = jnp.where(s == 0, at_zero, at_one)
            outs.append((jnp.where(s == 0, own, other), jnp.where(s == 0, other, own)))
        (big_a, big_b), (joint_a, joint_b) = outs
        side = lambda *cuts: jnp.concatenate([x[:, at : at + size] for x, at, size in cuts], axis=1)
        down_out = jnp.concatenate(
            [side((big_a, i * half_d, half_d), (big_b, i * half_d, half_d)) for i in range(times)]
        )
        at = times * half_d
        up_out = side((big_a, at, half_ff), (big_b, at, half_ff))
        mixer_out = side((big_a, at + half_ff, half_d), (big_b, at + half_ff, half_d))
        joint_out = side((joint_a, width, half_d), (joint_b, width, half_d), (joint_a, 0, width), (joint_b, 0, width))
    pre_out, post_out = (x.transpose(1, 0, 2) for x in mix_grads(small, behind))
    return (
        ends,
        gain_a_out[None],
        joint_out[None],
        pre_out,
        post_out,
        mixer_out[None],
        gain_b_out[None],
        up_out[None],
        down_out[None],
    )


def solution(mesh):
    in_specs = (
        P(None, "dp", "ctx", None),
        P(None, "dp"),
        P(None, "dp", "ctx", None),
        P("section", None),
        P("section", None, None),
        P("section", None, None),
        P("section", None, None),
        P("section", None, None),
        P("section", None),
        P("section", None, None),
        P("section", None, None),
    )
    out_specs = (
        P("section", None, "dp", "ctx", None),
        P("section", ("dp", "ctx")),
        P("section", ("dp", "ctx"), None),
        P("section", None, None),
        P("section", None, None),
        P("section", ("dp", "ctx"), None),
        P("section", ("dp", "ctx")),
        P("section", ("dp", "ctx"), None),
        P("section", ("dp", "ctx"), None),
    )
    return jax.shard_map(local, mesh=mesh, in_specs=in_specs, out_specs=out_specs, check_vma=False)
```

```python
import functools
import math
import types

import jax
import jax.numpy as jnp
from jax import lax
from jax.experimental import pallas as pl
from jax.experimental.pallas import tpu as pltpu
from jax.sharding import PartitionSpec as P

HEADS = 12
HEAD = 64
eps = 1e-06
MASKED = -1e30
f32 = jnp.float32
bf16 = jnp.bfloat16
MIB = 1024 * 1024
SMALL_VMEM = 36 * MIB
BIG_VMEM = 60 * MIB


def dense(left_side, right_side):
    return jnp.dot(left_side, right_side, preferred_element_type=f32)


def dense_tn(left_side, right_side):
    return lax.dot_general(
        left_side, right_side, (((0,), (0,)), ((), ())), preferred_element_type=f32
    )


def dense_nt(left_side, right_side):
    return lax.dot_general(
        left_side, right_side, (((1,), (1,)), ((), ())), preferred_element_type=f32
    )


GAIN_A, GAIN_B, PRE, POST = 0, 1, 8, 24
SECTION, CTX, DP, LENGTH, STARTS, WHICH, BLOCKS = 0, 1, 2, 3, 4, 6, 8
SMALL_ROWS = 40


def small_of(own, got, which):
    return lambda at, size: jnp.where(which == 0, own[at : at + size, :], got[at : at + size, :])


def rms_inverse(values):
    return lax.rsqrt(jnp.mean(values * values, axis=-1, keepdims=True) + eps)


def lane_parts(x):
    return [x[:, i : i + 128] for i in range(0, x.shape[1], 128)]


def bias_of(q_start, k_start, length, bq, bk):
    rows = q_start + lax.broadcasted_iota(jnp.int32, (bq, bk), 0)
    cols = k_start + lax.broadcasted_iota(jnp.int32, (bq, bk), 1)
    return jnp.where((cols <= rows) & (cols < length), 0.0, MASKED).astype(f32)


def attend_kernel(info, small_own, small_got, joint_own, joint_got, *rest, bk, count_in, layer):
    (
        att_ref, q_ref, own_ref, x_ref, token_ref, normed_hbm, k_hbm, v_hbm, u_hbm, lse_hbm,
        joint, raw, normed, k, v, u, lse, qp, logit, total, top, norm, sems,
    ) = rest[count_in:]
    token_ref[0] = 0
    length, which = info[LENGTH], info[WHICH + layer]
    fetch((joint_own, joint_got), which, joint, sems.at[0])
    seq, width = normed.shape
    count = att_ref.shape[0]
    bq = count // 2
    small = small_of(small_own, small_got, which)
    gain, pre, post = small(GAIN_A, 1), small(PRE, HEADS), small(POST, HEADS)
    at = BLOCKS + layer * (seq // bq)
    for piece in rest[:count_in]:
        for j in range(piece.shape[0] // bq):
            x = piece[j * bq : (j + 1) * bq, :]
            span = pl.ds(pl.multiple_of(info[at] * bq, bq), bq)
            raw[span, :] = x
            x = x.astype(f32)
            normed[span, :] = (x * rms_inverse(x) * gain).astype(bf16)
            at += 1
    for i in range(2):
        span = pl.ds(pl.multiple_of(info[STARTS + i], bq), bq)
        own_ref[i * bq : (i + 1) * bq, :] = normed[span, :]
        x_ref[i * bq : (i + 1) * bq, :] = raw[span, :]
    fetched((joint_own, joint_got), joint, sems.at[0])
    cut = width // 3
    for i in range(3):
        cols = slice(width + i * cut, width + (i + 1) * cut)
        k[:, i * cut : (i + 1) * cut] = dense(normed[...], joint[:, cols]).astype(bf16)
    for i in range(3):
        cols = slice(2 * width + i * cut, 2 * width + (i + 1) * cut)
        v[:, i * cut : (i + 1) * cut] = dense(normed[...], joint[:, cols]).astype(bf16)
    q_ref[...] = dense(own_ref[...], joint[:, :width]).astype(bf16)
    outs = [
        pltpu.make_async_copy(a, b, sems.at[1 + i])
        for i, (a, b) in enumerate(((normed, normed_hbm), (k, k_hbm), (v, v_hbm)))
    ]
    for out in outs:
        out.start()

    def rows_step(step, carry):
        q_start = info[STARTS + step]
        mine = pl.ds(pl.multiple_of(step * bq, bq), bq)
        q32 = q_ref[mine, :].astype(f32)
        for h in range(HEADS):
            qp[h * bq : (h + 1) * bq, :] = (q32 * pre[h : h + 1, :]).astype(bf16)
        blocks = (jnp.minimum(q_start + bq, length) + bk - 1) // bk
        top[...] = jnp.full_like(top, MASKED)
        total[...] = jnp.zeros_like(total)
        norm[...] = jnp.zeros_like(norm)

        def score(kb, c):
            bias = bias_of(q_start, kb * bk, length, bq, bk)
            tile = dense_nt(qp[...], k[pl.ds(pl.multiple_of(kb * bk, bk), bk), :])
            tile = (tile.reshape(HEADS, bq, bk) + bias[None]).reshape(HEADS * bq, bk)
            logit[kb] = tile
            top[...] = functools.reduce(jnp.maximum, lane_parts(tile), top[...])
            return c

        lax.fori_loop(0, blocks, score, 0)
        highest = jnp.max(top[...], axis=-1, keepdims=True)
        top[...] = jnp.broadcast_to(highest, top.shape)

        def apply(kb, c):
            high = top[...]
            parts = [jnp.exp(x - high) for x in lane_parts(logit[kb])]
            norm[...] = functools.reduce(jnp.add, parts, norm[...])
            e = jnp.concatenate([x.astype(bf16) for x in parts], axis=1)
            total[...] += dense(e, v[pl.ds(pl.multiple_of(kb * bk, bk), bk), :])
            return c

        lax.fori_loop(0, blocks, apply, 0)
        sums = jnp.sum(norm[...], axis=-1, keepdims=True)
        scale = 1.0 / sums
        rows = pl.ds(pl.multiple_of(step * HEADS * bq, HEADS * bq), HEADS * bq)
        lse[rows, :] = jnp.broadcast_to(highest + jnp.log(sums), top.shape)
        att = jnp.zeros((bq, width), f32)
        for g in range(HEADS):
            part = total[g * bq : (g + 1) * bq, :] * scale[g * bq : (g + 1) * bq]
            u[pl.ds(pl.multiple_of(step * HEADS * bq + g * bq, bq), bq), :] = part.astype(bf16)
            att = att + part * post[g : g + 1, :]
        att_ref[mine, :] = att.astype(bf16)
        for i, (x, y) in enumerate(((u, u_hbm), (lse, lse_hbm))):
            pltpu.make_async_copy(x.at[rows], y.at[rows], sems.at[4 + 2 * step + i]).start()
        return carry

    lax.fori_loop(0, 2, rows_step, 0)
    for step in range(2):
        rows = pl.ds(step * HEADS * bq, HEADS * bq)
        for i, (x, y) in enumerate(((u, u_hbm), (lse, lse_hbm))):
            outs.append(pltpu.make_async_copy(x.at[rows], y.at[rows], sems.at[4 + 2 * step + i]))
    for out in outs:
        out.wait()


VMEM_SPEC = pl.BlockSpec(memory_space=pltpu.VMEM)
FAR_SPEC = pl.BlockSpec(memory_space=pltpu.VMEM)
ANY_SPEC = pl.BlockSpec(memory_space=pl.ANY)
HBM_SPEC = pl.BlockSpec(memory_space=pltpu.HBM)
SMEM_SPEC = pl.BlockSpec(memory_space=pltpu.SMEM)
TOKEN = jax.ShapeDtypeStruct((1,), jnp.int32)

LARGE = 64 * 1024
SMALL_COST = pl.CostEstimate(flops=0, bytes_accessed=0, transcendentals=0)


def in_hbm(spec, x):
    return (spec is FAR_SPEC or spec is HBM_SPEC) and math.prod(x.shape) >= LARGE


def from_hbm(spec, x):
    return pltpu.with_memory_space_constraint(x, pltpu.HBM) if in_hbm(spec, x) else x


def result_in_hbm(spec, x):
    return pltpu.HBM(x.shape, x.dtype) if in_hbm(spec, x) else x


def one_step(kernel, *, in_specs, out_specs, out_shape, **rest):
    def whole(spec, x):
        if spec is not VMEM_SPEC and spec is not FAR_SPEC:
            return spec
        zeros = (0,) * len(x.shape)
        return pl.BlockSpec(x.shape, lambda i: zeros, pipeline_mode=pl.Buffered(1))

    def run(*args):
        return pl.pallas_call(
            kernel,
            cost_estimate=SMALL_COST,
            grid=(1,),
            in_specs=[whole(*x) for x in zip(in_specs, args, strict=True)],
            out_specs=[whole(*x) for x in zip(out_specs, out_shape, strict=True)],
            out_shape=[result_in_hbm(*x) for x in zip(out_specs, out_shape)],
            **rest,
        )(*[from_hbm(*x) for x in zip(in_specs, args)])

    return run


def attend(info, layer, pieces, count, smalls, joints, bk):
    width = pieces[0].shape[1]
    seq = sum(x.shape[0] for x in pieces)
    bq = count // 2
    shape = jax.ShapeDtypeStruct
    return one_step(
        functools.partial(attend_kernel, bk=bk, count_in=len(pieces), layer=layer),
        in_specs=[SMEM_SPEC] + [VMEM_SPEC] * 2 + [HBM_SPEC] * 2 + [VMEM_SPEC] * len(pieces),
        out_specs=[VMEM_SPEC, FAR_SPEC, FAR_SPEC, VMEM_SPEC, SMEM_SPEC] + [HBM_SPEC] * 5,
        out_shape=[shape((count, width), bf16)] * 4
        + [TOKEN]
        + [shape((seq, width), bf16)] * 3
        + [shape((HEADS * count, width), bf16), shape((HEADS * count, 128), f32)],
        scratch_shapes=[
            pltpu.VMEM((width, 3 * width), bf16),
            pltpu.VMEM((seq, width), bf16),
            pltpu.VMEM((seq, width), bf16),
            pltpu.VMEM((seq, width), bf16),
            pltpu.VMEM((seq, width), bf16),
            pltpu.VMEM((HEADS * count, width), bf16),
            pltpu.VMEM((HEADS * count, 128), f32),
            pltpu.VMEM((HEADS * bq, width), bf16),
            pltpu.VMEM((seq // bk, HEADS * bq, bk), f32),
            pltpu.VMEM((HEADS * bq, width), f32),
            pltpu.VMEM((HEADS * bq, 128), f32),
            pltpu.VMEM((HEADS * bq, 128), f32),
            pltpu.SemaphoreType.DMA((8,)),
        ],
        compiler_params=pltpu.CompilerParams(vmem_limit_bytes=BIG_VMEM),
    )(info, *smalls, *joints, *pieces)


def feed_kernel(
    info, x_ref, att_ref, small_own, small_got,
    mixer_own, mixer_got, up_own, up_got, down_own, down_got, *rest, tile, extra, layer,
):
    (
        out_ref, hidden_ref, two_ref, upward_hbm, active_hbm, token_ref,
        mixer, up, down, upward, active, sems,
    ) = rest[extra:]
    token_ref[0] = 0
    which = info[WHICH + layer]
    pairs = ((mixer_own, mixer_got), (up_own, up_got), (down_own, down_got))
    fetch(pairs[0], which, mixer, sems.at[0])
    tiles = down.shape[0] // tile
    for j in range(tiles):
        fetch(pairs[1], which, up, sems.at[1 + j], column_part(j, tile))
        fetch(pairs[2], which, down, sems.at[1 + tiles + j], row_part(j, tile))
    gain = small_of(small_own, small_got, which)(GAIN_B, 1)
    fetched(pairs[0], mixer, sems.at[0])
    hidden = x_ref[...].astype(f32) + dense(att_ref[...], mixer[...])
    hidden_ref[...] = hidden
    two = (hidden * rms_inverse(hidden) * gain).astype(bf16)
    two_ref[...] = two
    result, outs = hidden, []
    for j in range(tiles):
        span = slice(j * tile, (j + 1) * tile)
        fetched(pairs[1], up, sems.at[1 + j], column_part(j, tile))
        u = dense(two, up[:, span])
        upward[:, span] = u
        act = (0.5 * u * (1.0 + jnp.tanh(0.7978845608 * (u + 0.044715 * (u * u * u))))).astype(bf16)
        active[:, span] = act
        part = column_part(j, tile)
        for i, (x, y) in enumerate(((upward, upward_hbm), (active, active_hbm))):
            outs.append(pltpu.make_async_copy(x.at[part], y.at[part], sems.at[1 + (2 + i) * tiles + j]))
            outs[-1].start()
        fetched(pairs[2], down, sems.at[1 + tiles + j], row_part(j, tile))
        result = result + dense(act, down[span, :])
    out_ref[...] = result.astype(bf16)
    for out in outs:
        out.wait()


def feed(info, layer, x, attended, smalls, weights, ff, extras):
    count, width = x.shape
    shape = jax.ShapeDtypeStruct
    return one_step(
        functools.partial(feed_kernel, tile=width, extra=len(extras), layer=layer),
        in_specs=[SMEM_SPEC] + [VMEM_SPEC] * 4 + [HBM_SPEC] * (6 + len(extras)),
        out_specs=[VMEM_SPEC, FAR_SPEC, FAR_SPEC] + [HBM_SPEC] * 2 + [SMEM_SPEC],
        out_shape=[
            shape((count, width), bf16),
            shape((count, width), f32),
            shape((count, width), bf16),
            shape((count, ff), f32),
            shape((count, ff), bf16),
            TOKEN,
        ],
        scratch_shapes=[
            pltpu.VMEM((width, width), bf16),
            pltpu.VMEM((width, ff), bf16),
            pltpu.VMEM((ff, width), bf16),
            pltpu.VMEM((count, ff), f32),
            pltpu.VMEM((count, ff), bf16),
            pltpu.SemaphoreType.DMA((1 + 4 * (ff // width),)),
        ],
        compiler_params=pltpu.CompilerParams(vmem_limit_bytes=SMALL_VMEM),
    )(info, x, attended, *smalls, *weights, *extras)


def fetch(pair, which, buffer, semaphore, at=()):
    for i, ref in enumerate(pair):

        @pl.when(which == i)
        def _(ref=ref):
            pltpu.make_async_copy(ref.at[(0, *at)], buffer.at[at] if at else buffer, semaphore).start()


def fetched(pair, buffer, semaphore, at=()):
    pltpu.make_async_copy(pair[0].at[(0, *at)], buffer.at[at] if at else buffer, semaphore).wait()


def row_part(i, size):
    return pl.ds(i * size, size), slice(None)


def column_part(i, size):
    return slice(None), pl.ds(i * size, size)


def gelu_slope(u):
    inner = 0.7978845608 * (u + 0.044715 * (u * u * u))
    t = jnp.tanh(inner)
    return 0.5 * (1.0 + t) + 0.5 * u * (1.0 - t * t) * (0.7978845608 + 0.1070322243 * (u * u))


def feed_back_kernel(
    info, dy_ref, upward_hbm, hidden_hbm, small_own, small_got,
    mixer_own, mixer_got, up_own, up_got, down_own, down_got, *rest, tile, extra, layer,
):
    (
        keep_ref, send_ref, dhidden_ref, datt_ref, gain_grad_ref, token_ref,
        mixer, up, down, upward_ref, hidden_ref, sems,
    ) = rest[extra:]
    token_ref[0] = 0
    which = info[WHICH + layer]
    width = dy_ref.shape[1]
    half_ff, half = down.shape[0] // 2, width // 2

    def put(value, number, at):
        for ref, equal in ((keep_ref, True), (send_ref, False)):

            @pl.when((info[SECTION] == number) == equal)
            def _(ref=ref):
                ref[:, at : at + value.shape[1]] = value

    pairs = ((down_own, down_got), (up_own, up_got), (mixer_own, mixer_got))
    tiles = down.shape[0] // tile
    for j in range(tiles):
        fetch(pairs[0], which, down, sems.at[j], row_part(j, tile))
        if j == 0:
            upward_copy = pltpu.make_async_copy(upward_hbm, upward_ref, sems.at[2 * tiles])
            upward_copy.start()
        fetch(pairs[1], which, up, sems.at[tiles + j], column_part(j, tile))
    hidden_copy = pltpu.make_async_copy(hidden_hbm, hidden_ref, sems.at[2 * tiles + 1])
    hidden_copy.start()
    fetch(pairs[2], which, mixer, sems.at[2 * tiles + 2])
    gain = small_of(small_own, small_got, which)(GAIN_B, 1)
    dy = dy_ref[...]
    grad = jnp.zeros(hidden_ref.shape, f32)
    for j in range(tiles):
        span = slice(j * tile, (j + 1) * tile)
        fetched(pairs[0], down, sems.at[j], row_part(j, tile))
        dactive = dense_nt(dy, down[span, :])
        if j == 0:
            upward_copy.wait()
        dup = (dactive * gelu_slope(upward_ref[:, span])).astype(bf16)
        put(dup, j * tile // half_ff, j * tile % half_ff)
        fetched(pairs[1], up, sems.at[tiles + j], column_part(j, tile))
        grad = grad + dense_nt(dup, up[:, span])
    hidden_copy.wait()
    hidden = hidden_ref[...]
    inverse = rms_inverse(hidden)
    unit = hidden * inverse
    gain_grad_ref[...] = jnp.sum(grad * unit, axis=0, keepdims=True)
    scaled = grad * gain
    dhidden = dy.astype(f32) + inverse * (scaled - unit * jnp.mean(scaled * unit, axis=-1, keepdims=True))
    dhidden_ref[...] = dhidden
    low = dhidden.astype(bf16)
    for i in range(2):
        put(low[:, i * half : (i + 1) * half], i, half_ff)
        put(dy[:, i * half : (i + 1) * half], i, half_ff + half)
    fetched(pairs[2], mixer, sems.at[2 * tiles + 2])
    datt_ref[...] = dense_nt(low, mixer[...]).astype(bf16)


def feed_back(info, layer, dy, upward, hidden, smalls, weights, extras):
    count, width = dy.shape
    ff = upward.shape[1]
    shape = jax.ShapeDtypeStruct
    return one_step(
        functools.partial(feed_back_kernel, tile=width, extra=len(extras), layer=layer),
        in_specs=[SMEM_SPEC, VMEM_SPEC, HBM_SPEC, HBM_SPEC, VMEM_SPEC, VMEM_SPEC] + [HBM_SPEC] * (6 + len(extras)),
        out_specs=[VMEM_SPEC, VMEM_SPEC, FAR_SPEC, VMEM_SPEC, VMEM_SPEC, SMEM_SPEC],
        out_shape=[
            shape((count, ff // 2 + width), bf16),
            shape((count, ff // 2 + width), bf16),
            shape((count, width), f32),
            shape((count, width), bf16),
            shape((1, width), f32),
            TOKEN,
        ],
        scratch_shapes=[
            pltpu.VMEM((width, width), bf16),
            pltpu.VMEM((width, ff), bf16),
            pltpu.VMEM((ff, width), bf16),
            pltpu.VMEM((count, ff), f32),
            pltpu.VMEM((count, width), f32),
            pltpu.SemaphoreType.DMA((2 * (ff // width) + 3,)),
        ],
        compiler_params=pltpu.CompilerParams(vmem_limit_bytes=SMALL_VMEM),
    )(info, dy, upward, hidden, *smalls, *weights, *extras)


def attend_back_kernel(
    info, q_ref, datt_ref, u_ref, lse_ref, k_hbm, v_hbm, small_own, small_got, *rest, bq, bk, extra, layer
):
    (
        dq_ref, keep_ref, send_ref, pre_grad_ref, post_grad_ref, token_ref,
        qp, dp, dk, dv, w, delta, k_ref, v_ref, sems,
    ) = rest[extra:]
    token_ref[0] = 0
    step = pl.program_id(0)
    copies = [pltpu.make_async_copy(x, y, sems.at[i]) for i, (x, y) in enumerate(((k_hbm, k_ref), (v_hbm, v_ref)))]

    @pl.when(step == 0)
    def _():
        for copy in copies:
            copy.start()

    length, which, q_start = info[LENGTH], info[WHICH + layer], info[STARTS + step]
    small = small_of(small_own, small_got, which)
    pre, post = small(PRE, HEADS), small(POST, HEADS)

    @pl.when(step == 0)
    def _():
        dk[...] = jnp.zeros_like(dk)
        dv[...] = jnp.zeros_like(dv)
        pre_grad_ref[...] = jnp.zeros_like(pre_grad_ref)
        post_grad_ref[...] = jnp.zeros_like(post_grad_ref)

    q32 = q_ref[...].astype(f32)
    datt = datt_ref[...].astype(f32)
    for h in range(HEADS):
        part = slice(h * bq, (h + 1) * bq)
        qp[part, :] = (q32 * pre[h : h + 1, :]).astype(bf16)
        scaled = datt * post[h : h + 1, :]
        dp[part, :] = scaled.astype(bf16)
        u = u_ref[part, :].astype(f32)
        delta[part, :] = jnp.broadcast_to(jnp.sum(scaled * u, axis=-1, keepdims=True), (bq, 128))
        post_grad_ref[h : h + 1, :] += jnp.sum(datt * u, axis=0, keepdims=True)
    w[...] = jnp.zeros_like(w)
    blocks = (jnp.minimum(q_start + bq, length) + bk - 1) // bk

    @pl.when(step == 0)
    def _():
        for copy in copies:
            copy.wait()

    def block(kb, c):
        span = pl.ds(pl.multiple_of(kb * bk, bk), bk)
        bias = bias_of(q_start, kb * bk, length, bq, bk)
        k_blk, v_blk = k_ref[span, :], v_ref[span, :]
        logits = dense_nt(qp[...], k_blk)
        logits = (logits.reshape(HEADS, bq, bk) + bias[None]).reshape(HEADS * bq, bk)
        grad = dense_nt(dp[...], v_blk)
        lse, spread = lse_ref[...], delta[...]
        attention, dlog = [], []
        for x, g in zip(lane_parts(logits), lane_parts(grad)):
            a = jnp.exp(x - lse)
            attention.append(a.astype(bf16))
            dlog.append((a * (g - spread)).astype(bf16))
        attention, dlog = jnp.concatenate(attention, axis=1), jnp.concatenate(dlog, axis=1)
        dv[span, :] += dense_tn(attention, dp[...])
        dk[span, :] += dense_tn(dlog, qp[...])
        w[...] += dense(dlog, k_blk)
        return c

    lax.fori_loop(0, blocks, block, 0)
    dq = jnp.zeros_like(q32)
    for h in range(HEADS):
        part = w[h * bq : (h + 1) * bq, :]
        dq = dq + part * pre[h : h + 1, :]
        pre_grad_ref[h : h + 1, :] += jnp.sum(part * q32, axis=0, keepdims=True)
    dq_ref[...] = dq.astype(bf16)

    for section, (kept, sent) in enumerate(((dk, dv), (dv, dk))):

        @pl.when((step == pl.num_programs(0) - 1) & (info[SECTION] == section))
        def _(kept=kept, sent=sent):
            keep_ref[...] = kept[...].astype(bf16)
            send_ref[...] = sent[...].astype(bf16)


def attend_back(info, layer, q, datt, u, lse, k, v, smalls, bk, extras):
    count, width = q.shape
    seq = k.shape[0]
    bq = count // 2
    full = lambda i, place: (0, 0)
    row = lambda i, place: (i, 0)
    shape = jax.ShapeDtypeStruct
    return pl.pallas_call(
        cost_estimate=SMALL_COST,
        kernel=functools.partial(attend_back_kernel, bq=bq, bk=bk, extra=len(extras), layer=layer),
        grid_spec=pltpu.PrefetchScalarGridSpec(
            num_scalar_prefetch=1,
            grid=(2,),
            in_specs=[
                pl.BlockSpec((bq, width), row),
                pl.BlockSpec((bq, width), row),
                pl.BlockSpec((HEADS * bq, width), row),
                pl.BlockSpec((HEADS * bq, 128), row),
                HBM_SPEC,
                HBM_SPEC,
                pl.BlockSpec((SMALL_ROWS, width), full),
                pl.BlockSpec((SMALL_ROWS, width), full),
            ]
            + [HBM_SPEC] * len(extras),
            out_specs=[
                pl.BlockSpec((bq, width), row),
                pl.BlockSpec((seq, width), full),
                pl.BlockSpec((seq, width), full),
                pl.BlockSpec((HEADS, width), full),
                pl.BlockSpec((HEADS, width), full),
                SMEM_SPEC,
            ],
            scratch_shapes=[
                pltpu.VMEM((HEADS * bq, width), bf16),
                pltpu.VMEM((HEADS * bq, width), bf16),
                pltpu.VMEM((seq, width), f32),
                pltpu.VMEM((seq, width), f32),
                pltpu.VMEM((HEADS * bq, width), f32),
                pltpu.VMEM((HEADS * bq, 128), f32),
                pltpu.VMEM((seq, width), bf16),
                pltpu.VMEM((seq, width), bf16),
                pltpu.SemaphoreType.DMA((2,)),
            ],
        ),
        out_shape=[
            shape((count, width), bf16),
            shape((seq, width), bf16),
            shape((seq, width), bf16),
            shape((HEADS, width), f32),
            shape((HEADS, width), f32),
            TOKEN,
        ],
        compiler_params=pltpu.CompilerParams(vmem_limit_bytes=BIG_VMEM),
    )(info, q, datt, u, lse, k, v, *smalls, *extras)


def swap_section(x):
    return lax.ppermute(x, "section", [(0, 1), (1, 0)])


def xor_permute(x, axis, by):
    return lax.ppermute(x, axis, [(i, i ^ by) for i in range(lax.axis_size(axis))])


def from_xor_order(x, index):
    places = range(x.shape[0])
    return jnp.concatenate([lax.dynamic_index_in_dim(x, index ^ i, 0) for i in places])


def token_kernel(*refs):
    refs[-1][0] = 0


def token_after(*arrays):
    arrays = [x if x.ndim == 1 else x[(0,) * (x.ndim - 2)][:16, :128] for x in arrays]
    return pl.pallas_call(
        token_kernel,
        cost_estimate=SMALL_COST,
        in_specs=[SMEM_SPEC if x.ndim == 1 else VMEM_SPEC for x in arrays],
        out_specs=SMEM_SPEC,
        out_shape=TOKEN,
    )(*arrays)[0]


def half_columns(ref, which, size):
    return ref[:, pl.ds(pl.multiple_of(which * size, size), size)]


def split_blocks(blocks, kept, sent, mine):
    for i in range(kept.shape[0]):
        kept[i] = blocks[2 * i + mine]
        sent[i] = blocks[2 * i + 1 - mine]


def split_blocks_first(blocks, kept, sent, mine):
    for i in range(kept.shape[0]):
        at = 4 * (i // 2) + i % 2
        kept[i] = blocks[at + 2 * mine]
        sent[i] = blocks[at + 2 * (1 - mine)]


def products_kernel(
    seat, active_hbm, active_other_hbm, two, two_other, att, att_other, right, right_other,
    down_kept, down_sent, up_kept, up_sent, token_ref, active, active_other, down_blocks, up_blocks, sems,
):
    token_ref[0] = 0
    copies = [
        pltpu.make_async_copy(x, y, sems.at[i])
        for i, (x, y) in enumerate(((active_hbm, active), (active_other_hbm, active_other)))
    ]
    for copy in copies:
        copy.start()
    width = att.shape[1]
    half, half_ff = width // 2, active.shape[1] // 2
    both = lambda left, left_other, cols: dense_tn(left, right[:, cols]) + dense_tn(left_other, right_other[:, cols])
    rows = up_blocks.shape[1]
    tile = half_ff // 2
    for j in range(2):
        cols = slice(j * tile, (j + 1) * tile)
        up_blocks[:, :, cols] = both(two[...], two_other[...], cols).astype(bf16).reshape(-1, rows, tile)
    cols = slice(half_ff, half_ff + half)
    up_blocks[:, :, cols] = both(att[...], att_other[...], cols).astype(bf16).reshape(-1, rows, half)
    split_blocks_first(up_blocks, up_kept, up_sent, seat[CTX] // 2)
    for copy in copies:
        copy.wait()
    rows = down_blocks.shape[1]
    each = width // rows
    for j in range(active.shape[1] // width):
        cols = slice(j * width, (j + 1) * width)
        grad = both(active[:, cols], active_other[:, cols], slice(half_ff + half, half_ff + width))
        down_blocks[j * each : (j + 1) * each] = grad.astype(bf16).reshape(each, rows, half)
    split_blocks(down_blocks, down_kept, down_sent, seat[CTX] % 2)


def products(seat, arrays, count, rows):
    ff, width = arrays[0].shape[1], arrays[4].shape[1]
    down, up = (ff // count, width // 2), (rows, (ff + width) // 2)
    shape = lambda x: jax.ShapeDtypeStruct((count // 2, *x), bf16)
    outs = one_step(
        products_kernel,
        in_specs=[SMEM_SPEC] + [HBM_SPEC] * 2 + [FAR_SPEC] * 4 + [VMEM_SPEC] * 2,
        out_specs=[FAR_SPEC] * 4 + [SMEM_SPEC],
        out_shape=[shape(down)] * 2 + [shape(up)] * 2 + [TOKEN],
        scratch_shapes=[
            pltpu.VMEM(arrays[0].shape, bf16),
            pltpu.VMEM(arrays[1].shape, bf16),
            pltpu.VMEM((count, *down), bf16),
            pltpu.VMEM((count, *up), bf16),
            pltpu.SemaphoreType.DMA((2,)),
        ],
        compiler_params=pltpu.CompilerParams(vmem_limit_bytes=SMALL_VMEM),
    )(seat, *arrays)
    return FastSum(*outs[:2], (1, 2)), FastSum(*outs[2:4], (2, 1)), outs[4]


def second_kernel(seat, token_in, *refs, bits, passing, closing, behind):
    count = len(bits)
    refs = refs[behind + passing :]
    parts, refs = refs[2 * count : 2 * count + closing], refs[: 2 * count] + refs[2 * count + closing :]
    refs[4 * count][0] = token_in[0]
    if closing:
        refs[4 * count + 1][...] = functools.reduce(jnp.add, [x[...].astype(f32) for x in parts])
    for i, bit in enumerate(bits):
        kept, got = refs[2 * i], refs[2 * i + 1]
        kept_out, sent_out = refs[2 * count + 2 * i], refs[2 * count + 2 * i + 1]
        mine = (seat[1] // bit) % 2
        for j in range(kept_out.shape[0]):
            for out, at in ((kept_out, 2 * j + mine), (sent_out, 2 * j + 1 - mine)):
                out[j] = (kept[at].astype(f32) + got[at].astype(f32)).astype(bf16)


def last_kernel(seat, token_in, *refs, count, rows, dp_count, passing):
    refs = refs[passing:]
    total, outs, token_ref = refs[2 * count], refs[2 * count + 1 : 2 * count + dp_count], refs[2 * count + dp_count]
    token_ref[0] = token_in[0]
    at = 0
    for i in range(count):
        kept, got = refs[2 * i], refs[2 * i + 1]
        size = kept.shape[2]
        for j in range(kept.shape[1] // rows):
            part = slice(j * rows, (j + 1) * rows)
            for by in range(len(outs) + 1):
                z = seat[2] ^ by
                value = kept[z, part, :].astype(f32) + got[z, part, :].astype(f32)
                if by == 0:
                    total[:, at : at + size] = value
                else:
                    outs[by - 1][:, at : at + size] = value.astype(bf16)
            at += size


def halved_kernel(seat, token_in, *refs, count, rows, passing, closing):
    refs = refs[passing:]
    parts, refs = refs[2 * count : 2 * count + closing], refs[: 2 * count] + refs[2 * count + closing :]
    kept_out, sent_out, token_ref = refs[2 * count : 2 * count + 3]
    if closing:
        refs[2 * count + 3][...] = functools.reduce(jnp.add, [x[...].astype(f32) for x in parts])
    token_ref[0] = token_in[0]
    mine = seat[2] % 2
    at = 0
    for i in range(count):
        kept, got = refs[2 * i], refs[2 * i + 1]
        size = kept.shape[2]
        for j in range(kept.shape[1] // rows):
            part = slice(j * rows, (j + 1) * rows)
            for b in range(2):
                for out, z in ((kept_out, 2 * b + mine), (sent_out, 2 * b + 1 - mine)):
                    value = kept[z, part, :].astype(f32) + got[z, part, :].astype(f32)
                    out[b, :, at : at + size] = value.astype(bf16)
            at += size


def middle_kernel(seat, token_in, *refs, passing):
    kept, got, total, sent, token_ref = refs[passing : passing + 5]
    token_ref[0] = token_in[0]
    mine = seat[2] // 2
    total[...] = kept[mine].astype(f32) + got[mine].astype(f32)
    sent[...] = (kept[1 - mine].astype(f32) + got[1 - mine].astype(f32)).astype(bf16)


class Halved:
    def __init__(self, kept, sent):
        self.kept, self.got = kept, xor_permute(sent, "dp", 1)


def halved_step(seat, token, sums, rows, passing, closing, spec):
    closed = [jax.ShapeDtypeStruct(x.shape, f32) for x in closing[:1]]
    specs_in, specs_out, shapes, aliases = handed_on(passing, 2, 3 + len(closed))
    size = sum(x.kept.shape[1] // rows * x.kept.shape[2] for x in sums)
    shape = jax.ShapeDtypeStruct((2, rows, size), bf16)
    kept, sent, token, *rest = one_step(
        functools.partial(halved_kernel, count=len(sums), rows=rows, passing=len(passing), closing=len(closing)),
        in_specs=[SMEM_SPEC] * 2 + specs_in + [spec] * (2 * len(sums) + len(closing)),
        out_specs=[spec, VMEM_SPEC, SMEM_SPEC] + [FAR_SPEC] * len(closed) + specs_out,
        out_shape=[shape, shape, TOKEN] + closed + shapes,
        input_output_aliases=aliases,
        compiler_params=pltpu.CompilerParams(vmem_limit_bytes=SMALL_VMEM),
    )(seat, token, *passing, *[y for x in sums for y in (x.kept, x.got)], *closing)
    return Halved(kept, sent), token, tuple(rest[len(closed) :]), rest[0] if closed else None


def middle_step(seat, token, halved, passing, spec):
    specs_in, specs_out, shapes, aliases = handed_on(passing, 2, 3)
    shape = jax.ShapeDtypeStruct
    total, sent, token, *passing = one_step(
        functools.partial(middle_kernel, passing=len(passing)),
        in_specs=[SMEM_SPEC] * 2 + specs_in + [spec] * 2,
        out_specs=[FAR_SPEC, VMEM_SPEC, SMEM_SPEC] + specs_out,
        out_shape=[shape(halved.kept.shape[1:], f32), shape(halved.kept.shape[1:], bf16), TOKEN] + shapes,
        input_output_aliases=aliases,
        compiler_params=pltpu.CompilerParams(vmem_limit_bytes=SMALL_VMEM),
    )(seat, token, *passing, halved.kept, halved.got)
    halved.parts = (total, xor_permute(sent, "dp", 2))
    return token, tuple(passing)


class FastSum:
    def __init__(self, kept, sent, bits):
        self.kept, self.bits = kept, bits
        self.got = xor_permute(sent, "ctx", bits[0])

    def start(self):
        self.got = xor_permute(self.sent, "ctx", self.bits[1])


def handed_on(passing, before, after):
    specs = [ANY_SPEC] * len(passing)
    shapes = [jax.ShapeDtypeStruct(x.shape, x.dtype) for x in passing]
    return specs, specs, shapes, {before + i: after + i for i in range(len(passing))}


def hand_on_kernel(token_in, *refs, meanwhile, passing):
    refs[meanwhile + passing][0] = token_in[0]


def hand_on(token, meanwhile, passing):
    specs_in, specs_out, shapes, aliases = handed_on(passing, 1 + len(meanwhile), 1)
    outs = one_step(
        functools.partial(hand_on_kernel, meanwhile=len(meanwhile), passing=len(passing)),
        in_specs=[SMEM_SPEC] + [VMEM_SPEC] * len(meanwhile) + specs_in,
        out_specs=[SMEM_SPEC] + specs_out,
        out_shape=[TOKEN] + shapes,
        input_output_aliases=aliases,
    )(token, *meanwhile, *passing)
    return outs[0], outs[1:]


def second_step(seat, token, sums, passing, closing, behind, spec):
    closed = [jax.ShapeDtypeStruct(x.shape, f32) for x in closing[:1]]
    specs_in, specs_out, shapes, aliases = handed_on(passing, 2 + len(behind), 2 * len(sums) + 1 + len(closed))
    shape = lambda x: jax.ShapeDtypeStruct((x.shape[0] // 2,) + x.shape[1:], bf16)
    outs = one_step(
        functools.partial(second_kernel, bits=[x.bits[1] for x in sums], passing=len(passing), closing=len(closing), behind=len(behind)),
        in_specs=[SMEM_SPEC] * 2 + [ANY_SPEC] * len(behind) + specs_in + [spec] * (2 * len(sums) + len(closing)),
        out_specs=[VMEM_SPEC] * (2 * len(sums)) + [SMEM_SPEC] + [FAR_SPEC] * len(closed) + specs_out,
        out_shape=[shape(x.kept) for x in sums for _ in range(2)] + [TOKEN] + closed + shapes,
        input_output_aliases=aliases,
        compiler_params=pltpu.CompilerParams(vmem_limit_bytes=SMALL_VMEM),
    )(seat, token, *behind, *passing, *[y for x in sums for y in (x.kept, x.got)], *closing)
    for i, x in enumerate(sums):
        x.kept, x.sent = outs[2 * i], outs[2 * i + 1]
    outs = outs[2 * len(sums) :]
    return outs[0], outs[1 + len(closed) :], outs[1] if closed else None


def last_step(seat, token, sums, rows, passing):
    dp_count = sums[0].kept.shape[0]
    specs_in, specs_out, shapes, aliases = handed_on(passing, 2, dp_count + 1)
    size = sum(x.kept.shape[1] // rows * x.kept.shape[2] for x in sums)
    shape = jax.ShapeDtypeStruct((rows, size), bf16)
    outs = one_step(
        functools.partial(last_kernel, count=len(sums), rows=rows, dp_count=dp_count, passing=len(passing)),
        in_specs=[SMEM_SPEC] * 2 + specs_in + [VMEM_SPEC] * (2 * len(sums)),
        out_specs=[VMEM_SPEC] * dp_count + [SMEM_SPEC] + specs_out,
        out_shape=[jax.ShapeDtypeStruct((rows, size), f32)] + [shape] * (dp_count - 1) + [TOKEN] + shapes,
        input_output_aliases=aliases,
        compiler_params=pltpu.CompilerParams(vmem_limit_bytes=SMALL_VMEM),
    )(seat, token, *passing, *[y for x in sums for y in (x.kept, x.got)])
    gots = [xor_permute(x, "dp", by) for by, x in enumerate(outs[1:dp_count], 1)]
    return outs[0], gots, outs[dp_count], outs[dp_count + 1 :]


def final_parts_kernel(seat, *refs, counts):
    *refs, keep, send = refs
    sums, at = [], 0
    for count in counts:
        sums.append(functools.reduce(jnp.add, [x[...].astype(f32) for x in refs[at : at + count]]))
        at += count
    cut = sums[0].shape[1]
    for section in range(2):

        @pl.when(seat[0] == section)
        def _(section=section):
            for out, layer in ((keep, section), (send, 1 - section)):
                out[:, :cut] = sums[2 * layer]
                out[:, cut:] = sums[2 * layer + 1]


def final_parts(seat, groups):
    parts = [x for group in groups for x in group]
    rows = parts[0].shape[0]
    out = jax.ShapeDtypeStruct((rows, groups[0][0].shape[1] + groups[1][0].shape[1]), f32)
    return one_step(
        functools.partial(final_parts_kernel, counts=[len(x) for x in groups]),
        in_specs=[SMEM_SPEC] + [VMEM_SPEC] * len(parts),
        out_specs=[VMEM_SPEC] * 2,
        out_shape=[out, out],
        compiler_params=pltpu.CompilerParams(vmem_limit_bytes=SMALL_VMEM),
    )(seat, *parts)


def final_outs_kernel(seat, keep, got, joint, mixer, up, down):
    half, half_up, rows = mixer.shape[1] // 2, up.shape[1] // 2, mixer.shape[0]
    width = 2 * half
    for section in range(2):

        @pl.when(seat[0] == section)
        def _(section=section):
            for i, ref in enumerate((keep, got) if section == 0 else (got, keep)):
                times = down.shape[0] // rows
                for j in range(times):
                    down[j * rows : (j + 1) * rows, i * half : (i + 1) * half] = ref[:, j * half : (j + 1) * half]
                at = times * half
                up[:, i * half_up : (i + 1) * half_up] = ref[:, at : at + half_up]
                at += half_up
                mixer[:, i * half : (i + 1) * half] = ref[:, at : at + half]
                at += half
                joint[:, (1 + i) * width : (2 + i) * width] = ref[:, at : at + width]
                joint[:, i * half : (i + 1) * half] = ref[:, at + width : at + width + half]


def final_outs(seat, keep, got, width, ff):
    rows = keep.shape[0]
    shape = lambda *x: jax.ShapeDtypeStruct(x, f32)
    return one_step(
        final_outs_kernel,
        in_specs=[SMEM_SPEC] + [VMEM_SPEC] * 2,
        out_specs=[VMEM_SPEC] * 4,
        out_shape=[shape(rows, 3 * width), shape(rows, width), shape(rows, ff), shape(rows * (ff // width), width)],
        compiler_params=pltpu.CompilerParams(vmem_limit_bytes=SMALL_VMEM),
    )(seat, keep, got)


def mix_grads_kernel(small, _, pre, post):
    rows = lax.broadcasted_iota(jnp.int32, (HEADS, small.shape[1]), 0)
    cols = lax.broadcasted_iota(jnp.int32, (HEADS, small.shape[1]), 1)
    heads = jnp.where(cols // HEAD == rows, 1.0, 0.0).astype(f32)
    dot = lambda a, b: lax.dot_general(
        a, b, (((1,), (1,)), ((), ())), precision=lax.Precision.HIGHEST, preferred_element_type=f32
    )
    pre[:, 0, :] = 0.125 * dot(heads, small[2 : 2 + HEADS, :])
    post[:, 0, :] = dot(small[2 + HEADS : 2 + 2 * HEADS, :], heads)


def mix_grads(small, behind):
    out = jax.ShapeDtypeStruct((HEADS, 1, HEADS), f32)
    return one_step(
        mix_grads_kernel, in_specs=[VMEM_SPEC, ANY_SPEC], out_specs=[VMEM_SPEC] * 2, out_shape=[out, out]
    )(small, behind)


def total_of(part, gots):
    for got in gots:
        part = part + got.astype(f32)
    return part


def join_kernel(
    seat, token_in, keep_ref, got_ref, normed_ref, own, own_other, dq, dq_other, joint_own, joint_got,
    small_own, small_got, dn_kept, dn_sent, dnq_ref, a_kept, a_sent, b_kept, b_sent, gain_grad_ref, token_ref,
    kv_w, q_w, dkv, dn, a_blocks, b_blocks, sems, *, layer,
):
    token_ref[0] = token_in[0]
    width = dkv.shape[1]
    section, which = seat[SECTION], seat[WHICH + layer]
    for i, ref in enumerate((joint_own, joint_got)):

        @pl.when(which == i)
        def _(ref=ref):
            cols = pl.ds(pl.multiple_of((1 + section) * width, width), width)
            pltpu.make_async_copy(ref.at[0, :, cols], kv_w, sems.at[0]).start()
            pltpu.make_async_copy(ref.at[0, :, pl.ds(0, width)], q_w, sems.at[1]).start()

    dkv[...] = (keep_ref[...].astype(f32) + got_ref[...].astype(f32)).astype(bf16)
    rows, size_a, size_b = a_blocks.shape[1], a_blocks.shape[2], b_blocks.shape[2]
    grad = dense_tn(normed_ref[...], dkv[:, :size_a])
    a_blocks[...] = grad.astype(bf16).reshape(-1, rows, size_a)
    grad = dense_tn(normed_ref[...], dkv[:, size_a:])
    b_blocks[:, :, : width - size_a] = grad.astype(bf16).reshape(-1, rows, width - size_a)
    half = width // 2
    grad = dense_tn(own[...], half_columns(dq, section, half)) + dense_tn(
        own_other[...], half_columns(dq_other, section, half)
    )
    b_blocks[:, :, width - size_a :] = grad.astype(bf16).reshape(-1, rows, half)
    split_blocks(a_blocks, a_kept, a_sent, seat[1] % 2)
    split_blocks_first(b_blocks, b_kept, b_sent, seat[1] // 2)
    for i in range(2):
        pltpu.make_async_copy(joint_own.at[0, :, pl.ds(0, width)], (kv_w, q_w)[i], sems.at[i]).wait()
    back = dense_nt(dkv[...], kv_w[...])
    dn[...] = back.astype(bf16)
    back_q = dense_nt(dq[...], q_w[...])
    dnq_ref[...] = back_q
    gain_grad = jnp.sum(back * normed_ref[...].astype(f32), axis=0, keepdims=True)
    gain_grad = gain_grad + jnp.sum(back_q * own[...].astype(f32), axis=0, keepdims=True)
    gain_grad_ref[...] = gain_grad / small_of(small_own, small_got, which)(GAIN_A, 1)
    blk = own.shape[0] // 2
    last = dn.shape[0] // blk - 1
    for i in range(dn_kept.shape[0] // blk):
        for out, side in ((dn_kept, section), (dn_sent, 1 - section)):
            core = (i // 2) * 2 + side
            at = core if i % 2 == 0 else last - core
            out[i * blk : (i + 1) * blk, :] = dn[pl.ds(pl.multiple_of(at * blk, blk), blk), :]


def join(seat, layer, token, arrays, joints, smalls, count, rows):
    seq, width = arrays[0].shape
    own_count = arrays[3].shape[0]
    size_a = 2 * width // 3
    size_b = width - size_a + width // 2
    shape = jax.ShapeDtypeStruct
    a_shape, b_shape = (shape((count // 2, rows, size), bf16) for size in (size_a, size_b))
    half_rows = shape((seq // 2, width), bf16)
    return one_step(
        functools.partial(join_kernel, layer=layer),
        in_specs=[SMEM_SPEC] * 2
        + [VMEM_SPEC] * 2
        + [FAR_SPEC] * 3
        + [VMEM_SPEC] * 2
        + [HBM_SPEC] * 2
        + [VMEM_SPEC] * 2,
        out_specs=[VMEM_SPEC] * 8 + [SMEM_SPEC],
        out_shape=[half_rows, half_rows, shape((own_count, width), f32)]
        + [a_shape, a_shape, b_shape, b_shape, shape((1, width), f32), TOKEN],
        scratch_shapes=[
            pltpu.VMEM((width, width), bf16),
            pltpu.VMEM((width, width), bf16),
            pltpu.VMEM((seq, width), bf16),
            pltpu.VMEM((seq, width), bf16),
            pltpu.VMEM((count, rows, size_a), bf16),
            pltpu.VMEM((count, rows, size_b), bf16),
            pltpu.SemaphoreType.DMA((2,)),
        ],
        compiler_params=pltpu.CompilerParams(vmem_limit_bytes=SMALL_VMEM),
    )(seat, token, *arrays, *joints, *smalls)


class Summer:
    def __init__(self, blocks, backwards):
        self.dp_count, ctx_count = blocks[0].shape[:2]
        bits = [1 << i for i in range(ctx_count.bit_length() - 1)]
        self.left = bits[::-1]
        self.order = bits[::-1] if backwards else bits
        self.parts = [x.reshape((self.dp_count,) + (2,) * len(bits) + x.shape[2:]) for x in blocks]

    def send(self, token=0):
        bit, self.order = self.order[0], self.order[1:]
        self.axis = 1 + self.left.index(bit)
        self.left = [b for b in self.left if b != bit]
        self.mine = (lax.axis_index("ctx") // bit) % 2
        at = 1 - self.mine + token
        sent = [lax.dynamic_index_in_dim(x, at, self.axis, keepdims=False) for x in self.parts]
        sent = sent[0] if len(sent) == 1 else jnp.concatenate(sent, axis=-1)
        self.got = xor_permute(sent, "ctx", bit)
        return [sent]

    def add(self, token):
        at, parts = 0, []
        for x in self.parts:
            kept = lax.dynamic_index_in_dim(x, self.mine + token, self.axis, keepdims=False)
            got = self.got[..., at : at + x.shape[-1]]
            at += x.shape[-1]
            parts.append((kept.astype(f32) + got.astype(f32)).astype(bf16))
        self.parts = parts

    def rest(self, token):
        self.add(token)
        while self.order:
            self.send()
            self.add(0)


class LastSum:
    def __init__(self, summers, rows):
        pieces = []
        for x in [x for one in summers for x in one.parts]:
            pieces += [x[:, i : i + rows] for i in range(0, x.shape[1], rows)]
        self.part = jnp.concatenate(pieces, axis=-1)

    def send(self):
        dp = lax.axis_index("dp")
        sent = [
            lax.dynamic_index_in_dim(self.part, dp ^ by, 0, keepdims=False)
            for by in range(1, self.part.shape[0])
        ]
        self.got = [xor_permute(x, "dp", by) for by, x in enumerate(sent, 1)]
        return sent

    @property
    def total(self):
        return lax.dynamic_index_in_dim(self.part, lax.axis_index("dp"), 0, keepdims=False).astype(f32)


def all_sum(x, tokens):
    steps = [(axis, 1 << i) for axis in ("ctx", "dp") for i in range(lax.axis_size(axis).bit_length() - 1)]
    for i, (axis, bit) in enumerate(steps):
        got = xor_permute(x, axis, bit)
        x = x + tokens[min(i, len(tokens) - 1)].astype(f32) + got
    return x


def local(
    inputs, lengths, cotangent, first_gain, joint_weight, pre_mix, post_mix,
    mixer_weight, second_gain, up_weight, down_weight,
):
    s = lax.axis_index("section")
    ctx = lax.axis_index("ctx")
    n = lax.axis_size("ctx")
    dp_count = lax.axis_size("dp")
    chips = n // 2
    micro_count, row_count, local_len, width = inputs.shape
    ff = up_weight.shape[2]
    seq = local_len * n
    blk = local_len // 2
    m = ctx // chips
    xi = ctx % chips
    core = xi * 2 + s
    zero = jnp.zeros((), jnp.int32)
    inputs = inputs.reshape(micro_count, 2, blk, width)
    cotangent = cotangent.reshape(micro_count, 2, blk, width)
    pick = lambda arr, i: lax.dynamic_index_in_dim(arr, i, 0, keepdims=False)

    spread = lambda mix: jnp.dot(mix, jnp.repeat(jnp.eye(HEADS, dtype=f32), HEAD, axis=1), precision=lax.Precision.HIGHEST)
    lines = lambda x, size: jnp.pad(x, ((0, size - x.shape[0]), (0, 0)))
    gains = jnp.concatenate([first_gain, second_gain]).astype(f32)
    small_own = jnp.concatenate(
        [lines(gains, PRE), lines(0.125 * spread(pre_mix[0].T), POST - PRE), lines(spread(post_mix[0]), SMALL_ROWS - POST)]
    )
    smalls = (small_own, swap_section(small_own))
    joints, mixers, ups, downs = (
        (w, swap_section(w)) for w in (joint_weight, mixer_weight, up_weight, down_weight)
    )

    mine = pick(inputs, m)
    pieces = []
    for d in range(1, n):
        target = m ^ (1 if d >= chips else 0)
        pieces.append(xor_permute(pick(pick(inputs, target), s), "ctx", d))
    other_pieces = [swap_section(jnp.concatenate(pieces))]
    chip_of = [ctx ^ d for d in range(1, n)]
    blocks0 = [2 * ctx, 2 * ctx + 1] + [2 * c + s for c in chip_of] + [2 * c + 1 - s for c in chip_of]
    pieces0 = [mine.reshape(2 * blk, width)] + pieces + other_pieces

    length = pick(lengths.reshape(-1), m)
    low_start = core * blk
    high_start = (2 * n - 1 - core) * blk
    bk = min(256, seq)
    cores1 = [(xi ^ d) * 2 + side for side in (s, 1 - s) for d in range(chips)]
    blocks1 = [b for c in cores1 for b in (c, 2 * n - 1 - c)]
    info = [s, ctx, lax.axis_index("dp"), length, low_start, high_start, s != 0, s != 1, *blocks0, *blocks1]
    info = jnp.stack([jnp.asarray(x, jnp.int32) for x in info])

    def gather_row(x):
        got = [x] + [xor_permute(x, "ctx", d) for d in range(1, chips)]
        return got + [swap_section(y) for y in got]

    def forward(layer, pieces, meanwhile):
        attended, q, normed_own, x_own, token, normed_all, k, v, u, lse = attend(
            info, layer, pieces, 2 * blk, smalls, joints, bk
        )
        weights = [x for pair in (mixers, ups, downs) for x in pair]
        out, hidden, normed_two, upward, active, token = feed(
            info, layer, x_own, attended, smalls, weights, ff, meanwhile
        )
        rows = [(x, swap_section(x)) for x in (active, normed_two, attended, normed_own)]
        return out, (x_own, q, k, v, u, lse, hidden, upward, rows, normed_all)

    def half(x, which):
        return lax.dynamic_slice_in_dim(x, which * (x.shape[1] // 2), x.shape[1] // 2, 1)

    def product(left, right):
        return (dense_tn(left[0], right[0]) + dense_tn(left[1], right[1])).astype(bf16)

    def blocks_of(grad):
        return grad.reshape(dp_count, n, grad.shape[0] // (dp_count * n), grad.shape[1])

    shard = width // (dp_count * n)

    fast = n == 4 and dp_count == 4 and shard % 16 == 0
    count = dp_count * n

    class Slow:
        def first(rows, keep, other):
            active, two, att, _ = rows
            cut, end = ff // 2, (ff + width) // 2
            of = lambda *cols: (keep[:, slice(*cols)], other[:, slice(*cols)])
            down_sum = Summer([blocks_of(product(active, of(end, None)))], False)
            up_sum = Summer([blocks_of(product(two, of(0, cut))), blocks_of(product(att, of(cut, end)))], True)
            return down_sum, up_sum, token_after(*down_sum.send(), *up_sum.send()).reshape(1)

        def second(token, sums, passing=(), closing=(), behind=()):
            for one in sums:
                one.add(token[0])
            return token, passing, total_of(closing[0], closing[1:]) if closing else None

        def last(token, sums, passing=()):
            for one in sums:
                one.rest(token[0])
            one = LastSum(sums, shard)
            one.send()
            one.parts = (one.total, *one.got)
            return one, token, passing

        def halved(token, sums, passing=(), closing=()):
            return *Slow.last(token, sums, passing), total_of(closing[0], closing[1:]) if closing else None

        def middle(token, one, passing=()):
            return token, passing

    class Fast:
        def first(rows, keep, other):
            return products(info, (*rows[0], *rows[1], *rows[2], keep, other), count, shard)

        def second(token, sums, passing=(), closing=(), behind=()):
            return second_step(info, token, sums, passing, closing, behind, VMEM_SPEC if behind else FAR_SPEC)

        def last(token, sums, passing=()):
            part, gots, token, passing = last_step(info, token, sums, shard, passing)
            one = types.SimpleNamespace(parts=(part, *gots))
            return one, token, passing

        def halved(token, sums, passing=(), closing=()):
            return halved_step(info, token, sums, shard, passing, closing, VMEM_SPEC if closing else FAR_SPEC)

        def middle(token, one, passing=()):
            return middle_step(info, token, one, passing, FAR_SPEC if passing else VMEM_SPEC)

    steps = Fast if fast else Slow

    def backward(layer, dy, kept, earlier):
        x_own, q, k, v, u, lse, hidden, upward, rows, normed_all = kept
        rows_normed = rows[3]
        here = s == layer
        gain_a = jnp.where(here, smalls[0][GAIN_A], smalls[1][GAIN_A])
        earlier[0]()
        weights = [x for pair in (mixers, ups, downs) for x in pair]
        keep, send, dhidden, datt, gain_b_grad, token = feed_back(
            info, layer, dy, upward, hidden, smalls, weights, ()
        )
        token, (send,) = earlier[1](token, (send,))
        down_sum, up_sum, first_token = steps.first(rows, keep, swap_section(send))
        dq, dkv_keep, dkv_send, pre_rows, post_rows, token = attend_back(
            info, layer, q, datt, u, lse, k, v, smalls, bk, (token, first_token)
        )
        token, (dkv_send, dq) = earlier[2](token, (down_sum, up_sum), (dkv_send, dq))
        got, dq_other = swap_section(dkv_send), swap_section(dq)
        if fast:
            dn_kept, dn_sent, dnq, a_kept, a_sent, b_kept, b_sent, gain_a_grad, token = join(
                info, layer, token, (dkv_keep, got, normed_all, *rows_normed, dq, dq_other), joints, smalls, count, shard
            )
            kv_sum, q_sum = FastSum(a_kept, a_sent, (1, 2)), FastSum(b_kept, b_sent, (2, 1))
            dn_kept, dn_sent = (x.reshape(chips, 2, blk, width) for x in (dn_kept, dn_sent))
        else:
            joint_w = jnp.where(here, joints[0][0], joints[1][0])
            kv_w = lax.dynamic_slice_in_dim(joint_w, width * (1 + s), width, 1)
            dkv = (dkv_keep.astype(f32) + got.astype(f32)).astype(bf16)
            dn = dense_nt(dkv, kv_w)
            gain_a_grad = jnp.sum(dn * normed_all.astype(f32), axis=0)
            dn = dn.astype(bf16).reshape(2 * n, blk, width)
            dn = jnp.stack([dn[i if h == 0 else 2 * n - 1 - i] for i in range(n) for h in range(2)])
            dn = dn.reshape(chips, 2, 2, blk, width)
            dn_kept = lax.dynamic_index_in_dim(dn, s, 1, keepdims=False)
            dn_sent = lax.dynamic_index_in_dim(dn, 1 - s, 1, keepdims=False)
            dnq = dense_nt(dq, joint_w[:, :width])
            gain_a_grad = (gain_a_grad + jnp.sum(dnq * rows_normed[0].astype(f32), axis=0)) / gain_a
            kv_part = blocks_of(dense_tn(normed_all, dkv).astype(bf16))
            q_part = blocks_of(product(rows_normed, (half(dq, s), half(dq_other, s))))
            cut = 2 * width // 3
            kv_sum = Summer([kv_part[..., :cut]], False)
            q_sum = Summer([kv_part[..., cut:], q_part], True)
            kv_sum.send()
            q_sum.send()
        token, (dn_sent,) = earlier[3](token, (dn_sent,), (down_sum, up_sum))
        low = (dn_kept.astype(f32) + swap_section(dn_sent).astype(f32)).astype(bf16)
        gots = [xor_permute(pick(low, xi ^ d), "ctx", d) for d in range(1, chips)]
        sums = (down_sum, up_sum, kv_sum, q_sum)
        token = earlier[4](token, low, sums)
        scattered = pick(low, xi + token[0]).astype(f32)
        for x in gots:
            scattered = scattered + x.astype(f32)
        scaled = (scattered.reshape(2 * blk, width) + dnq) * gain_a
        values = x_own.astype(f32)
        inverse = rms_inverse(values)
        unit = values * inverse
        dfront = inverse * (scaled - unit * jnp.mean(scaled * unit, axis=-1, keepdims=True))
        small = jnp.concatenate([gain_a_grad.reshape(1, -1), gain_b_grad.reshape(1, -1), pre_rows, post_rows])
        return dhidden + dfront, sums, small, token

    low_chip = ctx < chips
    there = [(i, chips + i) for i in range(chips)] + [(n - 1 - i, i) for i in range(chips)]
    here = [(n - 1 - i, chips + i) for i in range(chips)] + [(i, i) for i in range(chips)]
    first = jnp.where(low_chip, s, 1 - s)
    halves = lax.dynamic_index_in_dim(cotangent, first, 1, keepdims=False)
    ones, twos = jnp.where(low_chip, halves[1], halves[0]), jnp.where(low_chip, halves[0], halves[1])
    one, two = lax.ppermute(ones, "ctx", there), lax.ppermute(twos, "ctx", here)
    dy1 = jnp.concatenate([jnp.where(m == 0, two, one), jnp.where(m == 0, one, two)])
    x1, kept0 = forward(0, pieces0, (one, two))
    y, kept1 = forward(1, gather_row(x1), ())

    def send_home(x):
        x = x.reshape(2, blk, width)
        one = lax.ppermute(jnp.where(m == 0, x[1], x[0]), "ctx", [(b, a) for a, b in there])
        two = lax.ppermute(jnp.where(m == 0, x[0], x[1]), "ctx", [(b, a) for a, b in here])
        return one, two

    def at_home(one, two):
        return jnp.where(low_chip, jnp.stack([two, one]), jnp.stack([one, two]))

    def start(sums):
        for one in sums:
            one.start() if fast else one.send()

    def no_step():
        return None

    state = {}

    def after_attention(token, sums, passing):
        token, passing, _ = steps.second(token, sums, passing)
        start(sums)
        return token, passing

    def after_join(token, passing, sums):
        state["big"], token, passing, _ = steps.halved(token, sums, passing)
        return token, passing

    def after_low(token, low, sums):
        token, _, _ = steps.second(token, sums[2:], behind=(low,))
        start(sums[2:])
        return token

    first_steps = (no_step, lambda token, passing: (token, passing), after_attention, after_join, after_low)
    dx1, (_, _, kv1, q1), small1, _ = backward(1, dy1, kept1, first_steps)
    dy0 = dx1.astype(bf16)
    y_sent = send_home(y)

    def after_feed(token, passing):
        state["joint1"], token, passing, _ = steps.halved(token, [kv1, q1], (*passing, *y_sent))
        token, (passing, *state["y"]) = steps.middle(token, state["big"], passing)
        return token, (passing,)

    def after_attention(token, sums, passing):
        token, passing, state["big1"] = steps.second(token, sums, passing, state["big"].parts)
        start(sums)
        token, passing = steps.middle(token, state["joint1"], passing)
        return token, passing

    def after_join(token, passing, sums):
        state["big0"], token, passing, state["joint1"] = steps.halved(token, sums, passing, state["joint1"].parts)
        state["token"] = token
        return token, passing

    def after_low(token, low, sums):
        token, _, _ = steps.second(token, sums[2:], behind=(low,))
        start(sums[2:])
        return steps.middle(token, state["big0"])[0]

    dx0, (down0, up0, kv0, q0), small0, token = backward(
        0, dy0, kept0, (no_step, after_feed, after_attention, after_join, after_low)
    )
    early = token
    dx0 = dx0.astype(bf16)
    dx_home = at_home(*send_home(dx0))
    y_home = at_home(*state["y"])

    small_got = swap_section(jnp.where(s == 0, small1, small0))
    small = jnp.where(s == 0, small0, small1) + small_got
    joint0, last_token, _ = steps.last(token, [kv0, q0], (dx0,))
    small = all_sum(small, (state["token"][0], early[0], token[0], last_token[0]))

    got = swap_section(jnp.where(s == 0, y_home, dx_home))
    held = jnp.where(s == 0, dx_home, y_home)
    is_first = jnp.where(low_chip, s, 1 - s) == 0
    ends = jnp.stack([jnp.where(is_first, held, got), jnp.where(is_first, got, held)], axis=1)
    ends = ends.reshape(1, micro_count, row_count, local_len, width)

    at = (lax.axis_index("dp") * n + ctx) * shard
    gain_a_out, gain_b_out = (lax.dynamic_slice_in_dim(small[i], at, shard, 0) for i in range(2))
    half_d, half_ff, times = width // 2, ff // 2, ff // width
    if fast:
        groups = (state["big0"].parts, joint0.parts, (state["big1"],), (state["joint1"],))
        keep, send = final_parts(info, groups)
        behind = keep
        joint_out, mixer_out, up_out, down_out = final_outs(info, keep, swap_section(send), width, ff)
    else:
        behind = small
        big0, joint0 = (total_of(x.parts[0], x.parts[1:]) for x in (state["big0"], joint0))
        pairs = ((big0, state["big1"]), (joint0, state["joint1"]))
        outs = []
        for at_zero, at_one in pairs:
            other = swap_section(jnp.where(s == 0, at_one, at_zero))
            own = jnp.where(s == 0, at_zero, at_one)
            outs.append((jnp.where(s == 0, own, other), jnp.where(s == 0, other, own)))
        (big_a, big_b), (joint_a, joint_b) = outs
        side = lambda *cuts: jnp.concatenate([x[:, at : at + size] for x, at, size in cuts], axis=1)
        down_out = jnp.concatenate(
            [side((big_a, i * half_d, half_d), (big_b, i * half_d, half_d)) for i in range(times)]
        )
        at = times * half_d
        up_out = side((big_a, at, half_ff), (big_b, at, half_ff))
        mixer_out = side((big_a, at + half_ff, half_d), (big_b, at + half_ff, half_d))
        joint_out = side((joint_a, width, half_d), (joint_b, width, half_d), (joint_a, 0, width), (joint_b, 0, width))
    pre_out, post_out = (x.transpose(1, 0, 2) for x in mix_grads(small, behind))
    return (
        ends,
        gain_a_out[None],
        joint_out[None],
        pre_out,
        post_out,
        mixer_out[None],
        gain_b_out[None],
        up_out[None],
        down_out[None],
    )


def solution(mesh):
    in_specs = (
        P(None, "dp", "ctx", None),
        P(None, "dp"),
        P(None, "dp", "ctx", None),
        P("section", None),
        P("section", None, None),
        P("section", None, None),
        P("section", None, None),
        P("section", None, None),
        P("section", None),
        P("section", None, None),
        P("section", None, None),
    )
    out_specs = (
        P("section", None, "dp", "ctx", None),
        P("section", ("dp", "ctx")),
        P("section", ("dp", "ctx"), None),
        P("section", None, None),
        P("section", None, None),
        P("section", ("dp", "ctx"), None),
        P("section", ("dp", "ctx")),
        P("section", ("dp", "ctx"), None),
        P("section", ("dp", "ctx"), None),
    )
    return jax.shard_map(local, mesh=mesh, in_specs=in_specs, out_specs=out_specs, check_vma=False)
```
